32 devices in a mesh: tm: 8 (over z, x), space: 4 (over y, core).
Axes of the slice: x: 2, y: 2, z: 4, core: 2. Of those that a mesh axis runs over, the one named last changes fastest.
Arguments:
- increment: float32 [32, 4, 32, 512], P('tm', None, 'space'), may hold values from -6 to 6
- trajectory: float32 [32, 4, 32, 512], P('tm', None, 'space'), may hold values from -6 to 6
- input_weight: float32 [32, 4, 3, 3], replicated, may hold values from -1 to 1
- bias: float32 [32], replicated, may hold values from -4 to 4
- output_weight: float32 [4, 32, 3, 3], replicated, may hold values from -0.375 to 0.375
- correlation: float32 [4, 32, 32], replicated, may hold values from -1 to 4, as said below
Outputs:
- corrected: float32 [32, 4, 32, 512], P('tm', None, 'space')
The draws below stay inside these ranges and needn't reach their ends.
Inputs may be any that keep to these rules, and one draw needn't show every extreme that they name: `correlation`: each field's matrix is symmetric positive definite.
All inputs are finite; a program needn't handle non-finite values.
Results may differ from the reference program's by a relative error of at most 0.0001.
Values sent between devices are 32-bit elements; how exact they have to be, the bound alone decides.
No kernel may reach another device: no remote copies, remote signals or barrier semaphores. Data moves between devices by JAX's collectives and lax.ppermute only.
A program may use at most 64 MiB of HBM per device.

```python
import jax
import jax.numpy as jnp
from jax import lax

FIELDS = 4
CHANNELS = 32
STEPS = 2
NX = 512
TIME = 32
NY = 32


def draw_correlation(key, part):
    base_rows = jax.random.uniform(key, (FIELDS, TIME, TIME), jnp.float32, -1.7, 1.7)
    gram = jnp.einsum('fik,fjk->fij', base_rows, base_rows) / TIME
    return 0.5 * jnp.eye(TIME, dtype=jnp.float32)[None] + gram


def shard_levels(stream_key, dims, split, smallest, largest):
    def one(dim, shards_of):
        steps = jax.random.uniform(jax.random.fold_in(jax.random.fold_in(stream_key, 6), dim), (shards_of,), jnp.float32, smallest / len(split), largest / len(split))
        return jnp.repeat(jnp.exp(steps), dims[dim] // shards_of).reshape((-1,) + (1,) * (len(dims) - dim - 1))

    level = one(*split[0])
    for cut in split[1:]:
        level = level * one(*cut)
    return level


def centred(stream_key, dims, deviation, reach, split=(), kind=jnp.bfloat16):
    factor_of = shard_levels(stream_key, dims, split, -0.22, 0.18) if split else 1.0
    entries = jax.random.normal(stream_key, dims, jnp.float32) * deviation * factor_of
    return jnp.minimum(jnp.maximum(entries, -reach), reach).astype(kind)


def setup_inputs(seed: int = 0) -> dict:
    arg_keys = jax.random.split(jax.random.key(seed), 7)
    return {
        "increment": centred(arg_keys[0], (TIME, FIELDS, NY, NX), 1.0, 6.0, ((0, 8), (2, 4)), jnp.float32),
        "trajectory": centred(arg_keys[1], (TIME, FIELDS, NY, NX), 1.0, 6.0, ((0, 8), (2, 4)), jnp.float32),
        "input_weight": centred(arg_keys[2], (CHANNELS, FIELDS, 3, 3), (FIELDS * 9) ** -0.5, 1.0, (), jnp.float32),
        "bias": centred(arg_keys[3], (CHANNELS,), 1.0, 4.0, (), jnp.float32),
        "output_weight": centred(arg_keys[4], (FIELDS, CHANNELS, 3, 3), (CHANNELS * 9) ** -0.5, 0.375, (), jnp.float32),
        "correlation": draw_correlation(jax.random.fold_in(arg_keys[6], 71), 0),
    }


tendency_scale = 0.5


def conv_same(field, weight):
    return lax.conv_general_dilated(field, weight, (1, 1), ((1, 1), (1, 1)), dimension_numbers=("NCHW", "OIHW", "NCHW"), precision=lax.Precision.HIGHEST)


def advance_time_slot(input_fields, input_weight, bias, output_weight):
    paired = jnp.stack([input_fields[0], input_fields[1]])
    for step_index in range(STEPS):
        mixed = conv_same(paired, input_weight)
        hidden = jnp.tanh(mixed[0] + bias[:, None, None])
        slope = (1.0 - hidden * hidden) * mixed[1]
        paired = paired + tendency_scale * conv_same(jnp.stack([hidden, slope]), output_weight)
    return paired[1]


def reference(increment, trajectory, input_weight, bias, output_weight, correlation):
    predicted_state = lax.map(lambda input_fields: advance_time_slot(input_fields, input_weight, bias, output_weight), (trajectory, increment))
    prior_state = jnp.concatenate([jnp.zeros_like(predicted_state[:1]), predicted_state[:-1]], axis=0)
    residual = increment - prior_state
    return jnp.einsum("fts,sfyx->tfyx", correlation, residual, precision=lax.Precision.HIGHEST)
```

```python
import functools

import jax
import jax.numpy as jnp
from jax import lax
from jax.experimental import pallas as pl
from jax.experimental.pallas import tpu as pltpu
from jax.sharding import PartitionSpec as P

STEPS = 2
TENDENCY = 0.5
HALO = 2 * STEPS
F32 = jnp.float32
BF16 = jnp.bfloat16
EXACT = lax.Precision.HIGHEST
VMEM = pl.BlockSpec(memory_space=pltpu.VMEM)

WIN_OUT = 4
LANES = 128
KEYS = 256


def iota(shape, dim):
    return lax.broadcasted_iota(jnp.int32, shape, dim)


def split(value):
    high = value.astype(BF16)
    return high, (value - high.astype(F32)).astype(BF16)


def pack_kernel(traj_ref, incr_ref, head_ref, tail_ref):
    slots, fields, rows, _ = traj_ref.shape
    half = rows // 2
    for kind, ref in enumerate((traj_ref, incr_ref)):
        for slot in range(slots):
            for f in range(fields):
                place = pl.ds(f, half, stride=fields)
                for piece in range(head_ref.shape[1]):
                    columns = slice(piece * LANES, (piece + 1) * LANES)
                    head_ref[kind * slots + slot, piece, place, :] = ref[slot, f, 0:half, columns]
                    tail_ref[kind * slots + slot, piece, place, :] = ref[slot, f, half:rows, columns]


def key_codes(shape, dim):
    key = iota(shape, dim)
    tap = (key >= 48).astype(jnp.int32) + (key >= 96).astype(jnp.int32)
    q = key - 48 * tap
    sub = jnp.where(q < 16, q, jnp.where(q < 32, q - 16, jnp.where(q < 40, q - 16, q - 24)))
    high = jnp.where(key < 144, tap * 24 + sub, -1000)
    rest = key - 144
    tap2 = rest // 32
    q2 = rest - 32 * tap2
    sub2 = jnp.where(q2 < 24, q2, q2 - 8)
    low = jnp.where((key >= 144) & (key < 240), tap2 * 24 + sub2, -1000)
    return high, low, key


def prepare_kernel(edge_ref, w1_ref, bias_ref, w2_ref, corr_ref, w1_out, w2_out, w2_last, mix_out, *, tm, slots):
    channels = w1_ref.shape[0]
    fields = corr_ref.shape[0]
    time = corr_ref.shape[1]
    j = iota((36, KEYS), 0)
    f = (j >= 9).astype(jnp.int32) + (j >= 18).astype(jnp.int32) + (j >= 27).astype(jnp.int32)
    r = j - 9 * f
    a = (r >= 3).astype(jnp.int32) + (r >= 6).astype(jnp.int32)
    b = r - 3 * a
    code = b * 24 + a * 4 + f
    high_code, low_code, _ = key_codes((36, KEYS), 1)
    w_high, w_low = split(w1_ref[...])
    bias = bias_ref[...]
    b0 = bias.astype(BF16).astype(F32)
    b1 = (bias - b0).astype(BF16).astype(F32)
    b2 = bias - b0 - b1
    key = iota((channels, KEYS), 1)
    bias_part = (
        jnp.where(key == 240, b0, 0.0) + jnp.where(key == 241, b1, 0.0) + jnp.where(key == 242, b2, 0.0)
    )
    for out in range(WIN_OUT):
        pick_high = jnp.where(code + 4 * out == high_code, 1.0, 0.0).astype(BF16)
        pick_low = jnp.where(code + 4 * out == low_code, 1.0, 0.0).astype(BF16)
        block = jnp.dot(w_high, pick_high, preferred_element_type=F32)
        block += jnp.dot(w_low, pick_low, preferred_element_type=F32)
        w1_out[out * channels : (out + 1) * channels, :] = (block + bias_part).astype(BF16)
    spread = jnp.where(iota((channels, 8 * channels), 1) % channels == iota((channels, 8 * channels), 0), 1.0, 0.0)
    halves = split(w2_ref[...] * TENDENCY)
    tables = [jnp.dot(h, spread.astype(BF16), preferred_element_type=F32).astype(BF16) for h in halves]
    m = iota((72, 8 * channels), 0)
    m_tap = (m >= 24).astype(jnp.int32) + (m >= 48).astype(jnp.int32)
    m_row = (m - 24 * m_tap) // 4
    k_row = iota((72, 8 * channels), 1) // channels
    mj = iota((72, 36), 0)
    mj_tap = (mj >= 24).astype(jnp.int32) + (mj >= 48).astype(jnp.int32)
    mj_field = mj % 4
    full = []
    for table in tables:
        total = jnp.zeros((72, 8 * channels), F32)
        for tap_row in range(3):
            pick = jnp.where(iota((72, 36), 1) == tap_row * 12 + mj_tap * 4 + mj_field, 1.0, 0.0).astype(BF16)
            part = jnp.dot(pick, table, preferred_element_type=F32)
            total = total + jnp.where(k_row == m_row + tap_row, part, 0.0)
        full.append(total)
    top = edge_ref[0]
    bottom = edge_ref[1]
    keep_top = 1.0 - top.astype(F32)
    keep_bottom = 1.0 - bottom.astype(F32)
    for part, total in enumerate(full):
        w2_out[0, part * 72 : (part + 1) * 72, :] = jnp.where(k_row < 3, total * keep_top, total).astype(BF16)
        w2_out[1, part * 72 : (part + 1) * 72, :] = jnp.where(k_row > 4, total * keep_bottom, total).astype(BF16)
        w2_out[2, part * 72 : (part + 1) * 72, :] = jnp.where(k_row < 1, total * keep_top, total).astype(BF16)
        last = jnp.concatenate([total[0:8], total[24:32], total[48:56]], axis=0)
        last_row = iota((24, 8 * channels), 1) // channels
        last = jnp.where(last_row > 2, last * keep_bottom, last)
        w2_last[part * 24 : (part + 1) * 24, :] = last[:, 0 : 4 * channels].astype(BF16)
    keys = mix_out.shape[1]
    block = (slots + 2) * fields
    key = iota((time, keys), 1)
    sender = key // block
    row = key - sender * block
    slot = slots * sender + row // fields
    valid = row < (slots + 1) * fields
    pick = jnp.where((iota((time, keys), 0) == slot) & valid, 1.0, 0.0)
    total = jnp.zeros(mix_out.shape, F32)
    wide = (time * fields, time)
    repeat = jnp.where(iota(wide, 0) // fields == iota(wide, 1), 1.0, 0.0)
    to_field = iota(mix_out.shape, 0) % fields
    from_field = iota(mix_out.shape, 1) % fields
    for f in range(fields):
        part = jnp.dot(corr_ref[f], pick, precision=EXACT, preferred_element_type=F32)
        part = jnp.dot(repeat, part, precision=EXACT, preferred_element_type=F32)
        total = jnp.where((to_field == f) & (from_field == f), part, total)
    mix_out[...] = total


def moved(value, shift):
    if shift == 0:
        return value
    cols = value.shape[1]
    column = iota(value.shape, 1)
    turned = pltpu.roll(value, shift % cols, 1)
    outside = column == (0 if shift > 0 else cols - 1)
    return jnp.where(outside, 0.0, turned)


def hidden_inputs(groups):
    parts = []
    for tap in range(3):
        highs, lows = [], []
        for group in groups:
            value = moved(group, 1 - tap)
            high = value.astype(BF16).astype(F32)
            highs.append(high)
            lows.append(value - high)
        parts.append((highs, lows))
    return parts


def window(parts, start, ones):
    def tile(first, second):
        return jnp.concatenate([first, second], axis=0).astype(BF16)

    front, back = [], []
    for highs, lows in parts:
        a = tile(highs[start], highs[start + 1])
        b = tile(lows[start], lows[start + 1])
        c = tile(highs[start + 2], lows[start + 2])
        front += [a, b, c]
        back += [a, c]
    return jnp.concatenate(front + back + [ones], axis=0)


def hidden_pair(state_groups, tangent_groups, starts, w1):
    cols = state_groups[0].shape[1]
    one = jnp.ones((16, cols), BF16)
    zero = jnp.zeros((16, cols), BF16)
    state_parts = hidden_inputs(state_groups)
    tangent_parts = hidden_inputs(tangent_groups)
    result = []
    for index, start in enumerate(starts):
        rows = w1 if index < len(starts) - 1 else w1[: w1.shape[0] // 2]
        z = jnp.dot(rows, window(state_parts, start, one), preferred_element_type=F32)
        dz = jnp.dot(rows, window(tangent_parts, start, zero), preferred_element_type=F32)
        h = jnp.tanh(z)
        g = (1.0 - h * h) * dz
        result.append((h, g))
    return result


def output_sum(pieces, weight):
    half = weight.shape[0] // 2
    high = jnp.concatenate([p[0] for p in pieces], axis=0)
    low = jnp.concatenate([p[1] for p in pieces], axis=0)
    both = jnp.dot(weight, high, preferred_element_type=F32)
    taps = both[:half] + both[half:] + jnp.dot(weight[:half], low, preferred_element_type=F32)
    third = half // 3
    return moved(taps[0:third], 1) + taps[third : 2 * third] + moved(taps[2 * third :], -1)


def forecast_kernel(
    edge_ref, head_ref, tail_ref, top_ref, bottom_ref, w1_ref, w2_ref, w2_last_ref, send_ref, done_ref, *, slots, parts_across
):
    channels = w1_ref.shape[0] // WIN_OUT
    pieces = head_ref.shape[1]
    cols = pieces * LANES
    keep_top = 1.0 - edge_ref[0].astype(F32)
    keep_bottom = 1.0 - edge_ref[1].astype(F32)
    blank = jnp.zeros((8, cols), F32)

    def group_of(ref, index, half):
        return jnp.concatenate([ref[index, p, 8 * half : 8 * half + 8, :] for p in range(pieces)], axis=1)

    def one_slot(slot, carry):
        frames = []
        for kind in range(2):
            index = kind * slots + slot
            groups = []
            for ref in (top_ref, head_ref, tail_ref, bottom_ref):
                groups += [group_of(ref, index, 0), group_of(ref, index, 1)]
            frames.append(groups + [blank])
        w1 = w1_ref[...]
        windows = hidden_pair(frames[0], frames[1], (0, 2, 4, 6), w1)
        advanced = []
        for kind in range(2):
            halves = [split(pair[kind]) for pair in windows]
            mid = 2 * channels
            upper = output_sum([halves[0], halves[1]], w2_ref[0])
            lower = output_sum(
                [tuple(p[mid:] for p in halves[1]), halves[2], halves[3]], w2_ref[1]
            )
            groups = [blank] + [frames[kind][g] for g in range(1, 7)] + [blank, blank]
            for g in range(3):
                groups[1 + g] = groups[1 + g] + upper[8 * g : 8 * g + 8]
                groups[4 + g] = groups[4 + g] + lower[8 * g : 8 * g + 8]
            groups[1] = groups[1] * keep_top
            groups[6] = groups[6] * keep_bottom
            advanced.append(groups)
        windows = hidden_pair(advanced[0], advanced[1], (1, 3, 5), w1)
        halves = [split(pair[1]) for pair in windows]
        upper = output_sum([halves[0], halves[1]], w2_ref[2])
        lower = output_sum([tuple(p[2 * channels :] for p in halves[1]), halves[2]], w2_last_ref[...])
        tangent = advanced[1]
        for g in range(3):
            done_ref[slot, 8 * g : 8 * g + 8, :] = tangent[2 + g] + upper[8 * g : 8 * g + 8]
        done_ref[slot, 24:32, :] = tangent[5] + lower
        return carry

    lax.fori_loop(0, slots, one_slot, 0)

    width = cols // parts_across
    fields = 4
    rows = 8
    for slot in range(slots + 1):
        if slot < slots:
            index = slots + slot
            start = jnp.concatenate([group_of(ref, index, h) for ref in (head_ref, tail_ref) for h in range(2)], axis=0)
            value = start - done_ref[slot - 1] if slot else start
        else:
            value = -done_ref[slot - 1]
        for y in range(rows):
            for block in range(parts_across):
                send_ref[y * parts_across + block, slot * fields : (slot + 1) * fields, :] = value[
                    y * fields : (y + 1) * fields, block * width : (block + 1) * width
                ]
    send_ref[:, (slots + 1) * fields :, :] = jnp.zeros((rows * parts_across, fields, width), F32)


def mix_kernel(mix_ref, block_ref, out_ref):
    count, rows, width = block_ref.shape
    keys = block_ref[...].reshape(count * rows, width)
    out = jnp.dot(mix_ref[...], keys, precision=EXACT, preferred_element_type=F32)
    out_ref[...] = out.reshape(out_ref.shape)


def params():
    return pltpu.CompilerParams(vmem_limit_bytes=24 * 1024 * 1024)


def body(increment, trajectory, input_weight, bias, output_weight, correlation):
    slots, fields, rows, cols = increment.shape
    channels = input_weight.shape[0]
    tm = lax.axis_size("tm")
    strips = lax.axis_size("space")
    time = correlation.shape[1]
    parts_across = tm // rows
    width = cols // parts_across
    me = lax.axis_index("space")
    edges = jnp.stack([me == 0, me == strips - 1]).astype(jnp.int32)

    half = jax.ShapeDtypeStruct((2 * slots, cols // LANES, rows // 2 * fields, LANES), F32)
    head, tail = pl.pallas_call(
        pack_kernel, out_shape=(half, half), in_specs=[VMEM] * 2, out_specs=(VMEM, VMEM), compiler_params=params(), name="pack"
    )(trajectory, increment)
    top = lax.ppermute(tail, "space", [(i, i + 1) for i in range(strips - 1)])
    bottom = lax.ppermute(head, "space", [(i + 1, i) for i in range(strips - 1)])

    block_rows = (slots + 2) * fields
    smem = pl.BlockSpec(memory_space=pltpu.SMEM)
    w1, w2, w2_last, mix = pl.pallas_call(
        functools.partial(prepare_kernel, tm=tm, slots=slots),
        out_shape=(
            jax.ShapeDtypeStruct((WIN_OUT * channels, KEYS), BF16),
            jax.ShapeDtypeStruct((3, 144, 8 * channels), BF16),
            jax.ShapeDtypeStruct((48, 4 * channels), BF16),
            jax.ShapeDtypeStruct((time * fields, tm * block_rows), F32),
        ),
        in_specs=[smem] + [VMEM] * 4,
        out_specs=(VMEM,) * 4,
        compiler_params=params(),
        name="prepare",
    )(
        edges,
        input_weight.reshape(channels, -1),
        bias[:, None],
        jnp.transpose(output_weight, (2, 3, 0, 1)).reshape(-1, channels),
        correlation,
    )

    send = pl.pallas_call(
        functools.partial(forecast_kernel, slots=slots, parts_across=parts_across),
        out_shape=jax.ShapeDtypeStruct((tm, block_rows, width), F32),
        in_specs=[smem] + [VMEM] * 7,
        out_specs=VMEM,
        scratch_shapes=[pltpu.VMEM((slots, rows * fields, cols), F32)],
        compiler_params=params(),
        name="forecast",
    )(edges, head, tail, top, bottom, w1, w2, w2_last)

    blocks = lax.all_to_all(send, "tm", split_axis=0, concat_axis=0, tiled=True)
    mixed = pl.pallas_call(
        mix_kernel,
        out_shape=jax.ShapeDtypeStruct((tm, slots * fields, width), F32),
        in_specs=[VMEM] * 2,
        out_specs=VMEM,
        compiler_params=params(),
        name="mix",
    )(mix, blocks)
    back = lax.all_to_all(mixed, "tm", split_axis=0, concat_axis=0, tiled=True)
    back = back.reshape(rows, parts_across, slots, fields, width)
    return jnp.transpose(back, (2, 3, 0, 1, 4)).reshape(slots, fields, rows, cols)


def solution(mesh):
    placed = (P("tm", None, "space", None), P("tm", None, "space", None), P(), P(), P(), P())
    return jax.shard_map(
        body, mesh=mesh, in_specs=placed, out_specs=P("tm", None, "space", None), check_vma=False
    )
```

```python
import functools

import jax
import jax.numpy as jnp
from jax import lax
from jax.experimental import pallas as pl
from jax.experimental.pallas import tpu as pltpu
from jax.sharding import PartitionSpec as P

STEPS = 2
TENDENCY = 0.5
HALO = 2 * STEPS
F32 = jnp.float32
BF16 = jnp.bfloat16
EXACT = lax.Precision.HIGHEST
VMEM = pl.BlockSpec(memory_space=pltpu.VMEM)

WIN_OUT = 4
LANES = 128
KEYS = 256


def iota(shape, dim):
    return lax.broadcasted_iota(jnp.int32, shape, dim)


def split(value):
    high = value.astype(BF16)
    return high, (value - high.astype(F32)).astype(BF16)


def pack_kernel(
    traj_hbm, incr_hbm, w1_hbm, bias_hbm, w2_hbm, corr_hbm,
    own_ref, core_ref, chip_ref, w1_ref, bias_ref, w2_ref, corr_ref,
    traj_ref, incr_ref, sems,
):
    pairs = (
        (traj_hbm, traj_ref), (incr_hbm, incr_ref), (w1_hbm, w1_ref), (bias_hbm, bias_ref), (w2_hbm, w2_ref), (corr_hbm, corr_ref)
    )
    copies = [pltpu.make_async_copy(src, dst, sems.at[n]) for n, (src, dst) in enumerate(pairs)]
    for copy in copies:
        copy.start()
    slots, fields, rows, _ = traj_ref.shape
    half = rows // 2 * fields
    odd = lax.axis_index("space") % 2
    core_half = pl.ds(pl.multiple_of((1 - odd) * half, half), half)
    chip_half = pl.ds(pl.multiple_of(odd * half, half), half)
    for kind, ref in enumerate((traj_ref, incr_ref)):
        copies[kind].wait()
        for slot in range(slots):
            index = kind * slots + slot
            for piece in range(own_ref.shape[1]):
                for f in range(fields):
                    own_ref[index, piece, pl.ds(f, rows, stride=fields), :] = ref[
                        slot, f, :, piece * LANES : (piece + 1) * LANES
                    ]
                core_ref[index, piece] = own_ref[index, piece, core_half, :]
                chip_ref[index, piece] = own_ref[index, piece, chip_half, :]
    for copy in copies[2:]:
        copy.wait()


def key_codes(shape, dim):
    key = iota(shape, dim)
    tap = (key >= 48).astype(jnp.int32) + (key >= 96).astype(jnp.int32)
    q = key - 48 * tap
    sub = jnp.where(q < 16, q, jnp.where(q < 32, q - 16, jnp.where(q < 40, q - 16, q - 24)))
    high = jnp.where(key < 144, tap * 24 + sub, -1000)
    rest = key - 144
    tap2 = rest // 32
    q2 = rest - 32 * tap2
    sub2 = jnp.where(q2 < 24, q2, q2 - 8)
    low = jnp.where((key >= 144) & (key < 240), tap2 * 24 + sub2, -1000)
    return high, low, key


def prepare_kernel(w1_ref, bias_ref, w2_ref, corr_ref, w1_out, w2_out, w2_last, mix_out, *, strips, slots):
    fields = w1_ref.shape[2]
    channels = w1_ref.shape[3]
    time = corr_ref.shape[1]
    taps = [(a, b) for a in range(3) for b in range(3)]
    j = iota((40, KEYS), 0)
    t = j // 4
    a = (t >= 3).astype(jnp.int32) + (t >= 6).astype(jnp.int32)
    code = jnp.where(j < 36, (t - 3 * a) * 24 + a * 4 + j % 4, -5000)
    high_code, low_code, key = key_codes((40, KEYS), 1)
    table = jnp.concatenate(
        [w1_ref[a, b] for a, b in taps] + [bias_ref[...], jnp.zeros((3, channels), F32)], axis=0
    )
    w_high, w_low = split(table)
    bias_row = j == 36
    over_rows = (((0,), (0,)), ((), ()))
    for out in range(WIN_OUT):
        pick_high = jnp.where((code + 4 * out == high_code) | (bias_row & (key == 240)), 1.0, 0.0).astype(BF16)
        pick_low = jnp.where((code + 4 * out == low_code) | (bias_row & (key == 241)), 1.0, 0.0).astype(BF16)
        block = lax.dot_general(w_high, pick_high, over_rows, preferred_element_type=F32)
        block += lax.dot_general(w_low, pick_low, over_rows, preferred_element_type=F32)
        w1_out[out * channels : (out + 1) * channels, :] = block.astype(BF16)
    spread = jnp.where(iota((channels, 8 * channels), 1) % channels == iota((channels, 8 * channels), 0), 1.0, 0.0)
    halves = split(jnp.concatenate([w2_ref[a, b] for a, b in taps], axis=0) * TENDENCY)
    tables = [jnp.dot(h, spread.astype(BF16), preferred_element_type=F32).astype(BF16) for h in halves]
    m = iota((72, 8 * channels), 0)
    m_tap = (m >= 24).astype(jnp.int32) + (m >= 48).astype(jnp.int32)
    m_row = (m - 24 * m_tap) // 4
    k_row = iota((72, 8 * channels), 1) // channels
    mj = iota((72, 36), 0)
    mj_tap = (mj >= 24).astype(jnp.int32) + (mj >= 48).astype(jnp.int32)
    mj_field = mj % 4
    full = []
    for table in tables:
        total = jnp.zeros((72, 8 * channels), F32)
        for tap_row in range(3):
            pick = jnp.where(iota((72, 36), 1) == tap_row * 12 + mj_tap * 4 + mj_field, 1.0, 0.0).astype(BF16)
            part = jnp.dot(pick, table, preferred_element_type=F32)
            total = total + jnp.where(k_row == m_row + tap_row, part, 0.0)
        full.append(total)
    keep_top, keep_bottom = inside(strips)
    for part, total in enumerate(full):
        w2_out[0, part * 72 : (part + 1) * 72, :] = jnp.where(k_row < 3, total * keep_top, total).astype(BF16)
        w2_out[1, part * 72 : (part + 1) * 72, :] = jnp.where(k_row > 4, total * keep_bottom, total).astype(BF16)
        w2_out[2, part * 72 : (part + 1) * 72, :] = jnp.where(k_row < 1, total * keep_top, total).astype(BF16)
        last = jnp.concatenate([total[0:8], total[24:32], total[48:56]], axis=0)
        last_row = iota((24, 8 * channels), 1) // channels
        last = jnp.where(last_row > 2, last * keep_bottom, last)
        w2_last[part * 24 : (part + 1) * 24, :] = last[:, 0 : 4 * channels].astype(BF16)
    keys = mix_out.shape[1]
    block = (slots + 2) * fields
    key = iota((time, keys), 1)
    sender = key // block
    row = key - sender * block
    slot = slots * sender + row // fields
    valid = row < (slots + 1) * fields
    pick = jnp.where((iota((time, keys), 0) == slot) & valid, 1.0, 0.0)
    total = jnp.zeros(mix_out.shape, F32)
    wide = (time * fields, time)
    repeat = jnp.where(iota(wide, 0) // fields == iota(wide, 1), 1.0, 0.0)
    to_field = iota(mix_out.shape, 0) % fields
    from_field = iota(mix_out.shape, 1) % fields
    for f in range(fields):
        part = jnp.dot(corr_ref[f], pick, precision=EXACT, preferred_element_type=F32)
        part = jnp.dot(repeat, part, precision=EXACT, preferred_element_type=F32)
        total = jnp.where((to_field == f) & (from_field == f), part, total)
    mix_out[...] = total


def moved(value, shift):
    if shift == 0:
        return value
    cols = value.shape[1]
    column = iota(value.shape, 1)
    turned = pltpu.roll(value, shift % cols, 1)
    outside = column == (0 if shift > 0 else cols - 1)
    return jnp.where(outside, 0.0, turned)


def hidden_inputs(groups):
    parts = []
    for tap in range(3):
        highs, lows = [], []
        for group in groups:
            value = moved(group, 1 - tap)
            high = value.astype(BF16).astype(F32)
            highs.append(high)
            lows.append(value - high)
        parts.append((highs, lows))
    return parts


def window(parts, start, ones):
    def tile(first, second):
        return jnp.concatenate([first, second], axis=0).astype(BF16)

    front, back = [], []
    for highs, lows in parts:
        a = tile(highs[start], highs[start + 1])
        b = tile(lows[start], lows[start + 1])
        c = tile(highs[start + 2], lows[start + 2])
        front += [a, b, c]
        back += [a, c]
    return jnp.concatenate(front + back + [ones], axis=0)


def hidden_pair(state_groups, tangent_groups, starts, w1):
    cols = state_groups[0].shape[1]
    one = jnp.ones((16, cols), BF16)
    zero = jnp.zeros((16, cols), BF16)
    state_parts = hidden_inputs(state_groups)
    tangent_parts = hidden_inputs(tangent_groups)
    result = []
    for index, start in enumerate(starts):
        rows = w1 if index < len(starts) - 1 else w1[: w1.shape[0] // 2]
        z = jnp.dot(rows, window(state_parts, start, one), preferred_element_type=F32)
        dz = jnp.dot(rows, window(tangent_parts, start, zero), preferred_element_type=F32)
        h = jnp.tanh(z)
        g = (1.0 - h * h) * dz
        result.append((h, g))
    return result


def output_sum(pieces, weight):
    half = weight.shape[0] // 2
    high = jnp.concatenate([p[0] for p in pieces], axis=0)
    low = jnp.concatenate([p[1] for p in pieces], axis=0)
    both = jnp.dot(weight, high, preferred_element_type=F32)
    taps = both[:half] + both[half:] + jnp.dot(weight[:half], low, preferred_element_type=F32)
    third = half // 3
    return moved(taps[0:third], 1) + taps[third : 2 * third] + moved(taps[2 * third :], -1)


def inside(strips):
    me = lax.axis_index("space")
    return jnp.where(me == 0, 0.0, 1.0), jnp.where(me == strips - 1, 0.0, 1.0)


def forecast_kernel(
    own_ref, core_got_ref, chip_got_ref, w1_ref, w2_ref, w2_last_ref, send_ref, done_ref, *, strips, slots, parts_across
):
    channels = w1_ref.shape[0] // WIN_OUT
    pieces = own_ref.shape[1]
    cols = pieces * LANES
    keep_top, keep_bottom = inside(strips)
    even = lax.axis_index("space") % 2 == 0
    blank = jnp.zeros((8, cols), F32)

    def own_group(index, g):
        return jnp.concatenate([own_ref[index, p, 8 * g : 8 * g + 8, :] for p in range(pieces)], axis=1)

    def got_group(above, index, g):
        first, second = (chip_got_ref, core_got_ref) if above else (core_got_ref, chip_got_ref)
        part = slice(8 * g, 8 * g + 8)
        return jnp.concatenate(
            [jnp.where(even, first[index, p, part, :], second[index, p, part, :]) for p in range(pieces)], axis=1
        )

    def one_slot(slot, carry):
        frames = []
        for kind in range(2):
            index = kind * slots + slot
            groups = [got_group(True, index, g) for g in range(2)]
            groups += [own_group(index, g) for g in range(4)]
            groups += [got_group(False, index, g) for g in range(2)]
            frames.append(groups + [blank])
        w1 = w1_ref[...]
        windows = hidden_pair(frames[0], frames[1], (0, 2, 4, 6), w1)
        advanced = []
        for kind in range(2):
            halves = [split(pair[kind]) for pair in windows]
            mid = 2 * channels
            upper = output_sum([halves[0], halves[1]], w2_ref[0])
            lower = output_sum(
                [tuple(p[mid:] for p in halves[1]), halves[2], halves[3]], w2_ref[1]
            )
            groups = [blank] + [frames[kind][g] for g in range(1, 7)] + [blank, blank]
            for g in range(3):
                groups[1 + g] = groups[1 + g] + upper[8 * g : 8 * g + 8]
                groups[4 + g] = groups[4 + g] + lower[8 * g : 8 * g + 8]
            groups[1] = groups[1] * keep_top
            groups[6] = groups[6] * keep_bottom
            advanced.append(groups)
        windows = hidden_pair(advanced[0], advanced[1], (1, 3, 5), w1)
        halves = [split(pair[1]) for pair in windows]
        upper = output_sum([halves[0], halves[1]], w2_ref[2])
        lower = output_sum([tuple(p[2 * channels :] for p in halves[1]), halves[2]], w2_last_ref[...])
        tangent = advanced[1]
        for g in range(3):
            done_ref[slot, 8 * g : 8 * g + 8, :] = tangent[2 + g] + upper[8 * g : 8 * g + 8]
        done_ref[slot, 24:32, :] = tangent[5] + lower
        return carry

    lax.fori_loop(0, slots, one_slot, 0)

    width = cols // parts_across
    fields = 4
    rows = 8
    for slot in range(slots + 1):
        if slot < slots:
            index = slots + slot
            start = jnp.concatenate([own_group(index, g) for g in range(4)], axis=0)
            value = start - done_ref[slot - 1] if slot else start
        else:
            value = -done_ref[slot - 1]
        for y in range(rows):
            for block in range(parts_across):
                send_ref[y * parts_across + block, slot * fields : (slot + 1) * fields, :] = value[
                    y * fields : (y + 1) * fields, block * width : (block + 1) * width
                ]
    send_ref[:, (slots + 1) * fields :, :] = jnp.zeros((rows * parts_across, fields, width), F32)


def mix_kernel(mix_ref, block_ref, out_ref):
    count, rows, width = block_ref.shape
    keys = block_ref[...].reshape(count * rows, width)
    out = jnp.dot(mix_ref[...], keys, precision=EXACT, preferred_element_type=F32)
    out_ref[...] = out.reshape(out_ref.shape)


def params():
    return pltpu.CompilerParams(vmem_limit_bytes=24 * 1024 * 1024)


def body(increment, trajectory, input_weight, bias, output_weight, correlation):
    slots, fields, rows, cols = increment.shape
    channels = input_weight.shape[0]
    tm = lax.axis_size("tm")
    strips = lax.axis_size("space")
    time = correlation.shape[1]
    parts_across = tm // rows
    width = cols // parts_across

    hbm = pl.BlockSpec(memory_space=pltpu.HBM)
    whole = jax.ShapeDtypeStruct((2 * slots, cols // LANES, rows * fields, LANES), F32)
    half = jax.ShapeDtypeStruct((2 * slots, cols // LANES, rows // 2 * fields, LANES), F32)
    w1_taps = jnp.transpose(input_weight, (2, 3, 1, 0))
    w2_taps = jnp.transpose(output_weight, (2, 3, 0, 1))
    loaded = [
        jax.ShapeDtypeStruct(shape, F32) for shape in (w1_taps.shape, (1, channels), w2_taps.shape, correlation.shape)
    ]
    strip = pltpu.VMEM(increment.shape, F32)
    own, core, chip, w1_taps, bias_row, w2_taps, correlation = pl.pallas_call(
        pack_kernel,
        out_shape=(whole, half, half, *loaded),
        in_specs=[hbm] * 6,
        out_specs=(VMEM,) * 7,
        scratch_shapes=[strip, strip, pltpu.SemaphoreType.DMA((6,))],
        compiler_params=params(),
        name="pack",
    )(trajectory, increment, w1_taps, bias[None], w2_taps, correlation)

    def swapped(value, first):
        pairs = [(i, i + 1) for i in range(first, strips - 1, 2)]
        return lax.ppermute(value, "space", pairs + [(j, i) for i, j in pairs])

    chip_got = swapped(chip, 1)
    core_got = swapped(core, 0)

    block_rows = (slots + 2) * fields
    w1, w2, w2_last, mix = pl.pallas_call(
        functools.partial(prepare_kernel, strips=strips, slots=slots),
        out_shape=(
            jax.ShapeDtypeStruct((WIN_OUT * channels, KEYS), BF16),
            jax.ShapeDtypeStruct((3, 144, 8 * channels), BF16),
            jax.ShapeDtypeStruct((48, 4 * channels), BF16),
            jax.ShapeDtypeStruct((time * fields, tm * block_rows), F32),
        ),
        in_specs=[VMEM] * 4,
        out_specs=(VMEM,) * 4,
        compiler_params=params(),
        name="prepare",
    )(w1_taps, bias_row, w2_taps, correlation)

    send = pl.pallas_call(
        functools.partial(forecast_kernel, strips=strips, slots=slots, parts_across=parts_across),
        out_shape=jax.ShapeDtypeStruct((tm, block_rows, width), F32),
        in_specs=[VMEM] * 6,
        out_specs=VMEM,
        scratch_shapes=[pltpu.VMEM((slots, rows * fields, cols), F32)],
        compiler_params=params(),
        name="forecast",
    )(own, core_got, chip_got, w1, w2, w2_last)

    blocks = lax.all_to_all(send, "tm", split_axis=0, concat_axis=0, tiled=True)
    mixed = pl.pallas_call(
        mix_kernel,
        out_shape=jax.ShapeDtypeStruct((tm, slots * fields, width), F32),
        in_specs=[VMEM] * 2,
        out_specs=VMEM,
        compiler_params=params(),
        name="mix",
    )(mix, blocks)
    back = lax.all_to_all(mixed, "tm", split_axis=0, concat_axis=0, tiled=True)
    back = back.reshape(rows, parts_across, slots, fields, width)
    return jnp.transpose(back, (2, 3, 0, 1, 4)).reshape(slots, fields, rows, cols)


def solution(mesh):
    placed = (P("tm", None, "space", None), P("tm", None, "space", None), P(), P(), P(), P())
    return jax.shard_map(
        body, mesh=mesh, in_specs=placed, out_specs=P("tm", None, "space", None), check_vma=False
    )
```

```python
import functools

import jax
import jax.numpy as jnp
from jax import lax
from jax.experimental import pallas as pl
from jax.experimental.pallas import tpu as pltpu
from jax.sharding import PartitionSpec as P

STEPS = 2
TENDENCY = 0.5
HALO = 2 * STEPS
F32 = jnp.float32
BF16 = jnp.bfloat16
EXACT = lax.Precision.HIGHEST
VMEM = pl.BlockSpec(memory_space=pltpu.VMEM)

WIN_OUT = 4
LANES = 128
KEYS = 256


def iota(shape, dim):
    return lax.broadcasted_iota(jnp.int32, shape, dim)


def split(value):
    high = value.astype(BF16)
    return high, (value - high.astype(F32)).astype(BF16)


def pack_kernel(
    traj_hbm, incr_hbm, w1_hbm, bias_hbm, w2_hbm, corr_hbm,
    own_ref, core_ref, chip_ref, w1_ref, bias_ref, w2_ref, corr_ref,
    traj_ref, incr_ref, sems,
):
    pairs = (
        (traj_hbm, traj_ref), (incr_hbm, incr_ref), (w1_hbm, w1_ref), (bias_hbm, bias_ref), (w2_hbm, w2_ref), (corr_hbm, corr_ref)
    )
    copies = [pltpu.make_async_copy(src, dst, sems.at[n]) for n, (src, dst) in enumerate(pairs)]
    for copy in copies:
        copy.start()
    slots, fields, rows, _ = traj_ref.shape
    half = rows // 2 * fields
    odd = lax.axis_index("space") % 2
    core_half = pl.ds(pl.multiple_of((1 - odd) * half, half), half)
    chip_half = pl.ds(pl.multiple_of(odd * half, half), half)
    for kind, ref in enumerate((traj_ref, incr_ref)):
        copies[kind].wait()
        for slot in range(slots):
            index = kind * slots + slot
            for piece in range(own_ref.shape[1]):
                for f in range(fields):
                    own_ref[index, piece, pl.ds(f, rows, stride=fields), :] = ref[
                        slot, f, :, piece * LANES : (piece + 1) * LANES
                    ]
                core_ref[index, piece] = own_ref[index, piece, core_half, :]
                chip_ref[index, piece] = own_ref[index, piece, chip_half, :]
    for copy in copies[2:]:
        copy.wait()


def key_codes(shape, dim):
    key = iota(shape, dim)
    tap = (key >= 48).astype(jnp.int32) + (key >= 96).astype(jnp.int32)
    q = key - 48 * tap
    sub = jnp.where(q < 16, q, jnp.where(q < 32, q - 16, jnp.where(q < 40, q - 16, q - 24)))
    high = jnp.where(key < 144, tap * 24 + sub, -1000)
    rest = key - 144
    tap2 = rest // 32
    q2 = rest - 32 * tap2
    sub2 = jnp.where(q2 < 24, q2, q2 - 8)
    low = jnp.where((key >= 144) & (key < 240), tap2 * 24 + sub2, -1000)
    return high, low, key


def prepare_kernel(w1_ref, bias_ref, w2_ref, corr_ref, w1_out, w2_out, w2_last, mix_out, *, strips, slots):
    fields = w1_ref.shape[2]
    channels = w1_ref.shape[3]
    time = corr_ref.shape[1]
    taps = [(a, b) for a in range(3) for b in range(3)]
    j = iota((40, KEYS), 0)
    t = j // 4
    a = (t >= 3).astype(jnp.int32) + (t >= 6).astype(jnp.int32)
    code = jnp.where(j < 36, (t - 3 * a) * 24 + a * 4 + j % 4, -5000)
    high_code, low_code, key = key_codes((40, KEYS), 1)
    table = jnp.concatenate(
        [w1_ref[a, b] for a, b in taps] + [bias_ref[...], jnp.zeros((3, channels), F32)], axis=0
    )
    w_high, w_low = split(table)
    bias_row = j == 36
    over_rows = (((0,), (0,)), ((), ()))
    for out in range(WIN_OUT):
        pick_high = jnp.where((code + 4 * out == high_code) | (bias_row & (key == 240)), 1.0, 0.0).astype(BF16)
        pick_low = jnp.where((code + 4 * out == low_code) | (bias_row & (key == 241)), 1.0, 0.0).astype(BF16)
        block = lax.dot_general(w_high, pick_high, over_rows, preferred_element_type=F32)
        block += lax.dot_general(w_low, pick_low, over_rows, preferred_element_type=F32)
        w1_out[out * channels : (out + 1) * channels, :] = block.astype(BF16)
    spread = jnp.where(iota((channels, 8 * channels), 1) % channels == iota((channels, 8 * channels), 0), 1.0, 0.0)
    halves = split(jnp.concatenate([w2_ref[a, b] for a, b in taps], axis=0) * TENDENCY)
    tables = [jnp.dot(h, spread.astype(BF16), preferred_element_type=F32).astype(BF16) for h in halves]
    m = iota((72, 8 * channels), 0)
    m_tap = (m >= 24).astype(jnp.int32) + (m >= 48).astype(jnp.int32)
    m_row = (m - 24 * m_tap) // 4
    k_row = iota((72, 8 * channels), 1) // channels
    mj = iota((72, 36), 0)
    mj_tap = (mj >= 24).astype(jnp.int32) + (mj >= 48).astype(jnp.int32)
    mj_field = mj % 4
    full = []
    for table in tables:
        total = jnp.zeros((72, 8 * channels), F32)
        for tap_row in range(3):
            pick = jnp.where(iota((72, 36), 1) == tap_row * 12 + mj_tap * 4 + mj_field, 1.0, 0.0).astype(BF16)
            part = jnp.dot(pick, table, preferred_element_type=F32)
            total = total + jnp.where(k_row == m_row + tap_row, part, 0.0)
        full.append(total)
    keep_top, keep_bottom = inside(strips)
    for part, total in enumerate(full):
        w2_out[0, part * 72 : (part + 1) * 72, :] = jnp.where(k_row < 3, total * keep_top, total).astype(BF16)
        w2_out[1, part * 72 : (part + 1) * 72, :] = jnp.where(k_row > 4, total * keep_bottom, total).astype(BF16)
        w2_out[2, part * 72 : (part + 1) * 72, :] = jnp.where(k_row < 1, total * keep_top, total).astype(BF16)
        last = jnp.concatenate([total[0:8], total[24:32], total[48:56]], axis=0)
        last_row = iota((24, 8 * channels), 1) // channels
        last = jnp.where(last_row > 2, last * keep_bottom, last)
        w2_last[part * 24 : (part + 1) * 24, :] = last[:, 0 : 4 * channels].astype(BF16)
    keys = mix_out.shape[1]
    block = (slots + 2) * fields
    key = iota((time, keys), 1)
    sender = key // block
    row = key - sender * block
    slot = slots * sender + row // fields
    valid = row < (slots + 1) * fields
    pick = jnp.where((iota((time, keys), 0) == slot) & valid, 1.0, 0.0)
    total = jnp.zeros(mix_out.shape, F32)
    wide = (time * fields, time)
    repeat = jnp.where(iota(wide, 0) // fields == iota(wide, 1), 1.0, 0.0)
    to_field = iota(mix_out.shape, 0) % fields
    from_field = iota(mix_out.shape, 1) % fields
    for f in range(fields):
        part = jnp.dot(corr_ref[f], pick, precision=EXACT, preferred_element_type=F32)
        part = jnp.dot(repeat, part, precision=EXACT, preferred_element_type=F32)
        total = jnp.where((to_field == f) & (from_field == f), part, total)
    mix_out[...] = total


def moved(value, shift):
    if shift == 0:
        return value
    cols = value.shape[1]
    column = iota(value.shape, 1)
    turned = pltpu.roll(value, shift % cols, 1)
    outside = column == (0 if shift > 0 else cols - 1)
    return jnp.where(outside, 0.0, turned)


def hidden_inputs(groups):
    parts = []
    for tap in range(3):
        highs, lows = [], []
        for group in groups:
            value = moved(group, 1 - tap)
            high = value.astype(BF16).astype(F32)
            highs.append(high)
            lows.append(value - high)
        parts.append((highs, lows))
    return parts


def window(parts, start, ones):
    def tile(first, second):
        return jnp.concatenate([first, second], axis=0).astype(BF16)

    front, back = [], []
    for highs, lows in parts:
        a = tile(highs[start], highs[start + 1])
        b = tile(lows[start], lows[start + 1])
        c = tile(highs[start + 2], lows[start + 2])
        front += [a, b, c]
        back += [a, c]
    return jnp.concatenate(front + back + [ones], axis=0)


def hidden_pair(state_groups, tangent_groups, starts, w1):
    cols = state_groups[0].shape[1]
    one = jnp.ones((16, cols), BF16)
    zero = jnp.zeros((16, cols), BF16)
    state_parts = hidden_inputs(state_groups)
    tangent_parts = hidden_inputs(tangent_groups)
    result = []
    for index, start in enumerate(starts):
        rows = w1 if index < len(starts) - 1 else w1[: w1.shape[0] // 2]
        z = jnp.dot(rows, window(state_parts, start, one), preferred_element_type=F32)
        dz = jnp.dot(rows, window(tangent_parts, start, zero), preferred_element_type=F32)
        h = jnp.tanh(z)
        g = (1.0 - h * h) * dz
        result.append((h, g))
    return result


def output_sum(pieces, weight):
    half = weight.shape[0] // 2
    high = jnp.concatenate([p[0] for p in pieces], axis=0)
    low = jnp.concatenate([p[1] for p in pieces], axis=0)
    both = jnp.dot(weight, high, preferred_element_type=F32)
    taps = both[:half] + both[half:] + jnp.dot(weight[:half], low, preferred_element_type=F32)
    third = half // 3
    return moved(taps[0:third], 1) + taps[third : 2 * third] + moved(taps[2 * third :], -1)


def inside(strips):
    me = lax.axis_index("space")
    return jnp.where(me == 0, 0.0, 1.0), jnp.where(me == strips - 1, 0.0, 1.0)


def forecast_kernel(
    own_ref, core_got_ref, chip_got_ref, w1_ref, w2_ref, w2_last_ref, send_ref, done_ref, *, strips, slots, parts_across
):
    channels = w1_ref.shape[0] // WIN_OUT
    pieces = own_ref.shape[1]
    cols = pieces * LANES
    keep_top, keep_bottom = inside(strips)
    even = lax.axis_index("space") % 2 == 0
    blank = jnp.zeros((8, cols), F32)

    def own_group(index, g):
        return jnp.concatenate([own_ref[index, p, 8 * g : 8 * g + 8, :] for p in range(pieces)], axis=1)

    def got_group(above, index, g):
        first, second = (chip_got_ref, core_got_ref) if above else (core_got_ref, chip_got_ref)
        part = slice(8 * g, 8 * g + 8)
        return jnp.concatenate(
            [jnp.where(even, first[index, p, part, :], second[index, p, part, :]) for p in range(pieces)], axis=1
        )

    def one_slot(slot, carry):
        frames = []
        for kind in range(2):
            index = kind * slots + slot
            groups = [got_group(True, index, g) for g in range(2)]
            groups += [own_group(index, g) for g in range(4)]
            groups += [got_group(False, index, g) for g in range(2)]
            frames.append(groups + [blank])
        w1 = w1_ref[...]
        windows = hidden_pair(frames[0], frames[1], (0, 2, 4, 6), w1)
        advanced = []
        for kind in range(2):
            halves = [split(pair[kind]) for pair in windows]
            mid = 2 * channels
            upper = output_sum([halves[0], halves[1]], w2_ref[0])
            lower = output_sum(
                [tuple(p[mid:] for p in halves[1]), halves[2], halves[3]], w2_ref[1]
            )
            groups = [blank] + [frames[kind][g] for g in range(1, 7)] + [blank, blank]
            for g in range(3):
                groups[1 + g] = groups[1 + g] + upper[8 * g : 8 * g + 8]
                groups[4 + g] = groups[4 + g] + lower[8 * g : 8 * g + 8]
            groups[1] = groups[1] * keep_top
            groups[6] = groups[6] * keep_bottom
            advanced.append(groups)
        windows = hidden_pair(advanced[0], advanced[1], (1, 3, 5), w1)
        halves = [split(pair[1]) for pair in windows]
        upper = output_sum([halves[0], halves[1]], w2_ref[2])
        lower = output_sum([tuple(p[2 * channels :] for p in halves[1]), halves[2]], w2_last_ref[...])
        tangent = advanced[1]
        for g in range(3):
            done_ref[slot, 8 * g : 8 * g + 8, :] = tangent[2 + g] + upper[8 * g : 8 * g + 8]
        done_ref[slot, 24:32, :] = tangent[5] + lower
        return carry

    lax.fori_loop(0, slots, one_slot, 0)

    width = cols // parts_across
    fields = 4
    rows = 8
    for slot in range(slots + 1):
        if slot < slots:
            index = slots + slot
            start = jnp.concatenate([own_group(index, g) for g in range(4)], axis=0)
            value = start - done_ref[slot - 1] if slot else start
        else:
            value = -done_ref[slot - 1]
        for y in range(rows):
            for block in range(parts_across):
                send_ref[y * parts_across + block, slot * fields : (slot + 1) * fields, :] = value[
                    y * fields : (y + 1) * fields, block * width : (block + 1) * width
                ]
    send_ref[:, (slots + 1) * fields :, :] = jnp.zeros((rows * parts_across, fields, width), F32)


def mix_kernel(mix_ref, block_ref, out_ref):
    count, rows, width = block_ref.shape
    keys = block_ref[...].reshape(count * rows, width)
    out = jnp.dot(mix_ref[...], keys, precision=EXACT, preferred_element_type=F32)
    out_ref[...] = out.reshape(out_ref.shape)


def params():
    return pltpu.CompilerParams(vmem_limit_bytes=24 * 1024 * 1024)


def body(increment, trajectory, input_weight, bias, output_weight, correlation):
    slots, fields, rows, cols = increment.shape
    channels = input_weight.shape[0]
    tm = lax.axis_size("tm")
    strips = lax.axis_size("space")
    time = correlation.shape[1]
    parts_across = tm // rows
    width = cols // parts_across

    hbm = pl.BlockSpec(memory_space=pltpu.HBM)
    whole = jax.ShapeDtypeStruct((2 * slots, cols // LANES, rows * fields, LANES), F32)
    half = jax.ShapeDtypeStruct((2 * slots, cols // LANES, rows // 2 * fields, LANES), F32)
    w1_taps = jnp.transpose(input_weight, (2, 3, 1, 0))
    w2_taps = jnp.transpose(output_weight, (2, 3, 0, 1))
    loaded = [
        jax.ShapeDtypeStruct(shape, F32) for shape in (w1_taps.shape, (1, channels), w2_taps.shape, correlation.shape)
    ]
    strip = pltpu.VMEM(increment.shape, F32)
    own, core, chip, w1_taps, bias_row, w2_taps, correlation = pl.pallas_call(
        pack_kernel,
        out_shape=(whole, half, half, *loaded),
        in_specs=[hbm] * 6,
        out_specs=(VMEM,) * 7,
        scratch_shapes=[strip, strip, pltpu.SemaphoreType.DMA((6,))],
        compiler_params=params(),
        name="pack",
    )(*[pltpu.with_memory_space_constraint(x, pltpu.HBM) for x in (trajectory, increment, w1_taps, bias[None], w2_taps, correlation)])

    def swapped(value, first):
        pairs = [(i, i + 1) for i in range(first, strips - 1, 2)]
        return lax.ppermute(value, "space", pairs + [(j, i) for i, j in pairs])

    chip_got = swapped(chip, 1)
    core_got = swapped(core, 0)

    block_rows = (slots + 2) * fields
    w1, w2, w2_last, mix = pl.pallas_call(
        functools.partial(prepare_kernel, strips=strips, slots=slots),
        out_shape=(
            jax.ShapeDtypeStruct((WIN_OUT * channels, KEYS), BF16),
            jax.ShapeDtypeStruct((3, 144, 8 * channels), BF16),
            jax.ShapeDtypeStruct((48, 4 * channels), BF16),
            jax.ShapeDtypeStruct((time * fields, tm * block_rows), F32),
        ),
        in_specs=[VMEM] * 4,
        out_specs=(VMEM,) * 4,
        compiler_params=params(),
        name="prepare",
    )(w1_taps, bias_row, w2_taps, correlation)

    send = pl.pallas_call(
        functools.partial(forecast_kernel, strips=strips, slots=slots, parts_across=parts_across),
        out_shape=jax.ShapeDtypeStruct((tm, block_rows, width), F32),
        in_specs=[VMEM] * 6,
        out_specs=VMEM,
        scratch_shapes=[pltpu.VMEM((slots, rows * fields, cols), F32)],
        compiler_params=params(),
        name="forecast",
    )(own, core_got, chip_got, w1, w2, w2_last)

    blocks = lax.all_to_all(send, "tm", split_axis=0, concat_axis=0, tiled=True)
    mixed = pl.pallas_call(
        mix_kernel,
        out_shape=jax.ShapeDtypeStruct((tm, slots * fields, width), F32),
        in_specs=[VMEM] * 2,
        out_specs=VMEM,
        compiler_params=params(),
        name="mix",
    )(mix, blocks)
    back = lax.all_to_all(mixed, "tm", split_axis=0, concat_axis=0, tiled=True)
    back = back.reshape(rows, parts_across, slots, fields, width)
    return jnp.transpose(back, (2, 3, 0, 1, 4)).reshape(slots, fields, rows, cols)


def solution(mesh):
    placed = (P("tm", None, "space", None), P("tm", None, "space", None), P(), P(), P(), P())
    return jax.shard_map(
        body, mesh=mesh, in_specs=placed, out_specs=P("tm", None, "space", None), check_vma=False
    )
```

```python
import functools

import jax
import jax.numpy as jnp
from jax import lax
from jax.experimental import pallas as pl
from jax.experimental.pallas import tpu as pltpu
from jax.sharding import PartitionSpec as P

STEPS = 2
TENDENCY = 0.5
HALO = 2 * STEPS
F32 = jnp.float32
BF16 = jnp.bfloat16
EXACT = lax.Precision.HIGHEST
VMEM = pl.BlockSpec(memory_space=pltpu.VMEM)

WIN_OUT = 4
LANES = 128
KEYS = 256
HALF_KEYS = 160


def iota(shape, dim):
    return lax.broadcasted_iota(jnp.int32, shape, dim)


def split(value):
    high = value.astype(BF16)
    return high, (value - high.astype(F32)).astype(BF16)


def pack_kernel(
    traj_hbm, incr_hbm, w1_hbm, bias_hbm, w2_hbm, corr_hbm,
    own_ref, core_ref, chip_ref, w1_ref, bias_ref, w2_ref, corr_ref,
    traj_ref, incr_ref, sems,
):
    pairs = (
        (traj_hbm, traj_ref), (incr_hbm, incr_ref), (w1_hbm, w1_ref), (bias_hbm, bias_ref), (w2_hbm, w2_ref), (corr_hbm, corr_ref)
    )
    copies = [pltpu.make_async_copy(src, dst, sems.at[n]) for n, (src, dst) in enumerate(pairs)]
    for copy in copies:
        copy.start()
    slots, fields, rows, _ = traj_ref.shape
    half = rows // 2 * fields
    odd = lax.axis_index("space") % 2
    core_half = pl.ds(pl.multiple_of((1 - odd) * half, half), half)
    chip_half = pl.ds(pl.multiple_of(odd * half, half), half)
    for kind, ref in enumerate((traj_ref, incr_ref)):
        copies[kind].wait()
        for slot in range(slots):
            index = kind * slots + slot
            for piece in range(own_ref.shape[1]):
                for f in range(fields):
                    own_ref[index, piece, pl.ds(f, rows, stride=fields), :] = ref[
                        slot, f, :, piece * LANES : (piece + 1) * LANES
                    ]
                core_ref[index, piece] = own_ref[index, piece, core_half, :]
                chip_ref[index, piece] = own_ref[index, piece, chip_half, :]
    for copy in copies[2:]:
        copy.wait()


def key_codes(shape, dim):
    key = iota(shape, dim)
    none = -1000
    q = key - 16
    front_high = (q // 32) * 24 + q % 16
    q = key - 112
    front_low = (q // 16) * 24 + q % 16
    q = key - 160
    back_high = (q // 16) * 24 + 16 + q % 8
    q = key - 208
    back_low = (q // 16) * 24 + 16 + q % 8
    high = jnp.where((key >= 16) & (key < 112), front_high, jnp.where((key >= 160) & (key < 208), back_high, none))
    low = jnp.where((key >= 112) & (key < 160), front_low, jnp.where(key >= 208, back_low, none))
    return high, low, key


def prepare_kernel(w1_ref, bias_ref, w2_ref, corr_ref, w1_out, w2_out, w2_half, mix_out, *, strips, slots):
    fields = w1_ref.shape[2]
    channels = w1_ref.shape[3]
    time = corr_ref.shape[1]
    taps = [(a, b) for a in range(3) for b in range(3)]
    j = iota((40, KEYS), 0)
    t = j // 4
    a = (t >= 3).astype(jnp.int32) + (t >= 6).astype(jnp.int32)
    code = jnp.where(j < 36, (t - 3 * a) * 24 + a * 4 + j % 4, -5000)
    high_code, low_code, key = key_codes((40, KEYS), 1)
    table = jnp.concatenate(
        [w1_ref[a, b] for a, b in taps] + [bias_ref[...], jnp.zeros((3, channels), F32)], axis=0
    )
    w_high, w_low = split(table)
    bias_row = j == 36
    over_rows = (((0,), (0,)), ((), ()))
    for out in range(WIN_OUT):
        pick_high = jnp.where((code + 4 * out == high_code) | (bias_row & (key == 0)), 1.0, 0.0).astype(BF16)
        pick_low = jnp.where((code + 4 * out == low_code) | (bias_row & (key == 1)), 1.0, 0.0).astype(BF16)
        block = lax.dot_general(w_high, pick_high, over_rows, preferred_element_type=F32)
        block += lax.dot_general(w_low, pick_low, over_rows, preferred_element_type=F32)
        w1_out[out * channels : (out + 1) * channels, :] = block.astype(BF16)
    keys = WIN_OUT * channels
    spread = jnp.where(iota((channels, keys), 1) % channels == iota((channels, keys), 0), 1.0, 0.0).astype(BF16)
    halves = split(jnp.concatenate([w2_ref[a, b] for a, b in taps], axis=0) * TENDENCY)
    tables = [jnp.dot(h, spread, preferred_element_type=F32).astype(BF16) for h in halves]
    m = iota((72, keys), 0)
    m_row = (m - jnp.where(m >= 48, 48, jnp.where(m >= 24, 24, 0))) // 4
    k_row = iota((72, keys), 1) // channels
    mj = iota((72, 36), 0)
    mj_tap = jnp.where(mj >= 48, 2, jnp.where(mj >= 24, 1, 0))
    full = []
    for table in tables:
        total = jnp.zeros((72, keys), F32)
        for tap_row in range(3):
            pick = jnp.where(iota((72, 36), 1) == tap_row * 12 + mj_tap * 4 + mj % 4, 1.0, 0.0).astype(BF16)
            part = jnp.dot(pick, table, preferred_element_type=F32)
            total = total + jnp.where(k_row == m_row - 2 + tap_row, part, 0.0)
        full.append(total)
    even, keep = chip_side(strips)
    outside = (
        None,
        (even & (k_row < 3)) | (~even & (k_row > 0)),
        (even & (k_row < 1)) | (~even & (k_row > 2)),
    )
    for form, rows_out in enumerate(outside):
        high, low = [t if rows_out is None else jnp.where(rows_out, t * keep, t) for t in full]
        w2_out[form, 0:72, 0:keys] = high.astype(BF16)
        w2_out[form, 0:72, keys:] = high.astype(BF16)
        w2_out[form, 72:, 0:keys] = low.astype(BF16)
        w2_out[form, 72:, keys:] = jnp.zeros((72, keys), BF16)
    short = keys // 2
    high, low = [
        jnp.concatenate([t[24 * tap : 24 * tap + 16, 0:short] for tap in range(3)], axis=0).astype(BF16) for t in full
    ]
    w2_half[0:48, :] = jnp.concatenate([high, high], axis=1)
    w2_half[48:, :] = jnp.concatenate([low, jnp.zeros((48, short), BF16)], axis=1)
    keys = mix_out.shape[1]
    block = (slots + 2) * fields
    key = iota((time, keys), 1)
    sender = key // block
    row = key - sender * block
    slot = slots * sender + row // fields
    valid = row < (slots + 1) * fields
    pick = jnp.where((iota((time, keys), 0) == slot) & valid, 1.0, 0.0)
    total = jnp.zeros(mix_out.shape, F32)
    wide = (time * fields, time)
    repeat = jnp.where(iota(wide, 0) // fields == iota(wide, 1), 1.0, 0.0)
    to_field = iota(mix_out.shape, 0) % fields
    from_field = iota(mix_out.shape, 1) % fields
    for f in range(fields):
        part = jnp.dot(corr_ref[f], pick, precision=EXACT, preferred_element_type=F32)
        part = jnp.dot(repeat, part, precision=EXACT, preferred_element_type=F32)
        total = jnp.where((to_field == f) & (from_field == f), part, total)
    mix_out[...] = total


def moved(value, shift):
    if shift == 0:
        return value
    cols = value.shape[1]
    column = iota(value.shape, 1)
    turned = pltpu.roll(value, shift % cols, 1)
    outside = column == (0 if shift > 0 else cols - 1)
    return jnp.where(outside, 0.0, turned)


def window_keys(groups, bias):
    cols = groups[0].shape[1]
    front_high, front_low, back_high, back_low = [], [], [], []
    for tap in range(3):
        value = moved(jnp.concatenate(groups[:2], axis=0), 1 - tap)
        high, low = split(value)
        front_high += [high, low]
        front_low.append(high)
        if len(groups) == 3:
            value = moved(groups[2], 1 - tap)
            high = value.astype(BF16).astype(F32)
            both = jnp.concatenate([high, value - high], axis=0).astype(BF16)
            back_high.append(both)
            back_low.append(both)
    first = jnp.full((16, cols), 1.0 if bias else 0.0, BF16)
    return jnp.concatenate([first] + front_high + front_low + back_high + back_low, axis=0)


def hidden_pair(state_groups, tangent_groups, w1_ref):
    rows, keys = w1_ref.shape
    if len(state_groups) == 2:
        rows, keys = rows // 2, HALF_KEYS
    w1 = w1_ref[0:rows, 0:keys]
    z = jnp.dot(w1, window_keys(state_groups, True), preferred_element_type=F32)
    dz = jnp.dot(w1, window_keys(tangent_groups, False), preferred_element_type=F32)
    h = jnp.tanh(z)
    return h, (1.0 - h * h) * dz


def spread_hidden(hidden, weight):
    taps = jnp.dot(weight, jnp.concatenate(split(hidden), axis=0), preferred_element_type=F32)
    half = taps.shape[0] // 2
    taps = taps[:half] + taps[half:]
    third = half // 3
    total = moved(taps[0:third], 1) + taps[third : 2 * third] + moved(taps[2 * third :], -1)
    return [total[g : g + 8] for g in range(0, third, 8)]


def chip_side(strips):
    me = lax.axis_index("space")
    even = me % 2 == 0
    return even, jnp.where((me == 0) | (me == strips - 1), 0.0, 1.0)


def read_group(ref, index, g):
    pieces = ref.shape[1]
    return jnp.concatenate([ref[index, p, 8 * g : 8 * g + 8, :] for p in range(pieces)], axis=1)


def inner_kernel(own_ref, core_got_ref, w1_ref, w2_ref, w2_half_ref, kept_ref, *, strips, slots):
    even, _ = chip_side(strips)

    def pick(if_even, if_odd):
        return jnp.where(even, if_even, if_odd)

    for slot in range(slots):
        line, ends = [], []
        for index in (slot, slots + slot):
            own = [read_group(own_ref, index, g) for g in range(4)]
            core = [read_group(core_got_ref, index, g) for g in range(2)]
            line.append([pick(a, b) for a, b in zip(own + core[:1], core[1:] + own)])
            ends.append(core)
        first = hidden_pair(line[0][0:3], line[1][0:3], w1_ref)
        second = hidden_pair(line[0][2:5], line[1][2:5], w1_ref)
        last = hidden_pair(ends[0], ends[1], w1_ref)
        moved_on = []
        for kind in range(2):
            a = spread_hidden(first[kind], w2_ref[0])
            b = spread_hidden(second[kind], w2_ref[0])
            c = spread_hidden(last[kind], w2_half_ref[...])
            added = [a[0] + pick(0.0, c[1]), a[1], a[2] + b[0], b[1], b[2] + pick(c[0], 0.0)]
            moved_on.append([x + y for x, y in zip(line[kind], added)])
        s, t = moved_on
        outer = hidden_pair(
            [pick(a, b) for a, b in zip(s[2:5], s[0:3])], [pick(a, b) for a, b in zip(t[2:5], t[0:3])], w1_ref
        )
        middle = hidden_pair(
            [pick(a, b) for a, b in zip(s[1:3], s[2:4])], [pick(a, b) for a, b in zip(t[1:3], t[2:4])], w1_ref
        )
        u = spread_hidden(outer[1], w2_ref[0])
        v = spread_hidden(middle[1], w2_half_ref[...])
        kept = [
            pick(t[3], t[1]) + u[1],
            t[2] + pick(u[0], u[2]) + pick(v[1], v[0]),
            pick(t[1], t[3]) + pick(v[0], v[1]),
            pick(s[0], s[4]),
            pick(t[0], t[4]),
            pick(s[1], s[3]),
            pick(t[1], t[3]),
        ]
        for g, value in enumerate(kept):
            kept_ref[slot, 8 * g : 8 * g + 8, :] = value


def outer_kernel(own_ref, chip_got_ref, kept_ref, w1_ref, w2_ref, send_ref, *, strips, slots, parts_across):
    even, keep = chip_side(strips)
    cols = kept_ref.shape[2]
    width = cols // parts_across
    fields, rows = 4, 8

    def pick(if_even, if_odd):
        return jnp.where(even, if_even, if_odd)

    def in_order(values):
        return [pick(a, b) for a, b in zip(values, values[::-1])]

    def send(value, slot):
        for y in range(rows):
            for block in range(parts_across):
                send_ref[y * parts_across + block, slot * fields : (slot + 1) * fields, :] = value[
                    y * fields : (y + 1) * fields, block * width : (block + 1) * width
                ]

    def start(slot):
        return jnp.concatenate([read_group(own_ref, slots + slot, g) for g in range(4)], axis=0)

    send(start(0), 0)
    for slot in range(slots):
        f_outer, f_middle, f_inner, s_near, t_near, s_next, t_next = [
            kept_ref[slot, 8 * g : 8 * g + 8, :] for g in range(7)
        ]
        frames = []
        for index in (slot, slots + slot):
            chip = [read_group(chip_got_ref, index, g) for g in range(2)]
            own = [read_group(own_ref, index, g) for g in (0, 3)]
            frames.append([pick(chip[0], own[1]), pick(chip[1], chip[0]), pick(own[0], chip[1])])
        pair = hidden_pair(frames[0], frames[1], w1_ref)
        state, tangent = [], []
        for kind, (near, result) in enumerate(((s_near, state), (t_near, tangent))):
            w = spread_hidden(pair[kind], w2_ref[1])
            result += [(frames[kind][1] + w[1]) * keep, near + pick(w[2], w[0])]
        pair = hidden_pair(in_order(state + [s_next]), in_order(tangent + [t_next]), w1_ref)
        x = spread_hidden(pair[1], w2_ref[2])
        ends = [tangent[1] + x[1], f_inner + pick(x[2], x[0]), f_middle, f_outer]
        final = jnp.concatenate(in_order(ends), axis=0)
        send(start(slot + 1) - final if slot < slots - 1 else -final, slot + 1)
    send_ref[:, (slots + 1) * fields :, :] = jnp.zeros((rows * parts_across, fields, width), F32)


def mix_kernel(mix_ref, block_ref, out_ref):
    count, rows, width = block_ref.shape
    keys = block_ref[...].reshape(count * rows, width)
    out = jnp.dot(mix_ref[...], keys, precision=EXACT, preferred_element_type=F32)
    out_ref[...] = out.reshape(out_ref.shape)


def params():
    return pltpu.CompilerParams(vmem_limit_bytes=24 * 1024 * 1024)


def body(increment, trajectory, input_weight, bias, output_weight, correlation):
    slots, fields, rows, cols = increment.shape
    channels = input_weight.shape[0]
    tm = lax.axis_size("tm")
    strips = lax.axis_size("space")
    time = correlation.shape[1]
    parts_across = tm // rows
    width = cols // parts_across

    hbm = pl.BlockSpec(memory_space=pltpu.HBM)
    whole = jax.ShapeDtypeStruct((2 * slots, cols // LANES, rows * fields, LANES), F32)
    half = jax.ShapeDtypeStruct((2 * slots, cols // LANES, rows // 2 * fields, LANES), F32)
    w1_taps = jnp.transpose(input_weight, (2, 3, 1, 0))
    w2_taps = jnp.transpose(output_weight, (2, 3, 0, 1))
    loaded = [
        jax.ShapeDtypeStruct(shape, F32) for shape in (w1_taps.shape, (1, channels), w2_taps.shape, correlation.shape)
    ]
    strip = pltpu.VMEM(increment.shape, F32)
    own, core, chip, w1_taps, bias_row, w2_taps, correlation = pl.pallas_call(
        pack_kernel,
        out_shape=(whole, half, half, *loaded),
        in_specs=[hbm] * 6,
        out_specs=(VMEM,) * 7,
        scratch_shapes=[strip, strip, pltpu.SemaphoreType.DMA((6,))],
        compiler_params=params(),
        name="pack",
    )(*[pltpu.with_memory_space_constraint(x, pltpu.HBM) for x in (trajectory, increment, w1_taps, bias[None], w2_taps, correlation)])

    def swapped(value, first):
        pairs = [(i, i + 1) for i in range(first, strips - 1, 2)]
        return lax.ppermute(value, "space", pairs + [(j, i) for i, j in pairs])

    chip_got = swapped(chip, 1)
    core_got = swapped(core, 0)

    block_rows = (slots + 2) * fields
    w1, w2, w2_half, mix = pl.pallas_call(
        functools.partial(prepare_kernel, strips=strips, slots=slots),
        out_shape=(
            jax.ShapeDtypeStruct((WIN_OUT * channels, KEYS), BF16),
            jax.ShapeDtypeStruct((3, 144, 2 * WIN_OUT * channels), BF16),
            jax.ShapeDtypeStruct((96, WIN_OUT * channels), BF16),
            jax.ShapeDtypeStruct((time * fields, tm * block_rows), F32),
        ),
        in_specs=[VMEM] * 4,
        out_specs=(VMEM,) * 4,
        compiler_params=params(),
        name="prepare",
    )(w1_taps, bias_row, w2_taps, correlation)

    kept = pl.pallas_call(
        functools.partial(inner_kernel, strips=strips, slots=slots),
        out_shape=jax.ShapeDtypeStruct((slots, 56, cols), F32),
        in_specs=[VMEM] * 5,
        out_specs=VMEM,
        compiler_params=params(),
        name="inner",
    )(own, core_got, w1, w2, w2_half)

    send = pl.pallas_call(
        functools.partial(outer_kernel, strips=strips, slots=slots, parts_across=parts_across),
        out_shape=jax.ShapeDtypeStruct((tm, block_rows, width), F32),
        in_specs=[VMEM] * 5,
        out_specs=VMEM,
        compiler_params=params(),
        name="outer",
    )(own, chip_got, kept, w1, w2)

    blocks = lax.all_to_all(send, "tm", split_axis=0, concat_axis=0, tiled=True)
    mixed = pl.pallas_call(
        mix_kernel,
        out_shape=jax.ShapeDtypeStruct((tm, slots * fields, width), F32),
        in_specs=[VMEM] * 2,
        out_specs=VMEM,
        compiler_params=params(),
        name="mix",
    )(mix, blocks)
    back = lax.all_to_all(mixed, "tm", split_axis=0, concat_axis=0, tiled=True)
    back = back.reshape(rows, parts_across, slots, fields, width)
    return jnp.transpose(back, (2, 3, 0, 1, 4)).reshape(slots, fields, rows, cols)


def solution(mesh):
    placed = (P("tm", None, "space", None), P("tm", None, "space", None), P(), P(), P(), P())
    return jax.shard_map(
        body, mesh=mesh, in_specs=placed, out_specs=P("tm", None, "space", None), check_vma=False
    )
```

```python
import functools

import jax
import jax.numpy as jnp
from jax import lax
from jax.experimental import pallas as pl
from jax.experimental.pallas import tpu as pltpu
from jax.sharding import PartitionSpec as P

STEPS = 2
TENDENCY = 0.5
HALO = 2 * STEPS
F32 = jnp.float32
BF16 = jnp.bfloat16
EXACT = lax.Precision.HIGHEST
VMEM = pl.BlockSpec(memory_space=pltpu.VMEM)

WIN_OUT = 4
LANES = 128
KEYS = 256
HALF_KEYS = 160


def iota(shape, dim):
    return lax.broadcasted_iota(jnp.int32, shape, dim)


def split(value):
    high = value.astype(BF16)
    return high, (value - high.astype(F32)).astype(BF16)


def pack_kernel(
    traj_hbm, incr_hbm, w1_hbm, bias_hbm, w2_hbm, corr_hbm,
    own_ref, core_ref, chip_ref, w1_ref, bias_ref, w2_ref, corr_ref,
    traj_ref, incr_ref, sems,
):
    pairs = (
        (traj_hbm, traj_ref), (incr_hbm, incr_ref), (w1_hbm, w1_ref), (bias_hbm, bias_ref), (w2_hbm, w2_ref), (corr_hbm, corr_ref)
    )
    copies = [pltpu.make_async_copy(src, dst, sems.at[n]) for n, (src, dst) in enumerate(pairs)]
    for copy in copies:
        copy.start()
    slots, fields, rows, _ = traj_ref.shape
    half = rows // 2 * fields
    odd = lax.axis_index("space") % 2
    core_half = pl.ds(pl.multiple_of((1 - odd) * half, half), half)
    chip_half = pl.ds(pl.multiple_of(odd * half, half), half)
    for kind, ref in enumerate((traj_ref, incr_ref)):
        copies[kind].wait()
        for slot in range(slots):
            index = kind * slots + slot
            for piece in range(own_ref.shape[1]):
                for f in range(fields):
                    own_ref[index, piece, pl.ds(f, rows, stride=fields), :] = ref[
                        slot, f, :, piece * LANES : (piece + 1) * LANES
                    ]
                core_ref[index, piece] = own_ref[index, piece, core_half, :]
                chip_ref[index, piece] = own_ref[index, piece, chip_half, :]
    for copy in copies[2:]:
        copy.wait()


def key_codes(shape, dim):
    key = iota(shape, dim)
    none = -1000
    q = key - 16
    front_high = (q // 32) * 24 + q % 16
    q = key - 112
    front_low = (q // 16) * 24 + q % 16
    q = key - 160
    back_high = (q // 16) * 24 + 16 + q % 8
    q = key - 208
    back_low = (q // 16) * 24 + 16 + q % 8
    high = jnp.where((key >= 16) & (key < 112), front_high, jnp.where((key >= 160) & (key < 208), back_high, none))
    low = jnp.where((key >= 112) & (key < 160), front_low, jnp.where(key >= 208, back_low, none))
    return high, low, key


def prepare_kernel(w1_ref, bias_ref, w2_ref, corr_ref, w1_out, w2_out, w2_half, mix_out, *, tm, strips, slots):
    fields = w1_ref.shape[2]
    channels = w1_ref.shape[3]
    time = corr_ref.shape[1]
    taps = [(a, b) for a in range(3) for b in range(3)]
    j = iota((40, KEYS), 0)
    t = j // 4
    a = (t >= 3).astype(jnp.int32) + (t >= 6).astype(jnp.int32)
    code = jnp.where(j < 36, (t - 3 * a) * 24 + a * 4 + j % 4, -5000)
    high_code, low_code, key = key_codes((40, KEYS), 1)
    table = jnp.concatenate(
        [w1_ref[a, b] for a, b in taps] + [bias_ref[...], jnp.zeros((3, channels), F32)], axis=0
    )
    bias_row = j == 36
    chosen = [
        jnp.concatenate([(code + 4 * out == codes) | (bias_row & (key == place)) for out in range(WIN_OUT)], axis=1)
        for codes, place in ((high_code, 0), (low_code, 1))
    ]
    chosen = jnp.concatenate([jnp.where(c, 1.0, 0.0) for c in chosen], axis=0).astype(BF16)
    parts = [p.astype(F32) for p in split(table)]
    blocks = lax.dot_general(
        jnp.concatenate(parts, axis=0).astype(BF16), chosen, (((0,), (0,)), ((), ())), preferred_element_type=F32
    )
    for out in range(WIN_OUT):
        w1_out[out * channels : (out + 1) * channels, :] = blocks[:, out * KEYS : (out + 1) * KEYS].astype(BF16)
    keys = WIN_OUT * channels
    spread = jnp.where(iota((channels, keys), 1) % channels == iota((channels, keys), 0), 1.0, 0.0).astype(BF16)
    halves = split(jnp.concatenate([w2_ref[a, b] for a, b in taps], axis=0) * TENDENCY)
    tables = jnp.concatenate([jnp.dot(h, spread, preferred_element_type=F32).astype(BF16) for h in halves], axis=1)
    mj = iota((72, 36), 0)
    mj_tap = jnp.where(mj >= 48, 2, jnp.where(mj >= 24, 1, 0))
    source = mj_tap * 4 + mj % 4
    repeat = jnp.concatenate(
        [jnp.where(iota((72, 36), 1) == tap_row * 12 + source, 1.0, 0.0) for tap_row in range(3)], axis=0
    ).astype(BF16)
    repeated = jnp.dot(repeat, tables, preferred_element_type=F32)
    m = iota((72, keys), 0)
    m_row = (m - jnp.where(m >= 48, 48, jnp.where(m >= 24, 24, 0))) // 4
    k_row = iota((72, keys), 1) // channels
    full = []
    for part in range(2):
        total = jnp.zeros((72, keys), F32)
        for tap_row in range(3):
            block = repeated[72 * tap_row : 72 * (tap_row + 1), keys * part : keys * (part + 1)]
            total = total + jnp.where(k_row == m_row - 2 + tap_row, block, 0.0)
        full.append(total)
    even, keep = chip_side(strips)
    outside = (
        None,
        (even & (k_row < 3)) | (~even & (k_row > 0)),
        (even & (k_row < 1)) | (~even & (k_row > 2)),
    )
    for form, rows_out in enumerate(outside):
        high, low = [t if rows_out is None else jnp.where(rows_out, t * keep, t) for t in full]
        w2_out[form, 0:72, 0:keys] = high.astype(BF16)
        w2_out[form, 0:72, keys:] = high.astype(BF16)
        w2_out[form, 72:, 0:keys] = low.astype(BF16)
        w2_out[form, 72:, keys:] = jnp.zeros((72, keys), BF16)
    short = keys // 2
    high, low = [
        jnp.concatenate([t[24 * tap : 24 * tap + 16, 0:short] for tap in range(3)], axis=0).astype(BF16) for t in full
    ]
    w2_half[0:48, :] = jnp.concatenate([high, high], axis=1)
    w2_half[48:, :] = jnp.concatenate([low, jnp.zeros((48, short), BF16)], axis=1)
    main = tm * slots * fields
    key = iota((time, main + tm * fields), 1)
    slot = jnp.where(key < main, key // fields, (key - main) // fields * slots + slots)
    met = slot == iota(key.shape, 0)
    for f in range(fields):
        pick = jnp.where(met & (key % fields == f), 1.0, 0.0).astype(BF16)
        first = corr_ref[f].astype(BF16)
        rest = corr_ref[f] - first.astype(F32)
        second = rest.astype(BF16)
        third = (rest - second.astype(F32)).astype(BF16)
        total = jnp.dot(first, pick, preferred_element_type=F32)
        total += jnp.dot(second, pick, preferred_element_type=F32) + jnp.dot(third, pick, preferred_element_type=F32)
        mix_out[f * time : (f + 1) * time, :] = total


def moved(value, shift):
    if shift == 0:
        return value
    cols = value.shape[1]
    column = iota(value.shape, 1)
    turned = pltpu.roll(value, shift % cols, 1)
    outside = column == (0 if shift > 0 else cols - 1)
    return jnp.where(outside, 0.0, turned)


def window_keys(groups, bias):
    cols = groups[0].shape[1]
    front_high, front_low, back_high, back_low = [], [], [], []
    high, low = split(jnp.concatenate(groups[:2], axis=0))
    if len(groups) == 3:
        rounded = groups[2].astype(BF16).astype(F32)
        both = jnp.concatenate([rounded, groups[2] - rounded], axis=0).astype(BF16)
    for tap in range(3):
        front_low.append(moved(high, 1 - tap))
        front_high += [front_low[-1], moved(low, 1 - tap)]
        if len(groups) == 3:
            back_high.append(moved(both, 1 - tap))
    back_low = back_high
    first = jnp.full((16, cols), 1.0 if bias else 0.0, BF16)
    return jnp.concatenate([first] + front_high + front_low + back_high + back_low, axis=0)


def hidden_pair(state_groups, tangent_groups, w1_ref):
    rows, keys = w1_ref.shape
    if len(state_groups) == 2:
        rows, keys = rows // 2, HALF_KEYS
    w1 = w1_ref[0:rows, 0:keys]
    z = jnp.dot(w1, window_keys(state_groups, True), preferred_element_type=F32)
    dz = jnp.dot(w1, window_keys(tangent_groups, False), preferred_element_type=F32)
    h = jnp.tanh(z)
    return h, (1.0 - h * h) * dz


def spread_hidden(hidden, weight):
    taps = jnp.dot(weight, jnp.concatenate(split(hidden), axis=0), preferred_element_type=F32)
    half = taps.shape[0] // 2
    taps = taps[:half] + taps[half:]
    third = half // 3
    total = moved(taps[0:third], 1) + taps[third : 2 * third] + moved(taps[2 * third :], -1)
    return [total[g : g + 8] for g in range(0, third, 8)]


def chip_side(strips):
    me = lax.axis_index("space")
    even = me % 2 == 0
    return even, jnp.where((me == 0) | (me == strips - 1), 0.0, 1.0)


def read_group(ref, index, g):
    pieces = ref.shape[1]
    return jnp.concatenate([ref[index, p, 8 * g : 8 * g + 8, :] for p in range(pieces)], axis=1)


def staggered(slots, one_slot, together):
    waiting = [one_slot(slot) for slot in range(slots)]
    running = []
    while waiting or running:
        starting = len(waiting) if together else 1
        running = waiting[:starting] + running
        waiting = waiting[starting:]
        running = [r for r in running if next(r, True) is None]


def inner_kernel(own_ref, core_got_ref, w1_ref, w2_ref, w2_half_ref, kept_ref, *, strips, slots):
    even, _ = chip_side(strips)

    def pick(if_even, if_odd):
        return jnp.where(even, if_even, if_odd)

    def one_slot(slot):
        line, ends = [], []
        for index in (slot, slots + slot):
            own = [read_group(own_ref, index, g) for g in range(4)]
            core = [read_group(core_got_ref, index, g) for g in range(2)]
            line.append([pick(a, b) for a, b in zip(own + core[:1], core[1:] + own)])
            ends.append(core)
        first = hidden_pair(line[0][0:3], line[1][0:3], w1_ref)
        second = hidden_pair(line[0][2:5], line[1][2:5], w1_ref)
        last = hidden_pair(ends[0], ends[1], w1_ref)
        yield
        moved_on = []
        for kind in range(2):
            a = spread_hidden(first[kind], w2_ref[0])
            b = spread_hidden(second[kind], w2_ref[0])
            c = spread_hidden(last[kind], w2_half_ref[...])
            added = [a[0] + pick(0.0, c[1]), a[1], a[2] + b[0], b[1], b[2] + pick(c[0], 0.0)]
            moved_on.append([x + y for x, y in zip(line[kind], added)])
        s, t = moved_on
        yield
        outer = hidden_pair(
            [pick(a, b) for a, b in zip(s[2:5], s[0:3])], [pick(a, b) for a, b in zip(t[2:5], t[0:3])], w1_ref
        )
        middle = hidden_pair(
            [pick(a, b) for a, b in zip(s[1:3], s[2:4])], [pick(a, b) for a, b in zip(t[1:3], t[2:4])], w1_ref
        )
        yield
        u = spread_hidden(outer[1], w2_ref[0])
        v = spread_hidden(middle[1], w2_half_ref[...])
        kept = [
            pick(t[3], t[1]) + u[1],
            t[2] + pick(u[0], u[2]) + pick(v[1], v[0]),
            pick(t[1], t[3]) + pick(v[0], v[1]),
            pick(s[0], s[4]),
            pick(t[0], t[4]),
            pick(s[1], s[3]),
            pick(t[1], t[3]),
        ]
        for g, value in enumerate(kept):
            kept_ref[slot, 8 * g : 8 * g + 8, :] = value

    staggered(slots, one_slot, False)


def outer_kernel(own_ref, chip_got_ref, kept_ref, w1_ref, w2_ref, send_ref, *, strips, slots, parts_across):
    even, keep = chip_side(strips)
    cols = kept_ref.shape[2]
    width = cols // parts_across
    fields, rows = 4, 8
    packed = send_ref.shape[2] > width

    def pick(if_even, if_odd):
        return jnp.where(even, if_even, if_odd)

    def in_order(values):
        return [pick(a, b) for a, b in zip(values, values[::-1])]

    def send(value, slot):
        for y in range(rows):
            for block in range(parts_across):
                part = value[y * fields : (y + 1) * fields, block * width : (block + 1) * width]
                if slot < slots or not packed:
                    send_ref[y * parts_across + block, slot * fields : (slot + 1) * fields, 0:width] = part
                    continue
                for q in range(slots):
                    send_ref[y * parts_across + block, q * fields : (q + 1) * fields, width:] = part[
                        :, q * width // slots : (q + 1) * width // slots
                    ]

    def start(slot):
        return jnp.concatenate([read_group(own_ref, slots + slot, g) for g in range(4)], axis=0)

    def one_slot(slot):
        near = [kept_ref[slot, 8 * g : 8 * g + 8, :] for g in (3, 4)]
        frames = []
        for index in (slot, slots + slot):
            chip = [read_group(chip_got_ref, index, g) for g in range(2)]
            own = [read_group(own_ref, index, g) for g in (0, 3)]
            frames.append([pick(chip[0], own[1]), pick(chip[1], chip[0]), pick(own[0], chip[1])])
        pair = hidden_pair(frames[0], frames[1], w1_ref)
        yield
        moved_on = []
        for kind in range(2):
            w = spread_hidden(pair[kind], w2_ref[1])
            moved_on.append([(frames[kind][1] + w[1]) * keep, near[kind] + pick(w[2], w[0])])
        state, tangent = moved_on
        yield
        f_outer, f_middle, f_inner, s_next, t_next = [kept_ref[slot, 8 * g : 8 * g + 8, :] for g in (0, 1, 2, 5, 6)]
        pair = hidden_pair(in_order(state + [s_next]), in_order(tangent + [t_next]), w1_ref)
        yield
        x = spread_hidden(pair[1], w2_ref[2])
        ends = [tangent[1] + x[1], f_inner + pick(x[2], x[0]), f_middle, f_outer]
        final = jnp.concatenate(in_order(ends), axis=0)
        send(start(slot + 1) - final if slot < slots - 1 else -final, slot + 1)

    send(start(0), 0)
    staggered(slots, one_slot, True)
    if not packed:
        send_ref[:, (slots + 1) * fields :, :] = jnp.zeros((rows * parts_across, fields, width), F32)


def mix_kernel(mix_ref, block_ref, out_ref, *, slots):
    count, pieces, rows, _ = out_ref.shape
    width = pieces * LANES
    fields = rows // slots
    time = count * slots
    main = block_ref[:, 0:rows, 0:width].reshape(count * rows, width)
    if block_ref.shape[2] > width:
        last = [
            jnp.concatenate([block_ref[d, q * fields : (q + 1) * fields, width:] for d in range(count)], axis=0)
            for q in range(slots)
        ]
        last = jnp.concatenate(last, axis=1)
    else:
        last = jnp.concatenate([block_ref[d, rows : rows + fields, :] for d in range(count)], axis=0)
    keys = jnp.concatenate([main, last], axis=0)
    out = jnp.dot(mix_ref[...], keys, precision=EXACT, preferred_element_type=F32)
    for d in range(count):
        for f in range(fields):
            start = f * time + d * slots
            for p in range(pieces):
                out_ref[d, p, f * slots : (f + 1) * slots, :] = out[start : start + slots, p * LANES : (p + 1) * LANES]


def place_kernel(rows_ref, out_hbm, out_ref, sems):
    slots, fields, rows, cols = out_ref.shape
    pieces = cols // LANES
    copies = []
    for slot in range(slots):
        for f in range(fields):
            for p in range(pieces):
                line = (p * fields + f) * slots + slot
                out_ref[slot, f, :, p * LANES : (p + 1) * LANES] = rows_ref[
                    pl.ds(line, rows, stride=pieces * fields * slots), :
                ]
        copies.append(pltpu.make_async_copy(out_ref.at[slot], out_hbm.at[slot], sems.at[slot]))
        copies[-1].start()
    for copy in copies:
        copy.wait()


def params():
    return pltpu.CompilerParams(vmem_limit_bytes=24 * 1024 * 1024)


def body(increment, trajectory, input_weight, bias, output_weight, correlation):
    slots, fields, rows, cols = increment.shape
    channels = input_weight.shape[0]
    tm = lax.axis_size("tm")
    strips = lax.axis_size("space")
    time = correlation.shape[1]
    parts_across = tm // rows
    width = cols // parts_across

    hbm = pl.BlockSpec(memory_space=pltpu.HBM)
    whole = jax.ShapeDtypeStruct((2 * slots, cols // LANES, rows * fields, LANES), F32)
    half = jax.ShapeDtypeStruct((2 * slots, cols // LANES, rows // 2 * fields, LANES), F32)
    w1_taps = jnp.transpose(input_weight, (2, 3, 1, 0))
    w2_taps = jnp.transpose(output_weight, (2, 3, 0, 1))
    loaded = [
        jax.ShapeDtypeStruct(shape, F32) for shape in (w1_taps.shape, (1, channels), w2_taps.shape, correlation.shape)
    ]
    strip = pltpu.VMEM(increment.shape, F32)
    own, core, chip, w1_taps, bias_row, w2_taps, correlation = pl.pallas_call(
        pack_kernel,
        out_shape=(whole, half, half, *loaded),
        in_specs=[hbm] * 6,
        out_specs=(VMEM,) * 7,
        scratch_shapes=[strip, strip, pltpu.SemaphoreType.DMA((6,))],
        compiler_params=params(),
        name="pack",
    )(*[pltpu.with_memory_space_constraint(x, pltpu.HBM) for x in (trajectory, increment, w1_taps, bias[None], w2_taps, correlation)])

    def swapped(value, first):
        pairs = [(i, i + 1) for i in range(first, strips - 1, 2)]
        return lax.ppermute(value, "space", pairs + [(j, i) for i, j in pairs])

    chip_got = swapped(chip, 1)
    core_got = swapped(core, 0)

    packed = width // slots % LANES == 0
    block = (slots * fields, width + width // slots) if packed else ((slots + 2) * fields, width)
    w1, w2, w2_half, mix = pl.pallas_call(
        functools.partial(prepare_kernel, tm=tm, strips=strips, slots=slots),
        out_shape=(
            jax.ShapeDtypeStruct((WIN_OUT * channels, KEYS), BF16),
            jax.ShapeDtypeStruct((3, 144, 2 * WIN_OUT * channels), BF16),
            jax.ShapeDtypeStruct((96, WIN_OUT * channels), BF16),
            jax.ShapeDtypeStruct((fields * time, tm * (slots + 1) * fields), F32),
        ),
        in_specs=[VMEM] * 4,
        out_specs=(VMEM,) * 4,
        compiler_params=params(),
        name="prepare",
    )(w1_taps, bias_row, w2_taps, correlation)

    kept = pl.pallas_call(
        functools.partial(inner_kernel, strips=strips, slots=slots),
        out_shape=jax.ShapeDtypeStruct((slots, 56, cols), F32),
        in_specs=[VMEM] * 5,
        out_specs=VMEM,
        compiler_params=params(),
        name="inner",
    )(own, core_got, w1, w2, w2_half)

    send = pl.pallas_call(
        functools.partial(outer_kernel, strips=strips, slots=slots, parts_across=parts_across),
        out_shape=jax.ShapeDtypeStruct((tm, *block), F32),
        in_specs=[VMEM] * 5,
        out_specs=VMEM,
        compiler_params=params(),
        name="outer",
    )(own, chip_got, kept, w1, w2)

    blocks = lax.all_to_all(send, "tm", split_axis=0, concat_axis=0, tiled=True)
    mixed = pl.pallas_call(
        functools.partial(mix_kernel, slots=slots),
        out_shape=jax.ShapeDtypeStruct((tm, width // LANES, slots * fields, LANES), F32),
        in_specs=[VMEM] * 2,
        out_specs=VMEM,
        compiler_params=params(),
        name="mix",
    )(mix, blocks)
    back = lax.all_to_all(mixed, "tm", split_axis=0, concat_axis=0, tiled=True)
    return pl.pallas_call(
        place_kernel,
        out_shape=jax.ShapeDtypeStruct(increment.shape, F32),
        in_specs=[VMEM],
        out_specs=hbm,
        scratch_shapes=[strip, pltpu.SemaphoreType.DMA((slots,))],
        compiler_params=params(),
        name="place",
    )(back.reshape(-1, LANES))


def solution(mesh):
    placed = (P("tm", None, "space", None), P("tm", None, "space", None), P(), P(), P(), P())
    return jax.shard_map(
        body, mesh=mesh, in_specs=placed, out_specs=P("tm", None, "space", None), check_vma=False
    )
```

```python
import functools

import jax
import jax.numpy as jnp
from jax import lax
from jax.experimental import pallas as pl
from jax.experimental.pallas import tpu as pltpu
from jax.sharding import PartitionSpec as P

STEPS = 2
TENDENCY = 0.5
HALO = 2 * STEPS
F32 = jnp.float32
BF16 = jnp.bfloat16
EXACT = lax.Precision.HIGHEST
VMEM = pl.BlockSpec(memory_space=pltpu.VMEM)

WIN_OUT = 4
LANES = 128
KEYS = 256
HALF_KEYS = 160


def iota(shape, dim):
    return lax.broadcasted_iota(jnp.int32, shape, dim)


def split(value):
    high = value.astype(BF16)
    return high, (value - high.astype(F32)).astype(BF16)


def pack_kernel(
    traj_hbm, incr_hbm, w1_hbm, bias_hbm, w2_hbm, corr_hbm,
    own_ref, core_ref, chip_ref, w1_ref, bias_ref, w2_ref, corr_ref,
    traj_ref, incr_ref, sems,
):
    pairs = (
        (traj_hbm, traj_ref), (incr_hbm, incr_ref), (w1_hbm, w1_ref), (bias_hbm, bias_ref), (w2_hbm, w2_ref), (corr_hbm, corr_ref)
    )
    copies = [pltpu.make_async_copy(src, dst, sems.at[n]) for n, (src, dst) in enumerate(pairs)]
    for copy in copies:
        copy.start()
    slots, fields, rows, _ = traj_ref.shape
    half = rows // 2 * fields
    odd = lax.axis_index("space") % 2
    core_half = pl.ds(pl.multiple_of((1 - odd) * half, half), half)
    chip_half = pl.ds(pl.multiple_of(odd * half, half), half)
    for kind, ref in enumerate((traj_ref, incr_ref)):
        copies[kind].wait()
        for slot in range(slots):
            index = kind * slots + slot
            for piece in range(own_ref.shape[1]):
                for f in range(fields):
                    own_ref[index, piece, pl.ds(f, rows, stride=fields), :] = ref[
                        slot, f, :, piece * LANES : (piece + 1) * LANES
                    ]
                core_ref[index, piece] = own_ref[index, piece, core_half, :]
                chip_ref[index, piece] = own_ref[index, piece, chip_half, :]
    for copy in copies[2:]:
        copy.wait()


def key_codes(shape, dim):
    key = iota(shape, dim)
    none = -1000
    q = key - 16
    front_high = (q // 32) * 24 + q % 16
    q = key - 112
    front_low = (q // 16) * 24 + q % 16
    q = key - 160
    back_high = (q // 16) * 24 + 16 + q % 8
    q = key - 208
    back_low = (q // 16) * 24 + 16 + q % 8
    high = jnp.where((key >= 16) & (key < 112), front_high, jnp.where((key >= 160) & (key < 208), back_high, none))
    low = jnp.where((key >= 112) & (key < 160), front_low, jnp.where(key >= 208, back_low, none))
    return high, low, key


def prepare_kernel(w1_ref, bias_ref, w2_ref, corr_ref, w1_out, w2_out, w2_half, mix_out, *, tm, strips, slots):
    fields = w1_ref.shape[2]
    channels = w1_ref.shape[3]
    time = corr_ref.shape[1]
    taps = [(a, b) for a in range(3) for b in range(3)]
    j = iota((40, KEYS), 0)
    t = j // 4
    a = (t >= 3).astype(jnp.int32) + (t >= 6).astype(jnp.int32)
    code = jnp.where(j < 36, (t - 3 * a) * 24 + a * 4 + j % 4, -5000)
    high_code, low_code, key = key_codes((40, KEYS), 1)
    table = jnp.concatenate(
        [w1_ref[a, b] for a, b in taps] + [bias_ref[...], jnp.zeros((3, channels), F32)], axis=0
    )
    bias_row = j == 36
    chosen = [
        jnp.concatenate([(code + 4 * out == codes) | (bias_row & (key == place)) for out in range(WIN_OUT)], axis=1)
        for codes, place in ((high_code, 0), (low_code, 1))
    ]
    chosen = jnp.concatenate([jnp.where(c, 1.0, 0.0) for c in chosen], axis=0).astype(BF16)
    parts = [p.astype(F32) for p in split(table)]
    blocks = lax.dot_general(
        jnp.concatenate(parts, axis=0).astype(BF16), chosen, (((0,), (0,)), ((), ())), preferred_element_type=F32
    )
    for out in range(WIN_OUT):
        w1_out[out * channels : (out + 1) * channels, :] = blocks[:, out * KEYS : (out + 1) * KEYS].astype(BF16)
    keys = WIN_OUT * channels
    spread = jnp.where(iota((channels, keys), 1) % channels == iota((channels, keys), 0), 1.0, 0.0).astype(BF16)
    halves = split(jnp.concatenate([w2_ref[a, b] for a, b in taps], axis=0) * TENDENCY)
    tables = jnp.concatenate([jnp.dot(h, spread, preferred_element_type=F32).astype(BF16) for h in halves], axis=1)
    mj = iota((72, 36), 0)
    mj_tap = jnp.where(mj >= 48, 2, jnp.where(mj >= 24, 1, 0))
    source = mj_tap * 4 + mj % 4
    repeat = jnp.concatenate(
        [jnp.where(iota((72, 36), 1) == tap_row * 12 + source, 1.0, 0.0) for tap_row in range(3)], axis=0
    ).astype(BF16)
    repeated = jnp.dot(repeat, tables, preferred_element_type=F32)
    m = iota((72, keys), 0)
    m_row = (m - jnp.where(m >= 48, 48, jnp.where(m >= 24, 24, 0))) // 4
    k_row = iota((72, keys), 1) // channels
    full = []
    for part in range(2):
        total = jnp.zeros((72, keys), F32)
        for tap_row in range(3):
            block = repeated[72 * tap_row : 72 * (tap_row + 1), keys * part : keys * (part + 1)]
            total = total + jnp.where(k_row == m_row - 2 + tap_row, block, 0.0)
        full.append(total)
    even, keep = chip_side(strips)
    outside = (
        None,
        (even & (k_row < 3)) | (~even & (k_row > 0)),
        (even & (k_row < 1)) | (~even & (k_row > 2)),
    )
    for form, rows_out in enumerate(outside):
        high, low = [t if rows_out is None else jnp.where(rows_out, t * keep, t) for t in full]
        w2_out[form, 0:72, 0:keys] = high.astype(BF16)
        w2_out[form, 0:72, keys:] = high.astype(BF16)
        w2_out[form, 72:, 0:keys] = low.astype(BF16)
        w2_out[form, 72:, keys:] = jnp.zeros((72, keys), BF16)
    short = keys // 2
    high, low = [
        jnp.concatenate([t[24 * tap : 24 * tap + 16, 0:short] for tap in range(3)], axis=0).astype(BF16) for t in full
    ]
    w2_half[0:48, :] = jnp.concatenate([high, high], axis=1)
    w2_half[48:, :] = jnp.concatenate([low, jnp.zeros((48, short), BF16)], axis=1)
    main = tm * slots * fields
    key = iota((time, main + tm * fields), 1)
    slot = jnp.where(key < main, key // fields, (key - main) // fields * slots + slots)
    met = slot == iota(key.shape, 0)
    for f in range(fields):
        pick = jnp.where(met & (key % fields == f), 1.0, 0.0).astype(BF16)
        first = corr_ref[f].astype(BF16)
        rest = corr_ref[f] - first.astype(F32)
        second = rest.astype(BF16)
        third = (rest - second.astype(F32)).astype(BF16)
        total = jnp.dot(first, pick, preferred_element_type=F32)
        total += jnp.dot(second, pick, preferred_element_type=F32) + jnp.dot(third, pick, preferred_element_type=F32)
        mix_out[f * time : (f + 1) * time, :] = total


def moved(value, shift):
    if shift == 0:
        return value
    cols = value.shape[1]
    column = iota(value.shape, 1)
    turned = pltpu.roll(value, shift % cols, 1)
    outside = column == (0 if shift > 0 else cols - 1)
    return jnp.where(outside, 0.0, turned)


def window_keys(groups, bias):
    cols = groups[0].shape[1]
    front_high, front_low, back_high, back_low = [], [], [], []
    high, low = split(jnp.concatenate(groups[:2], axis=0))
    if len(groups) == 3:
        rounded = groups[2].astype(BF16).astype(F32)
        both = jnp.concatenate([rounded, groups[2] - rounded], axis=0).astype(BF16)
    for tap in range(3):
        front_low.append(moved(high, 1 - tap))
        front_high += [front_low[-1], moved(low, 1 - tap)]
        if len(groups) == 3:
            back_high.append(moved(both, 1 - tap))
    back_low = back_high
    first = jnp.full((16, cols), 1.0 if bias else 0.0, BF16)
    return jnp.concatenate([first] + front_high + front_low + back_high + back_low, axis=0)


def hidden_pair(state_groups, tangent_groups, w1_ref):
    rows, keys = w1_ref.shape
    if len(state_groups) == 2:
        rows, keys = rows // 2, HALF_KEYS
    w1 = w1_ref[0:rows, 0:keys]
    z = jnp.dot(w1, window_keys(state_groups, True), preferred_element_type=F32)
    dz = jnp.dot(w1, window_keys(tangent_groups, False), preferred_element_type=F32)
    h = jnp.tanh(z)
    return h, (1.0 - h * h) * dz


def spread_hidden(hidden, weight):
    taps = jnp.dot(weight, jnp.concatenate(split(hidden), axis=0), preferred_element_type=F32)
    half = taps.shape[0] // 2
    taps = taps[:half] + taps[half:]
    third = half // 3
    total = moved(taps[0:third], 1) + taps[third : 2 * third] + moved(taps[2 * third :], -1)
    return [total[g : g + 8] for g in range(0, third, 8)]


def chip_side(strips):
    me = lax.axis_index("space")
    even = me % 2 == 0
    return even, jnp.where((me == 0) | (me == strips - 1), 0.0, 1.0)


def read_group(ref, index, g):
    pieces = ref.shape[1]
    return jnp.concatenate([ref[index, p, 8 * g : 8 * g + 8, :] for p in range(pieces)], axis=1)


def staggered(slots, one_slot, together):
    waiting = [one_slot(slot) for slot in range(slots)]
    running = []
    while waiting or running:
        starting = len(waiting) if together else 1
        running = waiting[:starting] + running
        waiting = waiting[starting:]
        running = [r for r in running if next(r, True) is None]


def inner_kernel(own_ref, core_got_ref, w1_ref, w2_ref, w2_half_ref, kept_ref, *, strips, slots):
    even, _ = chip_side(strips)

    def pick(if_even, if_odd):
        return jnp.where(even, if_even, if_odd)

    def one_slot(slot):
        line, ends = [], []
        for index in (slot, slots + slot):
            own = [read_group(own_ref, index, g) for g in range(4)]
            core = [read_group(core_got_ref, index, g) for g in range(2)]
            line.append([pick(a, b) for a, b in zip(own + core[:1], core[1:] + own)])
            ends.append(core)
        first = hidden_pair(line[0][0:3], line[1][0:3], w1_ref)
        second = hidden_pair(line[0][2:5], line[1][2:5], w1_ref)
        last = hidden_pair(ends[0], ends[1], w1_ref)
        yield
        moved_on = []
        for kind in range(2):
            a = spread_hidden(first[kind], w2_ref[0])
            b = spread_hidden(second[kind], w2_ref[0])
            c = spread_hidden(last[kind], w2_half_ref[...])
            added = [a[0] + pick(0.0, c[1]), a[1], a[2] + b[0], b[1], b[2] + pick(c[0], 0.0)]
            moved_on.append([x + y for x, y in zip(line[kind], added)])
        s, t = moved_on
        yield
        outer = hidden_pair(
            [pick(a, b) for a, b in zip(s[2:5], s[0:3])], [pick(a, b) for a, b in zip(t[2:5], t[0:3])], w1_ref
        )
        middle = hidden_pair(
            [pick(a, b) for a, b in zip(s[1:3], s[2:4])], [pick(a, b) for a, b in zip(t[1:3], t[2:4])], w1_ref
        )
        yield
        u = spread_hidden(outer[1], w2_ref[0])
        v = spread_hidden(middle[1], w2_half_ref[...])
        kept = [
            pick(t[3], t[1]) + u[1],
            t[2] + pick(u[0], u[2]) + pick(v[1], v[0]),
            pick(t[1], t[3]) + pick(v[0], v[1]),
            pick(s[0], s[4]),
            pick(t[0], t[4]),
            pick(s[1], s[3]),
            pick(t[1], t[3]),
        ]
        for g, value in enumerate(kept):
            kept_ref[slot, 8 * g : 8 * g + 8, :] = value

    staggered(slots, one_slot, False)


def outer_kernel(own_ref, chip_got_ref, kept_ref, w1_ref, w2_ref, send_ref, *, strips, slots, parts_across):
    even, keep = chip_side(strips)
    cols = kept_ref.shape[2]
    width = cols // parts_across
    fields, rows = 4, 8
    packed = send_ref.shape[2] > width

    def pick(if_even, if_odd):
        return jnp.where(even, if_even, if_odd)

    def in_order(values):
        return [pick(a, b) for a, b in zip(values, values[::-1])]

    def send(value, slot):
        for y in range(rows):
            for block in range(parts_across):
                part = value[y * fields : (y + 1) * fields, block * width : (block + 1) * width]
                if slot < slots or not packed:
                    send_ref[y * parts_across + block, slot * fields : (slot + 1) * fields, 0:width] = part
                    continue
                for q in range(slots):
                    send_ref[y * parts_across + block, q * fields : (q + 1) * fields, width:] = part[
                        :, q * width // slots : (q + 1) * width // slots
                    ]

    def start(slot):
        return jnp.concatenate([read_group(own_ref, slots + slot, g) for g in range(4)], axis=0)

    def one_slot(slot):
        near = [kept_ref[slot, 8 * g : 8 * g + 8, :] for g in (3, 4)]
        frames = []
        for index in (slot, slots + slot):
            chip = [read_group(chip_got_ref, index, g) for g in range(2)]
            own = [read_group(own_ref, index, g) for g in (0, 3)]
            frames.append([pick(chip[0], own[1]), pick(chip[1], chip[0]), pick(own[0], chip[1])])
        pair = hidden_pair(frames[0], frames[1], w1_ref)
        yield
        moved_on = []
        for kind in range(2):
            w = spread_hidden(pair[kind], w2_ref[1])
            moved_on.append([(frames[kind][1] + w[1]) * keep, near[kind] + pick(w[2], w[0])])
        state, tangent = moved_on
        yield
        f_outer, f_middle, f_inner, s_next, t_next = [kept_ref[slot, 8 * g : 8 * g + 8, :] for g in (0, 1, 2, 5, 6)]
        pair = hidden_pair(in_order(state + [s_next]), in_order(tangent + [t_next]), w1_ref)
        yield
        x = spread_hidden(pair[1], w2_ref[2])
        ends = [tangent[1] + x[1], f_inner + pick(x[2], x[0]), f_middle, f_outer]
        final = jnp.concatenate(in_order(ends), axis=0)
        send(start(slot + 1) - final if slot < slots - 1 else -final, slot + 1)

    send(start(0), 0)
    staggered(slots, one_slot, True)
    if not packed:
        send_ref[:, (slots + 1) * fields :, :] = jnp.zeros((rows * parts_across, fields, width), F32)


def mix_kernel(mix_ref, block_ref, out_ref, *, slots):
    count, pieces, rows, _ = out_ref.shape
    width = pieces * LANES
    fields = rows // slots
    time = count * slots
    main = block_ref[:, 0:rows, 0:width].reshape(count * rows, width)
    if block_ref.shape[2] > width:
        last = [
            jnp.concatenate([block_ref[d, q * fields : (q + 1) * fields, width:] for d in range(count)], axis=0)
            for q in range(slots)
        ]
        last = jnp.concatenate(last, axis=1)
    else:
        last = jnp.concatenate([block_ref[d, rows : rows + fields, :] for d in range(count)], axis=0)
    keys = jnp.concatenate([main, last], axis=0)
    out = jnp.dot(mix_ref[...], keys, precision=EXACT, preferred_element_type=F32)
    for d in range(count):
        for f in range(fields):
            start = f * time + d * slots
            for p in range(pieces):
                out_ref[d, p, f * slots : (f + 1) * slots, :] = out[start : start + slots, p * LANES : (p + 1) * LANES]


def place_kernel(rows_ref, out_hbm, out_ref, sems):
    slots, fields, rows, cols = out_ref.shape
    pieces = cols // LANES
    copies = []
    for slot in range(slots):
        for f in range(fields):
            for p in range(pieces):
                line = (p * fields + f) * slots + slot
                out_ref[slot, f, :, p * LANES : (p + 1) * LANES] = rows_ref[
                    pl.ds(line, rows, stride=pieces * fields * slots), :
                ]
        copies.append(pltpu.make_async_copy(out_ref.at[slot], out_hbm.at[slot], sems.at[slot]))
        copies[-1].start()
    for copy in copies:
        copy.wait()


def params():
    return pltpu.CompilerParams(vmem_limit_bytes=24 * 1024 * 1024)


def body(increment, trajectory, input_weight, bias, output_weight, correlation):
    slots, fields, rows, cols = increment.shape
    channels = input_weight.shape[0]
    tm = lax.axis_size("tm")
    strips = lax.axis_size("space")
    time = correlation.shape[1]
    parts_across = tm // rows
    width = cols // parts_across

    hbm = pl.BlockSpec(memory_space=pltpu.HBM)
    whole = jax.ShapeDtypeStruct((2 * slots, cols // LANES, rows * fields, LANES), F32)
    half = jax.ShapeDtypeStruct((2 * slots, cols // LANES, rows // 2 * fields, LANES), F32)
    w1_taps = jnp.transpose(input_weight, (2, 3, 1, 0))
    w2_taps = jnp.transpose(output_weight, (2, 3, 0, 1))
    loaded = [
        jax.ShapeDtypeStruct(shape, F32) for shape in (w1_taps.shape, (1, channels), w2_taps.shape, correlation.shape)
    ]
    strip = pltpu.VMEM(increment.shape, F32)
    own, core, chip, w1_taps, bias_row, w2_taps, correlation = pl.pallas_call(
        pack_kernel,
        out_shape=(whole, half, half, *loaded),
        in_specs=[hbm] * 6,
        out_specs=(VMEM,) * 7,
        scratch_shapes=[strip, strip, pltpu.SemaphoreType.DMA((6,))],
        compiler_params=params(),
        name="pack",
    )(*[pltpu.with_memory_space_constraint(x, pltpu.HBM) for x in (trajectory, increment, w1_taps, bias[None], w2_taps, correlation)])

    def swapped(value, first):
        pairs = [(i, i + 1) for i in range(first, strips - 1, 2)]
        return lax.ppermute(value, "space", pairs + [(j, i) for i, j in pairs])

    chip_got = swapped(chip, 1)
    core_got = swapped(core, 0)

    packed = width // slots % LANES == 0
    block = (slots * fields, width + width // slots) if packed else ((slots + 2) * fields, width)
    w1, w2, w2_half, mix = pl.pallas_call(
        functools.partial(prepare_kernel, tm=tm, strips=strips, slots=slots),
        out_shape=(
            jax.ShapeDtypeStruct((WIN_OUT * channels, KEYS), BF16),
            jax.ShapeDtypeStruct((3, 144, 2 * WIN_OUT * channels), BF16),
            jax.ShapeDtypeStruct((96, WIN_OUT * channels), BF16),
            jax.ShapeDtypeStruct((fields * time, tm * (slots + 1) * fields), F32),
        ),
        in_specs=[VMEM] * 4,
        out_specs=(VMEM,) * 4,
        compiler_params=params(),
        cost_estimate=pl.CostEstimate(flops=10**12, bytes_accessed=10**9, transcendentals=0),
        name="prepare",
    )(w1_taps, bias_row, w2_taps, correlation)

    kept = pl.pallas_call(
        functools.partial(inner_kernel, strips=strips, slots=slots),
        out_shape=jax.ShapeDtypeStruct((slots, 56, cols), F32),
        in_specs=[VMEM] * 5,
        out_specs=VMEM,
        compiler_params=params(),
        name="inner",
    )(own, core_got, w1, w2, w2_half)

    send = pl.pallas_call(
        functools.partial(outer_kernel, strips=strips, slots=slots, parts_across=parts_across),
        out_shape=jax.ShapeDtypeStruct((tm, *block), F32),
        in_specs=[VMEM] * 5,
        out_specs=VMEM,
        compiler_params=params(),
        name="outer",
    )(own, chip_got, kept, w1, w2)

    blocks = lax.all_to_all(send, "tm", split_axis=0, concat_axis=0, tiled=True)
    mixed = pl.pallas_call(
        functools.partial(mix_kernel, slots=slots),
        out_shape=jax.ShapeDtypeStruct((tm, width // LANES, slots * fields, LANES), F32),
        in_specs=[VMEM] * 2,
        out_specs=VMEM,
        compiler_params=params(),
        name="mix",
    )(mix, blocks)
    back = lax.all_to_all(mixed, "tm", split_axis=0, concat_axis=0, tiled=True)
    return pl.pallas_call(
        place_kernel,
        out_shape=jax.ShapeDtypeStruct(increment.shape, F32),
        in_specs=[VMEM],
        out_specs=hbm,
        scratch_shapes=[strip, pltpu.SemaphoreType.DMA((slots,))],
        compiler_params=params(),
        name="place",
    )(back.reshape(-1, LANES))


def solution(mesh):
    placed = (P("tm", None, "space", None), P("tm", None, "space", None), P(), P(), P(), P())
    return jax.shard_map(
        body, mesh=mesh, in_specs=placed, out_specs=P("tm", None, "space", None), check_vma=False
    )
```

```python
import functools

import jax
import jax.numpy as jnp
from jax import lax
from jax.experimental import pallas as pl
from jax.experimental.pallas import tpu as pltpu
from jax.sharding import PartitionSpec as P

STEPS = 2
TENDENCY = 0.5
HALO = 2 * STEPS
F32 = jnp.float32
BF16 = jnp.bfloat16
EXACT = lax.Precision.HIGHEST
VMEM = pl.BlockSpec(memory_space=pltpu.VMEM)

WIN_OUT = 4
LANES = 128
KEYS = 256
HALF_KEYS = 160
COLUMN_BLOCKS = 2
CHUNK = 16


def iota(shape, dim):
    return lax.broadcasted_iota(jnp.int32, shape, dim)


def split(value):
    high = value.astype(BF16)
    return high, (value - high.astype(F32)).astype(BF16)


def pack_kernel(
    traj_hbm, incr_hbm, w1_hbm, bias_hbm, w2_hbm, corr_hbm,
    own_ref, core_ref, chip_ref, w1_ref, bias_ref, w2_ref, corr_ref,
    traj_ref, incr_ref, sems,
):
    pairs = (
        (traj_hbm, traj_ref), (incr_hbm, incr_ref), (w1_hbm, w1_ref), (bias_hbm, bias_ref), (w2_hbm, w2_ref), (corr_hbm, corr_ref)
    )
    copies = [pltpu.make_async_copy(src, dst, sems.at[n]) for n, (src, dst) in enumerate(pairs)]
    for copy in copies:
        copy.start()
    slots, fields, rows, _ = traj_ref.shape
    half = rows // 2 * fields
    odd = lax.axis_index("space") % 2
    core_half = pl.ds(pl.multiple_of((1 - odd) * half, half), half)
    chip_half = pl.ds(pl.multiple_of(odd * half, half), half)
    for kind, ref in enumerate((traj_ref, incr_ref)):
        copies[kind].wait()
        for slot in range(slots):
            index = kind * slots + slot
            for piece in range(own_ref.shape[1]):
                for f in range(fields):
                    own_ref[index, piece, pl.ds(f, rows, stride=fields), :] = ref[
                        slot, f, :, piece * LANES : (piece + 1) * LANES
                    ]
                core_ref[index, piece] = own_ref[index, piece, core_half, :]
                chip_ref[index, piece] = own_ref[index, piece, chip_half, :]
    for copy in copies[2:]:
        copy.wait()


def key_codes(shape, dim):
    key = iota(shape, dim)
    none = -1000
    q = key - 16
    front_high = (q // 32) * 24 + q % 16
    q = key - 112
    front_low = (q // 16) * 24 + q % 16
    q = key - 160
    back_high = (q // 16) * 24 + 16 + q % 8
    q = key - 208
    back_low = (q // 16) * 24 + 16 + q % 8
    high = jnp.where((key >= 16) & (key < 112), front_high, jnp.where((key >= 160) & (key < 208), back_high, none))
    low = jnp.where((key >= 112) & (key < 160), front_low, jnp.where(key >= 208, back_low, none))
    return high, low, key


def prepare_kernel(w1_ref, bias_ref, w2_ref, corr_ref, w1_out, w2_out, w2_half, mix_out, *, tm, strips, slots):
    fields = w1_ref.shape[2]
    channels = w1_ref.shape[3]
    time = corr_ref.shape[1]
    taps = [(a, b) for a in range(3) for b in range(3)]
    j = iota((40, KEYS), 0)
    t = j // 4
    a = (t >= 3).astype(jnp.int32) + (t >= 6).astype(jnp.int32)
    code = jnp.where(j < 36, (t - 3 * a) * 24 + a * 4 + j % 4, -5000)
    high_code, low_code, key = key_codes((40, KEYS), 1)
    table = jnp.concatenate(
        [w1_ref[a, b] for a, b in taps] + [bias_ref[...], jnp.zeros((3, channels), F32)], axis=0
    )
    bias_row = j == 36
    chosen = [
        jnp.concatenate([(code + 4 * out == codes) | (bias_row & (key == place)) for out in range(WIN_OUT)], axis=1)
        for codes, place in ((high_code, 0), (low_code, 1))
    ]
    chosen = jnp.concatenate([jnp.where(c, 1.0, 0.0) for c in chosen], axis=0).astype(BF16)
    parts = [p.astype(F32) for p in split(table)]
    blocks = lax.dot_general(
        jnp.concatenate(parts, axis=0).astype(BF16), chosen, (((0,), (0,)), ((), ())), preferred_element_type=F32
    )
    for out in range(WIN_OUT):
        w1_out[out * channels : (out + 1) * channels, :] = blocks[:, out * KEYS : (out + 1) * KEYS].astype(BF16)
    keys = WIN_OUT * channels
    spread = jnp.where(iota((channels, keys), 1) % channels == iota((channels, keys), 0), 1.0, 0.0).astype(BF16)
    halves = split(jnp.concatenate([w2_ref[a, b] for a, b in taps], axis=0) * TENDENCY)
    tables = jnp.concatenate([jnp.dot(h, spread, preferred_element_type=F32).astype(BF16) for h in halves], axis=1)
    mj = iota((72, 36), 0)
    mj_tap = jnp.where(mj >= 48, 2, jnp.where(mj >= 24, 1, 0))
    source = mj_tap * 4 + mj % 4
    repeat = jnp.concatenate(
        [jnp.where(iota((72, 36), 1) == tap_row * 12 + source, 1.0, 0.0) for tap_row in range(3)], axis=0
    ).astype(BF16)
    repeated = jnp.dot(repeat, tables, preferred_element_type=F32)
    m = iota((72, keys), 0)
    m_row = (m - jnp.where(m >= 48, 48, jnp.where(m >= 24, 24, 0))) // 4
    k_row = iota((72, keys), 1) // channels
    full = []
    for part in range(2):
        total = jnp.zeros((72, keys), F32)
        for tap_row in range(3):
            block = repeated[72 * tap_row : 72 * (tap_row + 1), keys * part : keys * (part + 1)]
            total = total + jnp.where(k_row == m_row - 2 + tap_row, block, 0.0)
        full.append(total)
    even, keep = chip_side(strips)
    outside = (
        None,
        (even & (k_row < 3)) | (~even & (k_row > 0)),
        (even & (k_row < 1)) | (~even & (k_row > 2)),
    )
    for form, rows_out in enumerate(outside):
        high, low = [t if rows_out is None else jnp.where(rows_out, t * keep, t) for t in full]
        w2_out[form, 0:72, 0:keys] = high.astype(BF16)
        w2_out[form, 0:72, keys:] = high.astype(BF16)
        w2_out[form, 72:, 0:keys] = low.astype(BF16)
        w2_out[form, 72:, keys:] = jnp.zeros((72, keys), BF16)
    short = keys // 2
    high, low = [
        jnp.concatenate([t[24 * tap : 24 * tap + 16, 0:short] for tap in range(3)], axis=0).astype(BF16) for t in full
    ]
    w2_half[0:48, :] = jnp.concatenate([high, high], axis=1)
    w2_half[48:, :] = jnp.concatenate([low, jnp.zeros((48, short), BF16)], axis=1)
    main = tm * slots * fields
    key = iota((time, main + tm * fields), 1)
    slot = jnp.where(key < main, key // fields, (key - main) // fields * slots + slots)
    met = slot == iota(key.shape, 0)
    for f in range(fields):
        pick = jnp.where(met & (key % fields == f), 1.0, 0.0).astype(BF16)
        first = corr_ref[f].astype(BF16)
        rest = corr_ref[f] - first.astype(F32)
        second = rest.astype(BF16)
        rows = slice(f * time, (f + 1) * time)
        high = jnp.dot(first, pick, preferred_element_type=F32).astype(BF16)
        mix_out[rows, :] = jnp.concatenate([high, high, jnp.dot(second, pick, preferred_element_type=F32).astype(BF16)], axis=1)


def moved(value, shift):
    if shift == 0:
        return value
    cols = value.shape[1]
    column = iota(value.shape, 1)
    turned = pltpu.roll(value, shift % cols, 1)
    outside = column == (0 if shift > 0 else cols - 1)
    return jnp.where(outside, 0.0, turned)


def window_keys(groups, bias):
    cols = groups[0].shape[1]
    front_high, front_low, back_high, back_low = [], [], [], []
    high, low = split(jnp.concatenate(groups[:2], axis=0))
    if len(groups) == 3:
        rounded = groups[2].astype(BF16).astype(F32)
        both = jnp.concatenate([rounded, groups[2] - rounded], axis=0).astype(BF16)
    for tap in range(3):
        front_low.append(moved(high, 1 - tap))
        front_high += [front_low[-1], moved(low, 1 - tap)]
        if len(groups) == 3:
            back_high.append(moved(both, 1 - tap))
    back_low = back_high
    first = jnp.full((16, cols), 1.0 if bias else 0.0, BF16)
    return jnp.concatenate([first] + front_high + front_low + back_high + back_low, axis=0)


def hidden_pair(state_groups, tangent_groups, w1_ref):
    rows, keys = w1_ref.shape
    if len(state_groups) == 2:
        rows, keys = rows // 2, HALF_KEYS
    w1 = w1_ref[0:rows, 0:keys]
    state_keys = window_keys(state_groups, True)
    tangent_keys = window_keys(tangent_groups, False)
    cols = state_keys.shape[1]
    width = cols // COLUMN_BLOCKS
    result = ([], [])
    for start in range(0, cols, width):
        z = jnp.dot(w1, state_keys[:, start : start + width], preferred_element_type=F32)
        dz = jnp.dot(w1, tangent_keys[:, start : start + width], preferred_element_type=F32)
        parts = ([], [], [], [])
        for row in range(0, rows, CHUNK):
            h = jnp.tanh(z[row : row + CHUNK])
            g = (1.0 - h * h) * dz[row : row + CHUNK]
            for place, part in zip(parts, (*split(h), *split(g))):
                place.append(part)
        result[0].append(jnp.concatenate(parts[0] + parts[1], axis=0))
        result[1].append(jnp.concatenate(parts[2] + parts[3], axis=0))
    return result


def spread_hidden(hidden, weight):
    taps = []
    for block in hidden:
        product = jnp.dot(weight, block, preferred_element_type=F32)
        half = product.shape[0] // 2
        taps.append(product[:half] + product[half:])
    taps = jnp.concatenate(taps, axis=1)
    third = taps.shape[0] // 3
    total = moved(taps[0:third], 1) + taps[third : 2 * third] + moved(taps[2 * third :], -1)
    return [total[g : g + 8] for g in range(0, third, 8)]


def chip_side(strips):
    me = lax.axis_index("space")
    even = me % 2 == 0
    return even, jnp.where((me == 0) | (me == strips - 1), 0.0, 1.0)


def read_group(ref, index, g):
    pieces = ref.shape[1]
    return jnp.concatenate([ref[index, p, 8 * g : 8 * g + 8, :] for p in range(pieces)], axis=1)


def staggered(slots, one_slot, together):
    waiting = [one_slot(slot) for slot in range(slots)]
    running = []
    while waiting or running:
        starting = len(waiting) if together else 1
        running = waiting[:starting] + running
        waiting = waiting[starting:]
        running = [r for r in running if next(r, True) is None]


def inner_kernel(own_ref, core_got_ref, w1_ref, w2_ref, w2_half_ref, kept_ref, *, strips, slots):
    even, _ = chip_side(strips)

    def pick(if_even, if_odd):
        return jnp.where(even, if_even, if_odd)

    def one_slot(slot):
        line, ends = [], []
        for index in (slot, slots + slot):
            own = [read_group(own_ref, index, g) for g in range(4)]
            core = [read_group(core_got_ref, index, g) for g in range(2)]
            line.append([pick(a, b) for a, b in zip(own + core[:1], core[1:] + own)])
            ends.append(core)
        first = hidden_pair(line[0][0:3], line[1][0:3], w1_ref)
        second = hidden_pair(line[0][2:5], line[1][2:5], w1_ref)
        last = hidden_pair(ends[0], ends[1], w1_ref)
        yield
        moved_on = []
        for kind in range(2):
            a = spread_hidden(first[kind], w2_ref[0])
            b = spread_hidden(second[kind], w2_ref[0])
            c = spread_hidden(last[kind], w2_half_ref[...])
            added = [a[0] + pick(0.0, c[1]), a[1], a[2] + b[0], b[1], b[2] + pick(c[0], 0.0)]
            moved_on.append([x + y for x, y in zip(line[kind], added)])
        s, t = moved_on
        yield
        outer = hidden_pair(
            [pick(a, b) for a, b in zip(s[2:5], s[0:3])], [pick(a, b) for a, b in zip(t[2:5], t[0:3])], w1_ref
        )
        middle = hidden_pair(
            [pick(a, b) for a, b in zip(s[1:3], s[2:4])], [pick(a, b) for a, b in zip(t[1:3], t[2:4])], w1_ref
        )
        yield
        u = spread_hidden(outer[1], w2_ref[0])
        v = spread_hidden(middle[1], w2_half_ref[...])
        kept = [
            pick(t[3], t[1]) + u[1],
            t[2] + pick(u[0], u[2]) + pick(v[1], v[0]),
            pick(t[1], t[3]) + pick(v[0], v[1]),
            pick(s[0], s[4]),
            pick(t[0], t[4]),
            pick(s[1], s[3]),
            pick(t[1], t[3]),
        ]
        for g, value in enumerate(kept):
            kept_ref[slot, 8 * g : 8 * g + 8, :] = value

    staggered(slots, one_slot, False)


def outer_kernel(own_ref, chip_got_ref, kept_ref, w1_ref, w2_ref, send_ref, *, strips, slots, parts_across):
    even, keep = chip_side(strips)
    cols = kept_ref.shape[2]
    width = cols // parts_across
    fields, rows = 4, 8
    packed = send_ref.shape[2] > width

    def pick(if_even, if_odd):
        return jnp.where(even, if_even, if_odd)

    def in_order(values):
        return [pick(a, b) for a, b in zip(values, values[::-1])]

    def send(value, slot):
        for y in range(rows):
            for block in range(parts_across):
                part = value[y * fields : (y + 1) * fields, block * width : (block + 1) * width]
                if slot < slots or not packed:
                    send_ref[y * parts_across + block, slot * fields : (slot + 1) * fields, 0:width] = part
                    continue
                for q in range(slots):
                    send_ref[y * parts_across + block, q * fields : (q + 1) * fields, width:] = part[
                        :, q * width // slots : (q + 1) * width // slots
                    ]

    def start(slot):
        return jnp.concatenate([read_group(own_ref, slots + slot, g) for g in range(4)], axis=0)

    def one_slot(slot):
        near = [kept_ref[slot, 8 * g : 8 * g + 8, :] for g in (3, 4)]
        frames = []
        for index in (slot, slots + slot):
            chip = [read_group(chip_got_ref, index, g) for g in range(2)]
            own = [read_group(own_ref, index, g) for g in (0, 3)]
            frames.append([pick(chip[0], own[1]), pick(chip[1], chip[0]), pick(own[0], chip[1])])
        pair = hidden_pair(frames[0], frames[1], w1_ref)
        yield
        moved_on = []
        for kind in range(2):
            w = spread_hidden(pair[kind], w2_ref[1])
            moved_on.append([(frames[kind][1] + w[1]) * keep, near[kind] + pick(w[2], w[0])])
        state, tangent = moved_on
        yield
        f_outer, f_middle, f_inner, s_next, t_next = [kept_ref[slot, 8 * g : 8 * g + 8, :] for g in (0, 1, 2, 5, 6)]
        pair = hidden_pair(in_order(state + [s_next]), in_order(tangent + [t_next]), w1_ref)
        yield
        x = spread_hidden(pair[1], w2_ref[2])
        ends = [tangent[1] + x[1], f_inner + pick(x[2], x[0]), f_middle, f_outer]
        final = jnp.concatenate(in_order(ends), axis=0)
        send(start(slot + 1) - final if slot < slots - 1 else -final, slot + 1)

    send(start(0), 0)
    staggered(slots, one_slot, True)
    if not packed:
        send_ref[:, (slots + 1) * fields :, :] = jnp.zeros((rows * parts_across, fields, width), F32)


def mix_kernel(mix_ref, block_ref, out_ref, *, slots):
    count, pieces, rows, _ = out_ref.shape
    width = pieces * LANES
    fields = rows // slots
    time = count * slots
    main = block_ref[:, 0:rows, 0:width].reshape(count * rows, width)
    if block_ref.shape[2] > width:
        last = [
            jnp.concatenate([block_ref[d, q * fields : (q + 1) * fields, width:] for d in range(count)], axis=0)
            for q in range(slots)
        ]
        last = jnp.concatenate(last, axis=1)
    else:
        last = jnp.concatenate([block_ref[d, rows : rows + fields, :] for d in range(count)], axis=0)
    keys = jnp.concatenate([main, last], axis=0)
    high, low = split(keys)
    out = jnp.dot(mix_ref[...], jnp.concatenate([high, low, high], axis=0), preferred_element_type=F32)
    for d in range(count):
        for f in range(fields):
            start = f * time + d * slots
            for p in range(pieces):
                out_ref[d, p, f * slots : (f + 1) * slots, :] = out[start : start + slots, p * LANES : (p + 1) * LANES]


def place_kernel(rows_ref, out_hbm, out_ref, sems):
    slots, fields, rows, cols = out_ref.shape
    pieces = cols // LANES
    copies = []
    for slot in range(slots):
        for f in range(fields):
            for p in range(pieces):
                line = (p * fields + f) * slots + slot
                out_ref[slot, f, :, p * LANES : (p + 1) * LANES] = rows_ref[
                    pl.ds(line, rows, stride=pieces * fields * slots), :
                ]
        copies.append(pltpu.make_async_copy(out_ref.at[slot], out_hbm.at[slot], sems.at[slot]))
        copies[-1].start()
    for copy in copies:
        copy.wait()


def params():
    return pltpu.CompilerParams(vmem_limit_bytes=24 * 1024 * 1024)


def body(increment, trajectory, input_weight, bias, output_weight, correlation):
    slots, fields, rows, cols = increment.shape
    channels = input_weight.shape[0]
    tm = lax.axis_size("tm")
    strips = lax.axis_size("space")
    time = correlation.shape[1]
    parts_across = tm // rows
    width = cols // parts_across

    hbm = pl.BlockSpec(memory_space=pltpu.HBM)
    whole = jax.ShapeDtypeStruct((2 * slots, cols // LANES, rows * fields, LANES), F32)
    half = jax.ShapeDtypeStruct((2 * slots, cols // LANES, rows // 2 * fields, LANES), F32)
    w1_taps = jnp.transpose(input_weight, (2, 3, 1, 0))
    w2_taps = jnp.transpose(output_weight, (2, 3, 0, 1))
    loaded = [
        jax.ShapeDtypeStruct(shape, F32) for shape in (w1_taps.shape, (1, channels), w2_taps.shape, correlation.shape)
    ]
    strip = pltpu.VMEM(increment.shape, F32)
    own, core, chip, w1_taps, bias_row, w2_taps, correlation = pl.pallas_call(
        pack_kernel,
        out_shape=(whole, half, half, *loaded),
        in_specs=[hbm] * 6,
        out_specs=(VMEM,) * 7,
        scratch_shapes=[strip, strip, pltpu.SemaphoreType.DMA((6,))],
        compiler_params=params(),
        name="pack",
    )(*[pltpu.with_memory_space_constraint(x, pltpu.HBM) for x in (trajectory, increment, w1_taps, bias[None], w2_taps, correlation)])

    def swapped(value, first):
        pairs = [(i, i + 1) for i in range(first, strips - 1, 2)]
        return lax.ppermute(value, "space", pairs + [(j, i) for i, j in pairs])

    chip_got = swapped(chip, 1)
    core_got = swapped(core, 0)

    packed = width // slots % LANES == 0
    block = (slots * fields, width + width // slots) if packed else ((slots + 2) * fields, width)
    w1, w2, w2_half, mix = pl.pallas_call(
        functools.partial(prepare_kernel, tm=tm, strips=strips, slots=slots),
        out_shape=(
            jax.ShapeDtypeStruct((WIN_OUT * channels, KEYS), BF16),
            jax.ShapeDtypeStruct((3, 144, 2 * WIN_OUT * channels), BF16),
            jax.ShapeDtypeStruct((96, WIN_OUT * channels), BF16),
            jax.ShapeDtypeStruct((fields * time, 3 * tm * (slots + 1) * fields), BF16),
        ),
        in_specs=[VMEM] * 4,
        out_specs=(VMEM,) * 4,
        compiler_params=params(),
        name="prepare",
    )(w1_taps, bias_row, w2_taps, correlation)

    kept = pl.pallas_call(
        functools.partial(inner_kernel, strips=strips, slots=slots),
        out_shape=jax.ShapeDtypeStruct((slots, 56, cols), F32),
        in_specs=[VMEM] * 5,
        out_specs=VMEM,
        compiler_params=params(),
        name="inner",
    )(own, core_got, w1, w2, w2_half)

    send = pl.pallas_call(
        functools.partial(outer_kernel, strips=strips, slots=slots, parts_across=parts_across),
        out_shape=jax.ShapeDtypeStruct((tm, *block), F32),
        in_specs=[VMEM] * 5,
        out_specs=VMEM,
        compiler_params=params(),
        name="outer",
    )(own, chip_got, kept, w1, w2)

    blocks = lax.all_to_all(send, "tm", split_axis=0, concat_axis=0, tiled=True)
    mixed = pl.pallas_call(
        functools.partial(mix_kernel, slots=slots),
        out_shape=jax.ShapeDtypeStruct((tm, width // LANES, slots * fields, LANES), F32),
        in_specs=[VMEM] * 2,
        out_specs=VMEM,
        compiler_params=params(),
        name="mix",
    )(mix, blocks)
    back = lax.all_to_all(mixed, "tm", split_axis=0, concat_axis=0, tiled=True)
    return pl.pallas_call(
        place_kernel,
        out_shape=jax.ShapeDtypeStruct(increment.shape, F32),
        in_specs=[VMEM],
        out_specs=hbm,
        scratch_shapes=[strip, pltpu.SemaphoreType.DMA((slots,))],
        compiler_params=params(),
        name="place",
    )(back.reshape(-1, LANES))


def solution(mesh):
    placed = (P("tm", None, "space", None), P("tm", None, "space", None), P(), P(), P(), P())
    return jax.shard_map(
        body, mesh=mesh, in_specs=placed, out_specs=P("tm", None, "space", None), check_vma=False
    )
```

```python
import functools

import jax
import jax.numpy as jnp
from jax import lax
from jax.experimental import pallas as pl
from jax.experimental.pallas import tpu as pltpu
from jax.sharding import PartitionSpec as P

STEPS = 2
TENDENCY = 0.5
HALO = 2 * STEPS
F32 = jnp.float32
BF16 = jnp.bfloat16
EXACT = lax.Precision.HIGHEST
VMEM = pl.BlockSpec(memory_space=pltpu.VMEM)

WIN_OUT = 4
LANES = 128
KEYS = 256
HALF_KEYS = 160
COLUMN_BLOCKS = 2
CHUNK = 16


def iota(shape, dim):
    return lax.broadcasted_iota(jnp.int32, shape, dim)


def split(value):
    high = value.astype(BF16)
    return high, (value - high.astype(F32)).astype(BF16)


def pack_kernel(
    traj_hbm, incr_hbm, w1_hbm, bias_hbm, w2_hbm, corr_hbm,
    own_ref, core_ref, chip_ref, w1_ref, bias_ref, w2_ref, corr_ref,
    traj_ref, incr_ref, sems,
):
    pairs = (
        (traj_hbm, traj_ref), (incr_hbm, incr_ref), (w1_hbm, w1_ref), (bias_hbm, bias_ref), (w2_hbm, w2_ref), (corr_hbm, corr_ref)
    )
    copies = [pltpu.make_async_copy(src, dst, sems.at[n]) for n, (src, dst) in enumerate(pairs)]
    for copy in copies:
        copy.start()
    slots, fields, rows, _ = traj_ref.shape
    half = rows // 2 * fields
    odd = lax.axis_index("space") % 2
    core_half = pl.ds(pl.multiple_of((1 - odd) * half, half), half)
    chip_half = pl.ds(pl.multiple_of(odd * half, half), half)
    for kind, ref in enumerate((traj_ref, incr_ref)):
        copies[kind].wait()
        for slot in range(slots):
            index = kind * slots + slot
            for piece in range(own_ref.shape[1]):
                for f in range(fields):
                    own_ref[index, piece, pl.ds(f, rows, stride=fields), :] = ref[
                        slot, f, :, piece * LANES : (piece + 1) * LANES
                    ]
                core_ref[index, piece] = own_ref[index, piece, core_half, :]
                chip_ref[index, piece] = own_ref[index, piece, chip_half, :]
    for copy in copies[2:]:
        copy.wait()


def key_codes(shape, dim):
    key = iota(shape, dim)
    none = -1000
    q = key - 16
    front_high = (q // 32) * 24 + q % 16
    q = key - 112
    front_low = (q // 16) * 24 + q % 16
    q = key - 160
    back_high = (q // 16) * 24 + 16 + q % 8
    q = key - 208
    back_low = (q // 16) * 24 + 16 + q % 8
    high = jnp.where((key >= 16) & (key < 112), front_high, jnp.where((key >= 160) & (key < 208), back_high, none))
    low = jnp.where((key >= 112) & (key < 160), front_low, jnp.where(key >= 208, back_low, none))
    return high, low, key


def prepare_kernel(w1_ref, bias_ref, w2_ref, corr_ref, w1_out, w2_out, w2_side, w2_half, w2_end, mix_out, *, tm, strips, slots):
    fields = w1_ref.shape[2]
    channels = w1_ref.shape[3]
    time = corr_ref.shape[1]
    taps = [(a, b) for a in range(3) for b in range(3)]
    j = iota((40, KEYS), 0)
    t = j // 4
    a = (t >= 3).astype(jnp.int32) + (t >= 6).astype(jnp.int32)
    code = jnp.where(j < 36, (t - 3 * a) * 24 + a * 4 + j % 4, -5000)
    high_code, low_code, key = key_codes((40, KEYS), 1)
    table = jnp.concatenate(
        [w1_ref[a, b] for a, b in taps] + [bias_ref[...], jnp.zeros((3, channels), F32)], axis=0
    )
    bias_row = j == 36
    chosen = [
        jnp.concatenate([(code + 4 * out == codes) | (bias_row & (key == place)) for out in range(WIN_OUT)], axis=1)
        for codes, place in ((high_code, 0), (low_code, 1))
    ]
    chosen = jnp.concatenate([jnp.where(c, 1.0, 0.0) for c in chosen], axis=0).astype(BF16)
    parts = [p.astype(F32) for p in split(table)]
    blocks = lax.dot_general(
        jnp.concatenate(parts, axis=0).astype(BF16), chosen, (((0,), (0,)), ((), ())), preferred_element_type=F32
    )
    for out in range(WIN_OUT):
        w1_out[out * channels : (out + 1) * channels, :] = blocks[:, out * KEYS : (out + 1) * KEYS].astype(BF16)
    keys = WIN_OUT * channels
    spread = jnp.where(iota((channels, keys), 1) % channels == iota((channels, keys), 0), 1.0, 0.0).astype(BF16)
    halves = split(jnp.concatenate([w2_ref[a, b] for a, b in taps], axis=0) * TENDENCY)
    tables = jnp.concatenate([jnp.dot(h, spread, preferred_element_type=F32).astype(BF16) for h in halves], axis=1)
    mj = iota((72, 36), 0)
    mj_tap = jnp.where(mj >= 48, 2, jnp.where(mj >= 24, 1, 0))
    source = mj_tap * 4 + mj % 4
    repeat = jnp.concatenate(
        [jnp.where(iota((72, 36), 1) == tap_row * 12 + source, 1.0, 0.0) for tap_row in range(3)], axis=0
    ).astype(BF16)
    repeated = jnp.dot(repeat, tables, preferred_element_type=F32)
    m = iota((72, keys), 0)
    m_row = (m - jnp.where(m >= 48, 48, jnp.where(m >= 24, 24, 0))) // 4
    k_row = iota((72, keys), 1) // channels
    full = []
    for part in range(2):
        total = jnp.zeros((72, keys), F32)
        for tap_row in range(3):
            block = repeated[72 * tap_row : 72 * (tap_row + 1), keys * part : keys * (part + 1)]
            total = total + jnp.where(k_row == m_row - 2 + tap_row, block, 0.0)
        full.append(total)
    even, keep = chip_side(strips)

    def operand(tables):
        high, low = tables
        return jnp.concatenate(
            [jnp.concatenate([high, high], axis=1), jnp.concatenate([low, jnp.zeros(low.shape, F32)], axis=1)], axis=0
        ).astype(BF16)

    def groups_of(table, if_even, if_odd, count, width):
        rows = [
            jnp.where(even, table[24 * t + 8 * e : 24 * t + 8 * e + 8], table[24 * t + 8 * o : 24 * t + 8 * o + 8])
            for t in range(3)
            for e, o in list(zip(if_even, if_odd))[:count]
        ]
        return jnp.concatenate(rows, axis=0)[:, 0:width]

    first_out = (even & (k_row < 3)) | (~even & (k_row > 0))
    second_out = (even & (k_row < 1)) | (~even & (k_row > 2))
    w2_out[...] = operand(full)
    for form, (rows_out, if_even, if_odd) in enumerate(
        ((first_out, (1, 2), (1, 0)), (second_out, (1, 2), (1, 0)), (None, (1, 0), (1, 2)))
    ):
        kept = [t if rows_out is None else jnp.where(rows_out, t * keep, t) for t in full]
        w2_side[form] = operand([groups_of(t, if_even, if_odd, 2, keys) for t in kept])
    short = keys // 2
    w2_half[...] = operand([groups_of(t, (0, 1), (0, 1), 2, short) for t in full])
    w2_end[...] = operand([groups_of(t, (0,), (1,), 1, short) for t in full])
    main = tm * slots * fields
    key = iota((time, main + tm * fields), 1)
    slot = jnp.where(key < main, key // fields, (key - main) // fields * slots + slots)
    met = slot == iota(key.shape, 0)
    for f in range(fields):
        pick = jnp.where(met & (key % fields == f), 1.0, 0.0).astype(BF16)
        first = corr_ref[f].astype(BF16)
        rest = corr_ref[f] - first.astype(F32)
        second = rest.astype(BF16)
        rows = slice(f * time, (f + 1) * time)
        high = jnp.dot(first, pick, preferred_element_type=F32).astype(BF16)
        mix_out[rows, :] = jnp.concatenate([high, high, jnp.dot(second, pick, preferred_element_type=F32).astype(BF16)], axis=1)


def moved(value, shift):
    if shift == 0:
        return value
    cols = value.shape[1]
    column = iota(value.shape, 1)
    turned = pltpu.roll(value, shift % cols, 1)
    outside = column == (0 if shift > 0 else cols - 1)
    return jnp.where(outside, 0.0, turned)


def window_keys(groups, bias):
    cols = groups[0].shape[1]
    front_high, front_low, back_high, back_low = [], [], [], []
    high, low = split(jnp.concatenate(groups[:2], axis=0))
    if len(groups) == 3:
        rounded = groups[2].astype(BF16).astype(F32)
        both = jnp.concatenate([rounded, groups[2] - rounded], axis=0).astype(BF16)
    for tap in range(3):
        front_low.append(moved(high, 1 - tap))
        front_high += [front_low[-1], moved(low, 1 - tap)]
        if len(groups) == 3:
            back_high.append(moved(both, 1 - tap))
    back_low = back_high
    first = jnp.full((16, cols), 1.0 if bias else 0.0, BF16)
    return jnp.concatenate([first] + front_high + front_low + back_high + back_low, axis=0)


def hidden_pair(state_groups, tangent_groups, w1_ref):
    rows, keys = w1_ref.shape
    if len(state_groups) == 2:
        rows, keys = rows // 2, HALF_KEYS
    w1 = w1_ref[0:rows, 0:keys]
    state_keys = window_keys(state_groups, True)
    tangent_keys = window_keys(tangent_groups, False)
    cols = state_keys.shape[1]
    width = cols // COLUMN_BLOCKS
    result = ([], [])
    for start in range(0, cols, width):
        z = jnp.dot(w1, state_keys[:, start : start + width], preferred_element_type=F32)
        dz = jnp.dot(w1, tangent_keys[:, start : start + width], preferred_element_type=F32)
        parts = ([], [], [], [])
        for row in range(0, rows, CHUNK):
            h = jnp.tanh(z[row : row + CHUNK])
            g = (1.0 - h * h) * dz[row : row + CHUNK]
            for place, part in zip(parts, (*split(h), *split(g))):
                place.append(part)
        result[0].append(jnp.concatenate(parts[0] + parts[1], axis=0))
        result[1].append(jnp.concatenate(parts[2] + parts[3], axis=0))
    return result


def spread_hidden(hidden, weight):
    taps = []
    for block in hidden:
        product = jnp.dot(weight, block, preferred_element_type=F32)
        half = product.shape[0] // 2
        taps.append(product[:half] + product[half:])
    taps = jnp.concatenate(taps, axis=1)
    third = taps.shape[0] // 3
    total = moved(taps[0:third], 1) + taps[third : 2 * third] + moved(taps[2 * third :], -1)
    return [total[g : g + 8] for g in range(0, third, 8)]


def chip_side(strips):
    me = lax.axis_index("space")
    even = me % 2 == 0
    return even, jnp.where((me == 0) | (me == strips - 1), 0.0, 1.0)


def read_group(ref, index, g):
    pieces = ref.shape[1]
    return jnp.concatenate([ref[index, p, 8 * g : 8 * g + 8, :] for p in range(pieces)], axis=1)


def staggered(slots, one_slot, together):
    waiting = [one_slot(slot) for slot in range(slots)]
    running = []
    while waiting or running:
        starting = len(waiting) if together else 1
        running = waiting[:starting] + running
        waiting = waiting[starting:]
        running = [r for r in running if next(r, True) is None]


def inner_kernel(own_ref, core_got_ref, w1_ref, w2_ref, w2_side_ref, w2_half_ref, w2_end_ref, kept_ref, *, strips, slots):
    even, _ = chip_side(strips)

    def pick(if_even, if_odd):
        return jnp.where(even, if_even, if_odd)

    def one_slot(slot):
        line, ends = [], []
        for index in (slot, slots + slot):
            own = [read_group(own_ref, index, g) for g in range(4)]
            core = [read_group(core_got_ref, index, g) for g in range(2)]
            line.append([pick(a, b) for a, b in zip(own + core[:1], core[1:] + own)])
            ends.append(core)
        first = hidden_pair(line[0][0:3], line[1][0:3], w1_ref)
        second = hidden_pair(line[0][2:5], line[1][2:5], w1_ref)
        last = hidden_pair(ends[0], ends[1], w1_ref)
        yield
        moved_on = []
        for kind in range(2):
            a = spread_hidden(first[kind], w2_ref[...])
            b = spread_hidden(second[kind], w2_ref[...])
            (c,) = spread_hidden(last[kind], w2_end_ref[...])
            added = [a[0] + pick(0.0, c), a[1], a[2] + b[0], b[1], b[2] + pick(c, 0.0)]
            moved_on.append([x + y for x, y in zip(line[kind], added)])
        s, t = moved_on
        yield
        outer = hidden_pair(
            [pick(a, b) for a, b in zip(s[2:5], s[0:3])], [pick(a, b) for a, b in zip(t[2:5], t[0:3])], w1_ref
        )
        middle = hidden_pair(
            [pick(a, b) for a, b in zip(s[1:3], s[2:4])], [pick(a, b) for a, b in zip(t[1:3], t[2:4])], w1_ref
        )
        yield
        u = spread_hidden(outer[1], w2_side_ref[2])
        v = spread_hidden(middle[1], w2_half_ref[...])
        kept = [
            pick(t[3], t[1]) + u[0],
            t[2] + u[1] + pick(v[1], v[0]),
            pick(t[1], t[3]) + pick(v[0], v[1]),
            pick(s[0], s[4]),
            pick(t[0], t[4]),
            pick(s[1], s[3]),
            pick(t[1], t[3]),
        ]
        for g, value in enumerate(kept):
            kept_ref[slot, 8 * g : 8 * g + 8, :] = value

    staggered(slots, one_slot, False)


def outer_kernel(own_ref, chip_got_ref, kept_ref, w1_ref, w2_side_ref, send_ref, *, strips, slots, parts_across):
    even, keep = chip_side(strips)
    cols = kept_ref.shape[2]
    width = cols // parts_across
    fields, rows = 4, 8
    packed = send_ref.shape[2] > width

    def pick(if_even, if_odd):
        return jnp.where(even, if_even, if_odd)

    def in_order(values):
        return [pick(a, b) for a, b in zip(values, values[::-1])]

    def send(value, slot):
        for y in range(rows):
            for block in range(parts_across):
                part = value[y * fields : (y + 1) * fields, block * width : (block + 1) * width]
                if slot < slots or not packed:
                    send_ref[y * parts_across + block, slot * fields : (slot + 1) * fields, 0:width] = part
                    continue
                for q in range(slots):
                    send_ref[y * parts_across + block, q * fields : (q + 1) * fields, width:] = part[
                        :, q * width // slots : (q + 1) * width // slots
                    ]

    def start(slot):
        return jnp.concatenate([read_group(own_ref, slots + slot, g) for g in range(4)], axis=0)

    def one_slot(slot):
        near = [kept_ref[slot, 8 * g : 8 * g + 8, :] for g in (3, 4)]
        frames = []
        for index in (slot, slots + slot):
            chip = [read_group(chip_got_ref, index, g) for g in range(2)]
            own = [read_group(own_ref, index, g) for g in (0, 3)]
            frames.append([pick(chip[0], own[1]), pick(chip[1], chip[0]), pick(own[0], chip[1])])
        pair = hidden_pair(frames[0], frames[1], w1_ref)
        yield
        moved_on = []
        for kind in range(2):
            w = spread_hidden(pair[kind], w2_side_ref[0])
            moved_on.append([(frames[kind][1] + w[0]) * keep, near[kind] + w[1]])
        state, tangent = moved_on
        yield
        f_outer, f_middle, f_inner, s_next, t_next = [kept_ref[slot, 8 * g : 8 * g + 8, :] for g in (0, 1, 2, 5, 6)]
        pair = hidden_pair(in_order(state + [s_next]), in_order(tangent + [t_next]), w1_ref)
        yield
        x = spread_hidden(pair[1], w2_side_ref[1])
        ends = [tangent[1] + x[0], f_inner + x[1], f_middle, f_outer]
        final = jnp.concatenate(in_order(ends), axis=0)
        send(start(slot + 1) - final if slot < slots - 1 else -final, slot + 1)

    send(start(0), 0)
    staggered(slots, one_slot, True)
    if not packed:
        send_ref[:, (slots + 1) * fields :, :] = jnp.zeros((rows * parts_across, fields, width), F32)


def mix_kernel(mix_ref, block_ref, out_ref, *, slots):
    count, pieces, rows, _ = out_ref.shape
    width = pieces * LANES
    fields = rows // slots
    time = count * slots
    main = block_ref[:, 0:rows, 0:width].reshape(count * rows, width)
    if block_ref.shape[2] > width:
        last = [
            jnp.concatenate([block_ref[d, q * fields : (q + 1) * fields, width:] for d in range(count)], axis=0)
            for q in range(slots)
        ]
        last = jnp.concatenate(last, axis=1)
    else:
        last = jnp.concatenate([block_ref[d, rows : rows + fields, :] for d in range(count)], axis=0)
    keys = jnp.concatenate([main, last], axis=0)
    high, low = split(keys)
    out = jnp.dot(mix_ref[...], jnp.concatenate([high, low, high], axis=0), preferred_element_type=F32)
    for d in range(count):
        for f in range(fields):
            start = f * time + d * slots
            for p in range(pieces):
                out_ref[d, p, f * slots : (f + 1) * slots, :] = out[start : start + slots, p * LANES : (p + 1) * LANES]


def place_kernel(rows_ref, out_hbm, out_ref, sems):
    slots, fields, rows, cols = out_ref.shape
    pieces = cols // LANES
    copies = []
    for slot in range(slots):
        for f in range(fields):
            for p in range(pieces):
                line = (p * fields + f) * slots + slot
                out_ref[slot, f, :, p * LANES : (p + 1) * LANES] = rows_ref[
                    pl.ds(line, rows, stride=pieces * fields * slots), :
                ]
        copies.append(pltpu.make_async_copy(out_ref.at[slot], out_hbm.at[slot], sems.at[slot]))
        copies[-1].start()
    for copy in copies:
        copy.wait()


def params():
    return pltpu.CompilerParams(vmem_limit_bytes=24 * 1024 * 1024)


def body(increment, trajectory, input_weight, bias, output_weight, correlation):
    slots, fields, rows, cols = increment.shape
    channels = input_weight.shape[0]
    tm = lax.axis_size("tm")
    strips = lax.axis_size("space")
    time = correlation.shape[1]
    parts_across = tm // rows
    width = cols // parts_across

    hbm = pl.BlockSpec(memory_space=pltpu.HBM)
    whole = jax.ShapeDtypeStruct((2 * slots, cols // LANES, rows * fields, LANES), F32)
    half = jax.ShapeDtypeStruct((2 * slots, cols // LANES, rows // 2 * fields, LANES), F32)
    w1_taps = jnp.transpose(input_weight, (2, 3, 1, 0))
    w2_taps = jnp.transpose(output_weight, (2, 3, 0, 1))
    loaded = [
        jax.ShapeDtypeStruct(shape, F32) for shape in (w1_taps.shape, (1, channels), w2_taps.shape, correlation.shape)
    ]
    strip = pltpu.VMEM(increment.shape, F32)
    own, core, chip, w1_taps, bias_row, w2_taps, correlation = pl.pallas_call(
        pack_kernel,
        out_shape=(whole, half, half, *loaded),
        in_specs=[hbm] * 6,
        out_specs=(VMEM,) * 7,
        scratch_shapes=[strip, strip, pltpu.SemaphoreType.DMA((6,))],
        compiler_params=params(),
        name="pack",
    )(*[pltpu.with_memory_space_constraint(x, pltpu.HBM) for x in (trajectory, increment, w1_taps, bias[None], w2_taps, correlation)])

    def swapped(value, first):
        pairs = [(i, i + 1) for i in range(first, strips - 1, 2)]
        return lax.ppermute(value, "space", pairs + [(j, i) for i, j in pairs])

    chip_got = swapped(chip, 1)
    core_got = swapped(core, 0)

    packed = width // slots % LANES == 0
    block = (slots * fields, width + width // slots) if packed else ((slots + 2) * fields, width)
    w1, w2, w2_side, w2_half, w2_end, mix = pl.pallas_call(
        functools.partial(prepare_kernel, tm=tm, strips=strips, slots=slots),
        out_shape=(
            jax.ShapeDtypeStruct((WIN_OUT * channels, KEYS), BF16),
            jax.ShapeDtypeStruct((144, 2 * WIN_OUT * channels), BF16),
            jax.ShapeDtypeStruct((3, 96, 2 * WIN_OUT * channels), BF16),
            jax.ShapeDtypeStruct((96, WIN_OUT * channels), BF16),
            jax.ShapeDtypeStruct((48, WIN_OUT * channels), BF16),
            jax.ShapeDtypeStruct((fields * time, 3 * tm * (slots + 1) * fields), BF16),
        ),
        in_specs=[VMEM] * 4,
        out_specs=(VMEM,) * 6,
        compiler_params=params(),
        name="prepare",
    )(w1_taps, bias_row, w2_taps, correlation)

    kept = pl.pallas_call(
        functools.partial(inner_kernel, strips=strips, slots=slots),
        out_shape=jax.ShapeDtypeStruct((slots, 56, cols), F32),
        in_specs=[VMEM] * 7,
        out_specs=VMEM,
        compiler_params=params(),
        name="inner",
    )(own, core_got, w1, w2, w2_side, w2_half, w2_end)

    send = pl.pallas_call(
        functools.partial(outer_kernel, strips=strips, slots=slots, parts_across=parts_across),
        out_shape=jax.ShapeDtypeStruct((tm, *block), F32),
        in_specs=[VMEM] * 5,
        out_specs=VMEM,
        compiler_params=params(),
        name="outer",
    )(own, chip_got, kept, w1, w2_side)

    blocks = lax.all_to_all(send, "tm", split_axis=0, concat_axis=0, tiled=True)
    mixed = pl.pallas_call(
        functools.partial(mix_kernel, slots=slots),
        out_shape=jax.ShapeDtypeStruct((tm, width // LANES, slots * fields, LANES), F32),
        in_specs=[VMEM] * 2,
        out_specs=VMEM,
        compiler_params=params(),
        name="mix",
    )(mix, blocks)
    back = lax.all_to_all(mixed, "tm", split_axis=0, concat_axis=0, tiled=True)
    return pl.pallas_call(
        place_kernel,
        out_shape=jax.ShapeDtypeStruct(increment.shape, F32),
        in_specs=[VMEM],
        out_specs=hbm,
        scratch_shapes=[strip, pltpu.SemaphoreType.DMA((slots,))],
        compiler_params=params(),
        name="place",
    )(back.reshape(-1, LANES))


def solution(mesh):
    placed = (P("tm", None, "space", None), P("tm", None, "space", None), P(), P(), P(), P())
    return jax.shard_map(
        body, mesh=mesh, in_specs=placed, out_specs=P("tm", None, "space", None), check_vma=False
    )
```

```python
import functools

import jax
import jax.numpy as jnp
from jax import lax
from jax.experimental import pallas as pl
from jax.experimental.pallas import tpu as pltpu
from jax.sharding import PartitionSpec as P

STEPS = 2
TENDENCY = 0.5
HALO = 2 * STEPS
F32 = jnp.float32
BF16 = jnp.bfloat16
EXACT = lax.Precision.HIGHEST
VMEM = pl.BlockSpec(memory_space=pltpu.VMEM)

WIN_OUT = 4
LANES = 128
KEYS = 256
HALF_KEYS = 160
COLUMN_BLOCKS = 2
CHUNK = 16


def iota(shape, dim):
    return lax.broadcasted_iota(jnp.int32, shape, dim)


def split(value):
    high = value.astype(BF16)
    return high, (value - high.astype(F32)).astype(BF16)


def pack_kernel(
    traj_hbm, incr_hbm, w1_hbm, bias_hbm, w2_hbm, corr_hbm,
    own_ref, core_ref, chip_ref, w1_ref, bias_ref, w2_ref, corr_ref,
    traj_ref, incr_ref, sems,
):
    pairs = (
        (traj_hbm, traj_ref), (incr_hbm, incr_ref), (w1_hbm, w1_ref), (bias_hbm, bias_ref), (w2_hbm, w2_ref), (corr_hbm, corr_ref)
    )
    copies = [pltpu.make_async_copy(src, dst, sems.at[n]) for n, (src, dst) in enumerate(pairs)]
    for copy in copies:
        copy.start()
    slots, fields, rows, _ = traj_ref.shape
    half = rows // 2 * fields
    odd = lax.axis_index("space") % 2
    core_half = pl.ds(pl.multiple_of((1 - odd) * half, half), half)
    chip_half = pl.ds(pl.multiple_of(odd * half, half), half)
    for kind, ref in enumerate((traj_ref, incr_ref)):
        copies[kind].wait()
        for slot in range(slots):
            index = kind * slots + slot
            for piece in range(own_ref.shape[1]):
                for f in range(fields):
                    own_ref[index, piece, pl.ds(f, rows, stride=fields), :] = ref[
                        slot, f, :, piece * LANES : (piece + 1) * LANES
                    ]
                core_ref[index, piece] = own_ref[index, piece, core_half, :]
                chip_ref[index, piece] = own_ref[index, piece, chip_half, :]
    for copy in copies[2:]:
        copy.wait()


def key_codes(shape, dim):
    key = iota(shape, dim)
    none = -1000
    q = key - 16
    front_high = (q // 32) * 24 + q % 16
    q = key - 112
    front_low = (q // 16) * 24 + q % 16
    q = key - 160
    back_high = (q // 16) * 24 + 16 + q % 8
    q = key - 208
    back_low = (q // 16) * 24 + 16 + q % 8
    high = jnp.where((key >= 16) & (key < 112), front_high, jnp.where((key >= 160) & (key < 208), back_high, none))
    low = jnp.where((key >= 112) & (key < 160), front_low, jnp.where(key >= 208, back_low, none))
    return high, low, key


def prepare_kernel(w1_ref, bias_ref, w2_ref, corr_ref, w1_out, w2_out, w2_side, w2_half, w2_end, mix_out, *, tm, strips, slots):
    fields = w1_ref.shape[2]
    channels = w1_ref.shape[3]
    time = corr_ref.shape[1]
    taps = [(a, b) for a in range(3) for b in range(3)]
    j = iota((40, KEYS), 0)
    t = j // 4
    a = (t >= 3).astype(jnp.int32) + (t >= 6).astype(jnp.int32)
    code = jnp.where(j < 36, (t - 3 * a) * 24 + a * 4 + j % 4, -5000)
    high_code, low_code, key = key_codes((40, KEYS), 1)
    table = jnp.concatenate(
        [w1_ref[a, b] for a, b in taps] + [bias_ref[...], jnp.zeros((3, channels), F32)], axis=0
    )
    bias_row = j == 36
    chosen = [
        jnp.concatenate([(code + 4 * out == codes) | (bias_row & (key == place)) for out in range(WIN_OUT)], axis=1)
        for codes, place in ((high_code, 0), (low_code, 1))
    ]
    chosen = jnp.concatenate([jnp.where(c, 1.0, 0.0) for c in chosen], axis=0).astype(BF16)
    parts = [p.astype(F32) for p in split(table)]
    blocks = lax.dot_general(
        jnp.concatenate(parts, axis=0).astype(BF16), chosen, (((0,), (0,)), ((), ())), preferred_element_type=F32
    )
    for out in range(WIN_OUT):
        w1_out[out * channels : (out + 1) * channels, :] = blocks[:, out * KEYS : (out + 1) * KEYS].astype(BF16)
    keys = WIN_OUT * channels
    spread = jnp.where(iota((channels, keys), 1) % channels == iota((channels, keys), 0), 1.0, 0.0).astype(BF16)
    halves = split(jnp.concatenate([w2_ref[a, b] for a, b in taps], axis=0) * TENDENCY)
    tables = jnp.concatenate([jnp.dot(h, spread, preferred_element_type=F32).astype(BF16) for h in halves], axis=1)
    mj = iota((72, 36), 0)
    mj_tap = jnp.where(mj >= 48, 2, jnp.where(mj >= 24, 1, 0))
    source = mj_tap * 4 + mj % 4
    repeat = jnp.concatenate(
        [jnp.where(iota((72, 36), 1) == tap_row * 12 + source, 1.0, 0.0) for tap_row in range(3)], axis=0
    ).astype(BF16)
    repeated = jnp.dot(repeat, tables, preferred_element_type=F32)
    m = iota((72, keys), 0)
    m_row = (m - jnp.where(m >= 48, 48, jnp.where(m >= 24, 24, 0))) // 4
    k_row = iota((72, keys), 1) // channels
    full = []
    for part in range(2):
        total = jnp.zeros((72, keys), F32)
        for tap_row in range(3):
            block = repeated[72 * tap_row : 72 * (tap_row + 1), keys * part : keys * (part + 1)]
            total = total + jnp.where(k_row == m_row - 2 + tap_row, block, 0.0)
        full.append(total)
    even, keep = chip_side(strips)

    def operand(tables):
        high, low = tables
        return jnp.concatenate(
            [jnp.concatenate([high, high], axis=1), jnp.concatenate([low, jnp.zeros(low.shape, F32)], axis=1)], axis=0
        ).astype(BF16)

    def groups_of(table, if_even, if_odd, count, width):
        rows = [
            jnp.where(even, table[24 * t + 8 * e : 24 * t + 8 * e + 8], table[24 * t + 8 * o : 24 * t + 8 * o + 8])
            for t in range(3)
            for e, o in list(zip(if_even, if_odd))[:count]
        ]
        return jnp.concatenate(rows, axis=0)[:, 0:width]

    first_out = (even & (k_row < 3)) | (~even & (k_row > 0))
    second_out = (even & (k_row < 1)) | (~even & (k_row > 2))
    w2_out[...] = operand(full)
    for form, (rows_out, if_even, if_odd) in enumerate(
        ((first_out, (1, 2), (1, 0)), (second_out, (1, 2), (1, 0)), (None, (1, 0), (1, 2)))
    ):
        kept = [t if rows_out is None else jnp.where(rows_out, t * keep, t) for t in full]
        w2_side[form] = operand([groups_of(t, if_even, if_odd, 2, keys) for t in kept])
    short = keys // 2
    w2_half[...] = operand([groups_of(t, (0, 1), (0, 1), 2, short) for t in full])
    w2_end[...] = operand([groups_of(t, (0,), (1,), 1, short) for t in full])
    main = tm * slots * fields
    key = iota((time, main + tm * fields), 1)
    slot = jnp.where(key < main, key // fields, (key - main) // fields * slots + slots)
    met = slot == iota(key.shape, 0)
    for f in range(fields):
        pick = jnp.where(met & (key % fields == f), 1.0, 0.0).astype(BF16)
        first = corr_ref[f].astype(BF16)
        rest = corr_ref[f] - first.astype(F32)
        second = rest.astype(BF16)
        rows = slice(f * time, (f + 1) * time)
        high = jnp.dot(first, pick, preferred_element_type=F32).astype(BF16)
        mix_out[rows, :] = jnp.concatenate([high, high, jnp.dot(second, pick, preferred_element_type=F32).astype(BF16)], axis=1)


def moved(value, shift):
    if shift == 0:
        return value
    cols = value.shape[1]
    column = iota(value.shape, 1)
    turned = pltpu.roll(value, shift % cols, 1)
    outside = column == (0 if shift > 0 else cols - 1)
    return jnp.where(outside, 0.0, turned)


def window_keys(groups, bias):
    cols = groups[0].shape[1]
    front_high, front_low, back_high, back_low = [], [], [], []
    high, low = split(jnp.concatenate(groups[:2], axis=0))
    if len(groups) == 3:
        rounded = groups[2].astype(BF16).astype(F32)
        both = jnp.concatenate([rounded, groups[2] - rounded], axis=0).astype(BF16)
    for tap in range(3):
        front_low.append(moved(high, 1 - tap))
        front_high += [front_low[-1], moved(low, 1 - tap)]
        if len(groups) == 3:
            back_high.append(moved(both, 1 - tap))
    back_low = back_high
    first = jnp.full((16, cols), 1.0 if bias else 0.0, BF16)
    return jnp.concatenate([first] + front_high + front_low + back_high + back_low, axis=0)


def hidden_pair(state_groups, tangent_groups, w1_ref):
    rows, keys = w1_ref.shape
    if len(state_groups) == 2:
        rows, keys = rows // 2, HALF_KEYS
    w1 = w1_ref[0:rows, 0:keys]
    state_keys = window_keys(state_groups, True)
    tangent_keys = window_keys(tangent_groups, False)
    cols = state_keys.shape[1]
    width = cols // COLUMN_BLOCKS
    result = ([], [])
    for start in range(0, cols, width):
        z = jnp.dot(w1, state_keys[:, start : start + width], preferred_element_type=F32)
        dz = jnp.dot(w1, tangent_keys[:, start : start + width], preferred_element_type=F32)
        parts = ([], [], [], [])
        for row in range(0, rows, CHUNK):
            h = jnp.tanh(z[row : row + CHUNK])
            g = (1.0 - h * h) * dz[row : row + CHUNK]
            for place, part in zip(parts, (*split(h), *split(g))):
                place.append(part)
        result[0].append(jnp.concatenate(parts[0] + parts[1], axis=0))
        result[1].append(jnp.concatenate(parts[2] + parts[3], axis=0))
    return result


def spread_hidden(hidden, weight):
    taps = []
    for block in hidden:
        product = jnp.dot(weight, block, preferred_element_type=F32)
        half = product.shape[0] // 2
        taps.append(product[:half] + product[half:])
    taps = jnp.concatenate(taps, axis=1)
    third = taps.shape[0] // 3
    total = moved(taps[0:third], 1) + taps[third : 2 * third] + moved(taps[2 * third :], -1)
    return [total[g : g + 8] for g in range(0, third, 8)]


def chip_side(strips):
    me = lax.axis_index("space")
    even = me % 2 == 0
    return even, jnp.where((me == 0) | (me == strips - 1), 0.0, 1.0)


def read_group(ref, index, g):
    pieces = ref.shape[1]
    return jnp.concatenate([ref[index, p, 8 * g : 8 * g + 8, :] for p in range(pieces)], axis=1)


def staggered(slots, one_slot, together):
    waiting = [one_slot(slot) for slot in range(slots)]
    running = []
    while waiting or running:
        starting = len(waiting) if together else 1
        running = waiting[:starting] + running
        waiting = waiting[starting:]
        running = [r for r in running if next(r, True) is None]


def inner_kernel(own_ref, core_got_ref, w1_ref, w2_ref, w2_side_ref, w2_half_ref, w2_end_ref, kept_ref, *, strips, slots):
    even, keep = chip_side(strips)

    def pick(if_even, if_odd):
        return jnp.where(even, if_even, if_odd)

    def in_order(values):
        return [pick(a, b) for a, b in zip(values, values[::-1])]

    def edge_slot(slot):
        outside = jnp.zeros((8, kept_ref.shape[2]), F32)
        lines = []
        for index in (slot, slots + slot):
            own = [read_group(own_ref, index, g) for g in range(4)]
            core = [read_group(core_got_ref, index, g) for g in range(2)]
            lines.append([outside] + in_order(own) + [pick(a, b) for a, b in zip(core, core[::-1])])
        pairs = []
        for start in (0, 2, 4):
            windows = [in_order(line[start : start + 3]) for line in lines]
            pairs.append(hidden_pair(windows[0], windows[1], w1_ref))
            yield
        moved_on = []
        for kind, line in enumerate(lines):
            a = spread_hidden(pairs[0][kind], w2_side_ref[1])
            b = in_order(spread_hidden(pairs[1][kind], w2_ref[...]))
            c = spread_hidden(pairs[2][kind], w2_side_ref[2])
            added = [a[0], a[1] + b[0], b[1], b[2] + c[1], c[0]]
            moved_on.append([outside] + [x + y for x, y in zip(line[1:6], added)])
        s, t = moved_on
        yield
        near = hidden_pair(in_order(s[0:3]), in_order(t[0:3]), w1_ref)
        middle = hidden_pair(in_order(s[2:5]), in_order(t[2:5]), w1_ref)
        far = hidden_pair(in_order(s[4:6]), in_order(t[4:6]), w1_ref)
        yield
        a = spread_hidden(near[1], w2_side_ref[1])
        b = in_order(spread_hidden(middle[1], w2_ref[...]))
        (c,) = spread_hidden(far[1], w2_end_ref[...])
        for g, value in enumerate([a[0], a[1] + b[0], b[1], b[2] + c]):
            kept_ref[slot, 8 * g : 8 * g + 8, :] = t[1 + g] + value

    def one_slot(slot):
        line, ends = [], []
        for index in (slot, slots + slot):
            own = [read_group(own_ref, index, g) for g in range(4)]
            core = [read_group(core_got_ref, index, g) for g in range(2)]
            line.append([pick(a, b) for a, b in zip(own + core[:1], core[1:] + own)])
            ends.append(core)
        first = hidden_pair(line[0][0:3], line[1][0:3], w1_ref)
        second = hidden_pair(line[0][2:5], line[1][2:5], w1_ref)
        last = hidden_pair(ends[0], ends[1], w1_ref)
        yield
        moved_on = []
        for kind in range(2):
            a = spread_hidden(first[kind], w2_ref[...])
            b = spread_hidden(second[kind], w2_ref[...])
            (c,) = spread_hidden(last[kind], w2_end_ref[...])
            added = [a[0] + pick(0.0, c), a[1], a[2] + b[0], b[1], b[2] + pick(c, 0.0)]
            moved_on.append([x + y for x, y in zip(line[kind], added)])
        s, t = moved_on
        yield
        outer = hidden_pair(
            [pick(a, b) for a, b in zip(s[2:5], s[0:3])], [pick(a, b) for a, b in zip(t[2:5], t[0:3])], w1_ref
        )
        middle = hidden_pair(
            [pick(a, b) for a, b in zip(s[1:3], s[2:4])], [pick(a, b) for a, b in zip(t[1:3], t[2:4])], w1_ref
        )
        yield
        u = spread_hidden(outer[1], w2_side_ref[2])
        v = spread_hidden(middle[1], w2_half_ref[...])
        kept = [
            pick(t[3], t[1]) + u[0],
            t[2] + u[1] + pick(v[1], v[0]),
            pick(t[1], t[3]) + pick(v[0], v[1]),
            pick(s[0], s[4]),
            pick(t[0], t[4]),
            pick(s[1], s[3]),
            pick(t[1], t[3]),
        ]
        for g, value in enumerate(kept):
            kept_ref[slot, 8 * g : 8 * g + 8, :] = value

    @pl.when(keep == 0.0)
    def _():
        staggered(slots, edge_slot, False)

    @pl.when(keep != 0.0)
    def _():
        staggered(slots, one_slot, False)


def outer_kernel(own_ref, chip_got_ref, kept_ref, w1_ref, w2_side_ref, send_ref, *, strips, slots, parts_across):
    even, keep = chip_side(strips)
    cols = kept_ref.shape[2]
    width = cols // parts_across
    fields, rows = 4, 8
    packed = send_ref.shape[2] > width

    def pick(if_even, if_odd):
        return jnp.where(even, if_even, if_odd)

    def in_order(values):
        return [pick(a, b) for a, b in zip(values, values[::-1])]

    def send(value, slot):
        for y in range(rows):
            for block in range(parts_across):
                part = value[y * fields : (y + 1) * fields, block * width : (block + 1) * width]
                if slot < slots or not packed:
                    send_ref[y * parts_across + block, slot * fields : (slot + 1) * fields, 0:width] = part
                    continue
                for q in range(slots):
                    send_ref[y * parts_across + block, q * fields : (q + 1) * fields, width:] = part[
                        :, q * width // slots : (q + 1) * width // slots
                    ]

    def start(slot):
        return jnp.concatenate([read_group(own_ref, slots + slot, g) for g in range(4)], axis=0)

    def one_slot(slot):
        near = [kept_ref[slot, 8 * g : 8 * g + 8, :] for g in (3, 4)]
        frames = []
        for index in (slot, slots + slot):
            chip = [read_group(chip_got_ref, index, g) for g in range(2)]
            own = [read_group(own_ref, index, g) for g in (0, 3)]
            frames.append([pick(chip[0], own[1]), pick(chip[1], chip[0]), pick(own[0], chip[1])])
        pair = hidden_pair(frames[0], frames[1], w1_ref)
        yield
        moved_on = []
        for kind in range(2):
            w = spread_hidden(pair[kind], w2_side_ref[0])
            moved_on.append([frames[kind][1] + w[0], near[kind] + w[1]])
        state, tangent = moved_on
        yield
        f_outer, f_middle, f_inner, s_next, t_next = [kept_ref[slot, 8 * g : 8 * g + 8, :] for g in (0, 1, 2, 5, 6)]
        pair = hidden_pair(in_order(state + [s_next]), in_order(tangent + [t_next]), w1_ref)
        yield
        x = spread_hidden(pair[1], w2_side_ref[1])
        ends = [tangent[1] + x[0], f_inner + x[1], f_middle, f_outer]
        residual(slot, ends)

    def residual(slot, ends):
        final = jnp.concatenate(in_order(ends), axis=0)
        send(start(slot + 1) - final if slot < slots - 1 else -final, slot + 1)

    send(start(0), 0)

    @pl.when(keep == 0.0)
    def _():
        for slot in range(slots):
            residual(slot, [kept_ref[slot, 8 * g : 8 * g + 8, :] for g in range(4)])

    @pl.when(keep != 0.0)
    def _():
        staggered(slots, one_slot, True)

    if not packed:
        send_ref[:, (slots + 1) * fields :, :] = jnp.zeros((rows * parts_across, fields, width), F32)


def mix_kernel(mix_ref, block_ref, out_ref, *, slots):
    count, pieces, rows, _ = out_ref.shape
    width = pieces * LANES
    fields = rows // slots
    time = count * slots
    main = block_ref[:, 0:rows, 0:width].reshape(count * rows, width)
    if block_ref.shape[2] > width:
        last = [
            jnp.concatenate([block_ref[d, q * fields : (q + 1) * fields, width:] for d in range(count)], axis=0)
            for q in range(slots)
        ]
        last = jnp.concatenate(last, axis=1)
    else:
        last = jnp.concatenate([block_ref[d, rows : rows + fields, :] for d in range(count)], axis=0)
    keys = jnp.concatenate([main, last], axis=0)
    high, low = split(keys)
    out = jnp.dot(mix_ref[...], jnp.concatenate([high, low, high], axis=0), preferred_element_type=F32)
    for d in range(count):
        for f in range(fields):
            start = f * time + d * slots
            for p in range(pieces):
                out_ref[d, p, f * slots : (f + 1) * slots, :] = out[start : start + slots, p * LANES : (p + 1) * LANES]


def place_kernel(rows_ref, out_hbm, out_ref, sems):
    slots, fields, rows, cols = out_ref.shape
    pieces = cols // LANES
    copies = []
    for slot in range(slots):
        for f in range(fields):
            for p in range(pieces):
                line = (p * fields + f) * slots + slot
                out_ref[slot, f, :, p * LANES : (p + 1) * LANES] = rows_ref[
                    pl.ds(line, rows, stride=pieces * fields * slots), :
                ]
        copies.append(pltpu.make_async_copy(out_ref.at[slot], out_hbm.at[slot], sems.at[slot]))
        copies[-1].start()
    for copy in copies:
        copy.wait()


def params():
    return pltpu.CompilerParams(vmem_limit_bytes=24 * 1024 * 1024)


def body(increment, trajectory, input_weight, bias, output_weight, correlation):
    slots, fields, rows, cols = increment.shape
    channels = input_weight.shape[0]
    tm = lax.axis_size("tm")
    strips = lax.axis_size("space")
    time = correlation.shape[1]
    parts_across = tm // rows
    width = cols // parts_across

    hbm = pl.BlockSpec(memory_space=pltpu.HBM)
    whole = jax.ShapeDtypeStruct((2 * slots, cols // LANES, rows * fields, LANES), F32)
    half = jax.ShapeDtypeStruct((2 * slots, cols // LANES, rows // 2 * fields, LANES), F32)
    w1_taps = jnp.transpose(input_weight, (2, 3, 1, 0))
    w2_taps = jnp.transpose(output_weight, (2, 3, 0, 1))
    loaded = [
        jax.ShapeDtypeStruct(shape, F32) for shape in (w1_taps.shape, (1, channels), w2_taps.shape, correlation.shape)
    ]
    strip = pltpu.VMEM(increment.shape, F32)
    own, core, chip, w1_taps, bias_row, w2_taps, correlation = pl.pallas_call(
        pack_kernel,
        out_shape=(whole, half, half, *loaded),
        in_specs=[hbm] * 6,
        out_specs=(VMEM,) * 7,
        scratch_shapes=[strip, strip, pltpu.SemaphoreType.DMA((6,))],
        compiler_params=params(),
        name="pack",
    )(*[pltpu.with_memory_space_constraint(x, pltpu.HBM) for x in (trajectory, increment, w1_taps, bias[None], w2_taps, correlation)])

    def swapped(value, first):
        pairs = [(i, i + 1) for i in range(first, strips - 1, 2)]
        return lax.ppermute(value, "space", pairs + [(j, i) for i, j in pairs])

    chip_got = swapped(chip, 1)
    core_got = swapped(core, 0)

    packed = width // slots % LANES == 0
    block = (slots * fields, width + width // slots) if packed else ((slots + 2) * fields, width)
    w1, w2, w2_side, w2_half, w2_end, mix = pl.pallas_call(
        functools.partial(prepare_kernel, tm=tm, strips=strips, slots=slots),
        out_shape=(
            jax.ShapeDtypeStruct((WIN_OUT * channels, KEYS), BF16),
            jax.ShapeDtypeStruct((144, 2 * WIN_OUT * channels), BF16),
            jax.ShapeDtypeStruct((3, 96, 2 * WIN_OUT * channels), BF16),
            jax.ShapeDtypeStruct((96, WIN_OUT * channels), BF16),
            jax.ShapeDtypeStruct((48, WIN_OUT * channels), BF16),
            jax.ShapeDtypeStruct((fields * time, 3 * tm * (slots + 1) * fields), BF16),
        ),
        in_specs=[VMEM] * 4,
        out_specs=(VMEM,) * 6,
        compiler_params=params(),
        name="prepare",
    )(w1_taps, bias_row, w2_taps, correlation)

    kept = pl.pallas_call(
        functools.partial(inner_kernel, strips=strips, slots=slots),
        out_shape=jax.ShapeDtypeStruct((slots, 56, cols), F32),
        in_specs=[VMEM] * 7,
        out_specs=VMEM,
        compiler_params=params(),
        name="inner",
    )(own, core_got, w1, w2, w2_side, w2_half, w2_end)

    send = pl.pallas_call(
        functools.partial(outer_kernel, strips=strips, slots=slots, parts_across=parts_across),
        out_shape=jax.ShapeDtypeStruct((tm, *block), F32),
        in_specs=[VMEM] * 5,
        out_specs=VMEM,
        compiler_params=params(),
        name="outer",
    )(own, chip_got, kept, w1, w2_side)

    blocks = lax.all_to_all(send, "tm", split_axis=0, concat_axis=0, tiled=True)
    mixed = pl.pallas_call(
        functools.partial(mix_kernel, slots=slots),
        out_shape=jax.ShapeDtypeStruct((tm, width // LANES, slots * fields, LANES), F32),
        in_specs=[VMEM] * 2,
        out_specs=VMEM,
        compiler_params=params(),
        name="mix",
    )(mix, blocks)
    back = lax.all_to_all(mixed, "tm", split_axis=0, concat_axis=0, tiled=True)
    return pl.pallas_call(
        place_kernel,
        out_shape=jax.ShapeDtypeStruct(increment.shape, F32),
        in_specs=[VMEM],
        out_specs=hbm,
        scratch_shapes=[strip, pltpu.SemaphoreType.DMA((slots,))],
        compiler_params=params(),
        name="place",
    )(back.reshape(-1, LANES))


def solution(mesh):
    placed = (P("tm", None, "space", None), P("tm", None, "space", None), P(), P(), P(), P())
    return jax.shard_map(
        body, mesh=mesh, in_specs=placed, out_specs=P("tm", None, "space", None), check_vma=False
    )
```

```python
import functools

import jax
import jax.numpy as jnp
from jax import lax
from jax.experimental import pallas as pl
from jax.experimental.pallas import tpu as pltpu
from jax.sharding import PartitionSpec as P

STEPS = 2
TENDENCY = 0.5
HALO = 2 * STEPS
F32 = jnp.float32
BF16 = jnp.bfloat16
EXACT = lax.Precision.HIGHEST
VMEM = pl.BlockSpec(memory_space=pltpu.VMEM)

WIN_OUT = 4
LANES = 128
KEYS = 256
HALF_KEYS = 160
COLUMN_BLOCKS = 2
CHUNK = 16


def iota(shape, dim):
    return lax.broadcasted_iota(jnp.int32, shape, dim)


def split(value):
    high = value.astype(BF16)
    return high, (value - high.astype(F32)).astype(BF16)


def pack_kernel(
    traj_hbm, incr_hbm, w1_hbm, bias_hbm, w2_hbm, corr_hbm,
    own_ref, core_ref, chip_ref, w1_ref, bias_ref, w2_ref, corr_ref,
    traj_ref, incr_ref, sems,
):
    pairs = (
        (traj_hbm, traj_ref), (incr_hbm, incr_ref), (w1_hbm, w1_ref), (bias_hbm, bias_ref), (w2_hbm, w2_ref), (corr_hbm, corr_ref)
    )
    copies = [pltpu.make_async_copy(src, dst, sems.at[n]) for n, (src, dst) in enumerate(pairs)]
    for copy in copies:
        copy.start()
    slots, fields, rows, _ = traj_ref.shape
    half = rows // 2 * fields
    odd = lax.axis_index("space") % 2
    core_half = pl.ds(pl.multiple_of((1 - odd) * half, half), half)
    chip_half = pl.ds(pl.multiple_of(odd * half, half), half)
    for kind, ref in enumerate((traj_ref, incr_ref)):
        copies[kind].wait()
        for slot in range(slots):
            index = kind * slots + slot
            for piece in range(own_ref.shape[1]):
                for f in range(fields):
                    own_ref[index, piece, pl.ds(f, rows, stride=fields), :] = ref[
                        slot, f, :, piece * LANES : (piece + 1) * LANES
                    ]
                core_ref[index, piece] = own_ref[index, piece, core_half, :]
                chip_ref[index, piece] = own_ref[index, piece, chip_half, :]
    for copy in copies[2:]:
        copy.wait()


def key_codes(shape, dim):
    key = iota(shape, dim)
    none = -1000
    q = key - 16
    front_high = (q // 32) * 24 + q % 16
    q = key - 112
    front_low = (q // 16) * 24 + q % 16
    q = key - 160
    back_high = (q // 16) * 24 + 16 + q % 8
    q = key - 208
    back_low = (q // 16) * 24 + 16 + q % 8
    high = jnp.where((key >= 16) & (key < 112), front_high, jnp.where((key >= 160) & (key < 208), back_high, none))
    low = jnp.where((key >= 112) & (key < 160), front_low, jnp.where(key >= 208, back_low, none))
    return high, low, key


def prepare_kernel(w1_ref, bias_ref, w2_ref, corr_ref, w1_out, w2_out, w2_side, w2_half, w2_end, mix_out, *, tm, strips, slots):
    fields = w1_ref.shape[2]
    channels = w1_ref.shape[3]
    time = corr_ref.shape[1]
    taps = [(a, b) for a in range(3) for b in range(3)]
    j = iota((40, KEYS), 0)
    t = j // 4
    a = (t >= 3).astype(jnp.int32) + (t >= 6).astype(jnp.int32)
    code = jnp.where(j < 36, (t - 3 * a) * 24 + a * 4 + j % 4, -5000)
    high_code, low_code, key = key_codes((40, KEYS), 1)
    table = jnp.concatenate(
        [w1_ref[a, b] for a, b in taps] + [bias_ref[...], jnp.zeros((3, channels), F32)], axis=0
    )
    bias_row = j == 36
    chosen = [
        jnp.concatenate([(code + 4 * out == codes) | (bias_row & (key == place)) for out in range(WIN_OUT)], axis=1)
        for codes, place in ((high_code, 0), (low_code, 1))
    ]
    chosen = jnp.concatenate([jnp.where(c, 1.0, 0.0) for c in chosen], axis=0).astype(BF16)
    parts = [p.astype(F32) for p in split(table)]
    blocks = lax.dot_general(
        jnp.concatenate(parts, axis=0).astype(BF16), chosen, (((0,), (0,)), ((), ())), preferred_element_type=F32
    )
    for out in range(WIN_OUT):
        w1_out[out * channels : (out + 1) * channels, :] = blocks[:, out * KEYS : (out + 1) * KEYS].astype(BF16)
    keys = WIN_OUT * channels
    spread = jnp.where(iota((channels, keys), 1) % channels == iota((channels, keys), 0), 1.0, 0.0).astype(BF16)
    halves = split(jnp.concatenate([w2_ref[a, b] for a, b in taps], axis=0) * TENDENCY)
    tables = jnp.concatenate([jnp.dot(h, spread, preferred_element_type=F32).astype(BF16) for h in halves], axis=1)
    mj = iota((72, 36), 0)
    mj_tap = jnp.where(mj >= 48, 2, jnp.where(mj >= 24, 1, 0))
    source = mj_tap * 4 + mj % 4
    repeat = jnp.concatenate(
        [jnp.where(iota((72, 36), 1) == tap_row * 12 + source, 1.0, 0.0) for tap_row in range(3)], axis=0
    ).astype(BF16)
    repeated = jnp.dot(repeat, tables, preferred_element_type=F32)
    m = iota((72, keys), 0)
    m_row = (m - jnp.where(m >= 48, 48, jnp.where(m >= 24, 24, 0))) // 4
    k_row = iota((72, keys), 1) // channels
    full = []
    for part in range(2):
        total = jnp.zeros((72, keys), F32)
        for tap_row in range(3):
            block = repeated[72 * tap_row : 72 * (tap_row + 1), keys * part : keys * (part + 1)]
            total = total + jnp.where(k_row == m_row - 2 + tap_row, block, 0.0)
        full.append(total)
    even, keep = chip_side(strips)

    def operand(tables):
        high, low = tables
        return jnp.concatenate(
            [jnp.concatenate([high, high], axis=1), jnp.concatenate([low, jnp.zeros(low.shape, F32)], axis=1)], axis=0
        ).astype(BF16)

    def groups_of(table, if_even, if_odd, count, width):
        rows = [
            jnp.where(even, table[24 * t + 8 * e : 24 * t + 8 * e + 8], table[24 * t + 8 * o : 24 * t + 8 * o + 8])
            for t in range(3)
            for e, o in list(zip(if_even, if_odd))[:count]
        ]
        return jnp.concatenate(rows, axis=0)[:, 0:width]

    first_out = (even & (k_row < 3)) | (~even & (k_row > 0))
    second_out = (even & (k_row < 1)) | (~even & (k_row > 2))
    w2_out[...] = operand(full)
    for form, (rows_out, if_even, if_odd) in enumerate(
        ((first_out, (1, 2), (1, 0)), (second_out, (1, 2), (1, 0)), (None, (1, 0), (1, 2)))
    ):
        kept = [t if rows_out is None else jnp.where(rows_out, t * keep, t) for t in full]
        w2_side[form] = operand([groups_of(t, if_even, if_odd, 2, keys) for t in kept])
    short = keys // 2
    w2_half[...] = operand([groups_of(t, (0, 1), (0, 1), 2, short) for t in full])
    w2_end[...] = operand([groups_of(t, (0,), (1,), 1, short) for t in full])
    main = tm * slots * fields
    key = iota((time, main + tm * fields), 1)
    slot = jnp.where(key < main, key // fields, (key - main) // fields * slots + slots)
    met = slot == iota(key.shape, 0)
    for f in range(fields):
        pick = jnp.where(met & (key % fields == f), 1.0, 0.0).astype(BF16)
        first = corr_ref[f].astype(BF16)
        rest = corr_ref[f] - first.astype(F32)
        second = rest.astype(BF16)
        rows = slice(f * time, (f + 1) * time)
        high = jnp.dot(first, pick, preferred_element_type=F32).astype(BF16)
        mix_out[rows, :] = jnp.concatenate([high, high, jnp.dot(second, pick, preferred_element_type=F32).astype(BF16)], axis=1)


def moved(value, shift):
    if shift == 0:
        return value
    cols = value.shape[1]
    column = iota(value.shape, 1)
    turned = pltpu.roll(value, shift % cols, 1)
    outside = column == (0 if shift > 0 else cols - 1)
    return jnp.where(outside, 0.0, turned)


def window_keys(groups, bias):
    cols = groups[0].shape[1]
    front_high, front_low, back_high, back_low = [], [], [], []
    high, low = split(jnp.concatenate(groups[:2], axis=0))
    if len(groups) == 3:
        rounded = groups[2].astype(BF16).astype(F32)
        both = jnp.concatenate([rounded, groups[2] - rounded], axis=0).astype(BF16)
    for tap in range(3):
        front_low.append(moved(high, 1 - tap))
        front_high += [front_low[-1], moved(low, 1 - tap)]
        if len(groups) == 3:
            back_high.append(moved(both, 1 - tap))
    back_low = back_high
    first = jnp.full((16, cols), 1.0 if bias else 0.0, BF16)
    return jnp.concatenate([first] + front_high + front_low + back_high + back_low, axis=0)


def hidden_pair(state_groups, tangent_groups, w1_ref):
    rows, keys = w1_ref.shape
    if len(state_groups) == 2:
        rows, keys = rows // 2, HALF_KEYS
    w1 = w1_ref[0:rows, 0:keys]
    state_keys = window_keys(state_groups, True)
    tangent_keys = window_keys(tangent_groups, False)
    cols = state_keys.shape[1]
    width = cols // COLUMN_BLOCKS
    result = ([], [])
    for start in range(0, cols, width):
        z = jnp.dot(w1, state_keys[:, start : start + width], preferred_element_type=F32)
        dz = jnp.dot(w1, tangent_keys[:, start : start + width], preferred_element_type=F32)
        parts = ([], [], [], [])
        for row in range(0, rows, CHUNK):
            h = jnp.tanh(z[row : row + CHUNK])
            g = (1.0 - h * h) * dz[row : row + CHUNK]
            for place, part in zip(parts, (*split(h), *split(g))):
                place.append(part)
        result[0].append(jnp.concatenate(parts[0] + parts[1], axis=0))
        result[1].append(jnp.concatenate(parts[2] + parts[3], axis=0))
    return result


def spread_hidden(hidden, weight):
    taps = []
    for block in hidden:
        product = jnp.dot(weight, block, preferred_element_type=F32)
        half = product.shape[0] // 2
        taps.append(product[:half] + product[half:])
    taps = jnp.concatenate(taps, axis=1)
    third = taps.shape[0] // 3
    total = moved(taps[0:third], 1) + taps[third : 2 * third] + moved(taps[2 * third :], -1)
    return [total[g : g + 8] for g in range(0, third, 8)]


def chip_side(strips):
    me = lax.axis_index("space")
    even = me % 2 == 0
    return even, jnp.where((me == 0) | (me == strips - 1), 0.0, 1.0)


def read_group(ref, index, g):
    pieces = ref.shape[1]
    return jnp.concatenate([ref[index, p, 8 * g : 8 * g + 8, :] for p in range(pieces)], axis=1)


def staggered(slots, one_slot, together, first=0):
    waiting = [one_slot(first + slot) for slot in range(slots)]
    running = []
    while waiting or running:
        starting = len(waiting) if together else 1
        running = waiting[:starting] + running
        waiting = waiting[starting:]
        running = [r for r in running if next(r, True) is None]


def inner_kernel(own_ref, core_got_ref, w1_ref, w2_ref, w2_side_ref, w2_half_ref, w2_end_ref, kept_ref, *, strips, slots):
    even, keep = chip_side(strips)

    def pick(if_even, if_odd):
        return jnp.where(even, if_even, if_odd)

    def in_order(values):
        return [pick(a, b) for a, b in zip(values, values[::-1])]

    def edge_slot(slot):
        outside = jnp.zeros((8, kept_ref.shape[2]), F32)
        lines = []
        for index in (slot, slots + slot):
            own = [read_group(own_ref, index, g) for g in range(4)]
            core = [read_group(core_got_ref, index, g) for g in range(2)]
            lines.append([outside] + in_order(own) + [pick(a, b) for a, b in zip(core, core[::-1])])
        pairs = []
        for start in (0, 2, 4):
            windows = [in_order(line[start : start + 3]) for line in lines]
            pairs.append(hidden_pair(windows[0], windows[1], w1_ref))
            yield
        moved_on = []
        for kind, line in enumerate(lines):
            a = spread_hidden(pairs[0][kind], w2_side_ref[1])
            b = in_order(spread_hidden(pairs[1][kind], w2_ref[...]))
            c = spread_hidden(pairs[2][kind], w2_side_ref[2])
            added = [a[0], a[1] + b[0], b[1], b[2] + c[1], c[0]]
            moved_on.append([outside] + [x + y for x, y in zip(line[1:6], added)])
        s, t = moved_on
        yield
        near = hidden_pair(in_order(s[0:3]), in_order(t[0:3]), w1_ref)
        middle = hidden_pair(in_order(s[2:5]), in_order(t[2:5]), w1_ref)
        far = hidden_pair(in_order(s[4:6]), in_order(t[4:6]), w1_ref)
        yield
        a = spread_hidden(near[1], w2_side_ref[1])
        b = in_order(spread_hidden(middle[1], w2_ref[...]))
        (c,) = spread_hidden(far[1], w2_end_ref[...])
        for g, value in enumerate([a[0], a[1] + b[0], b[1], b[2] + c]):
            kept_ref[slot, 8 * g : 8 * g + 8, :] = t[1 + g] + value

    def one_slot(slot):
        line, ends = [], []
        for index in (slot, slots + slot):
            own = [read_group(own_ref, index, g) for g in range(4)]
            core = [read_group(core_got_ref, index, g) for g in range(2)]
            line.append([pick(a, b) for a, b in zip(own + core[:1], core[1:] + own)])
            ends.append(core)
        first = hidden_pair(line[0][0:3], line[1][0:3], w1_ref)
        second = hidden_pair(line[0][2:5], line[1][2:5], w1_ref)
        last = hidden_pair(ends[0], ends[1], w1_ref)
        yield
        moved_on = []
        for kind in range(2):
            a = spread_hidden(first[kind], w2_ref[...])
            b = spread_hidden(second[kind], w2_ref[...])
            (c,) = spread_hidden(last[kind], w2_end_ref[...])
            added = [a[0] + pick(0.0, c), a[1], a[2] + b[0], b[1], b[2] + pick(c, 0.0)]
            moved_on.append([x + y for x, y in zip(line[kind], added)])
        s, t = moved_on
        yield
        outer = hidden_pair(
            [pick(a, b) for a, b in zip(s[2:5], s[0:3])], [pick(a, b) for a, b in zip(t[2:5], t[0:3])], w1_ref
        )
        middle = hidden_pair(
            [pick(a, b) for a, b in zip(s[1:3], s[2:4])], [pick(a, b) for a, b in zip(t[1:3], t[2:4])], w1_ref
        )
        yield
        u = spread_hidden(outer[1], w2_side_ref[2])
        v = spread_hidden(middle[1], w2_half_ref[...])
        kept = [
            pick(t[3], t[1]) + u[0],
            t[2] + u[1] + pick(v[1], v[0]),
            pick(t[1], t[3]) + pick(v[0], v[1]),
            pick(s[0], s[4]),
            pick(t[0], t[4]),
            pick(s[1], s[3]),
            pick(t[1], t[3]),
        ]
        for g, value in enumerate(kept):
            kept_ref[slot, 8 * g : 8 * g + 8, :] = value

    @pl.when(keep == 0.0)
    def _():
        staggered(slots, edge_slot, False)

    @pl.when(keep != 0.0)
    def _():
        staggered(slots, one_slot, False)


def outer_kernel(own_ref, chip_got_ref, kept_ref, w1_ref, w2_side_ref, send_ref, done_ref, *, strips, slots, parts_across):
    even, keep = chip_side(strips)
    cols = kept_ref.shape[2]
    width = cols // parts_across
    fields, rows = 4, 8
    packed = send_ref.shape[2] > width

    def pick(if_even, if_odd):
        return jnp.where(even, if_even, if_odd)

    def in_order(values):
        return [pick(a, b) for a, b in zip(values, values[::-1])]

    def send(value, slot):
        for y in range(rows):
            for block in range(parts_across):
                part = value[y * fields : (y + 1) * fields, block * width : (block + 1) * width]
                if slot < slots or not packed:
                    send_ref[y * parts_across + block, slot * fields : (slot + 1) * fields, 0:width] = part
                    continue
                for q in range(slots):
                    send_ref[y * parts_across + block, q * fields : (q + 1) * fields, width:] = part[
                        :, q * width // slots : (q + 1) * width // slots
                    ]

    def start(slot):
        return jnp.concatenate([read_group(own_ref, slots + slot, g) for g in range(4)], axis=0)

    def one_slot(slot):
        near = [kept_ref[slot, 8 * g : 8 * g + 8, :] for g in (3, 4)]
        frames = []
        for index in (slot, slots + slot):
            chip = [read_group(chip_got_ref, index, g) for g in range(2)]
            own = [read_group(own_ref, index, g) for g in (0, 3)]
            frames.append([pick(chip[0], own[1]), pick(chip[1], chip[0]), pick(own[0], chip[1])])
        pair = hidden_pair(frames[0], frames[1], w1_ref)
        yield
        moved_on = []
        for kind in range(2):
            w = spread_hidden(pair[kind], w2_side_ref[0])
            moved_on.append([frames[kind][1] + w[0], near[kind] + w[1]])
        state, tangent = moved_on
        yield
        f_outer, f_middle, f_inner, s_next, t_next = [kept_ref[slot, 8 * g : 8 * g + 8, :] for g in (0, 1, 2, 5, 6)]
        pair = hidden_pair(in_order(state + [s_next]), in_order(tangent + [t_next]), w1_ref)
        yield
        x = spread_hidden(pair[1], w2_side_ref[1])
        ends = [tangent[1] + x[0], f_inner + x[1], f_middle, f_outer]
        for g, value in enumerate(ends):
            done_ref[slot, 8 * g : 8 * g + 8, :] = value

    def residual(slot, ref):
        final = jnp.concatenate(in_order([ref[slot, 8 * g : 8 * g + 8, :] for g in range(4)]), axis=0)
        send(start(slot + 1) - final if slot < slots - 1 else -final, slot + 1)

    send(start(0), 0)

    @pl.when(keep == 0.0)
    def _():
        for slot in range(slots):
            residual(slot, kept_ref)

    @pl.when(keep != 0.0)
    def _():
        def some_slots(turn, carry):
            staggered(2, one_slot, True, 2 * turn)
            return carry

        lax.fori_loop(0, slots // 2, some_slots, 0)
        for slot in range(slots):
            residual(slot, done_ref)

    if not packed:
        send_ref[:, (slots + 1) * fields :, :] = jnp.zeros((rows * parts_across, fields, width), F32)


def mix_kernel(mix_ref, block_ref, out_ref, *, slots):
    count, pieces, rows, _ = out_ref.shape
    width = pieces * LANES
    fields = rows // slots
    time = count * slots
    main = block_ref[:, 0:rows, 0:width].reshape(count * rows, width)
    if block_ref.shape[2] > width:
        last = [
            jnp.concatenate([block_ref[d, q * fields : (q + 1) * fields, width:] for d in range(count)], axis=0)
            for q in range(slots)
        ]
        last = jnp.concatenate(last, axis=1)
    else:
        last = jnp.concatenate([block_ref[d, rows : rows + fields, :] for d in range(count)], axis=0)
    keys = jnp.concatenate([main, last], axis=0)
    high, low = split(keys)
    out = jnp.dot(mix_ref[...], jnp.concatenate([high, low, high], axis=0), preferred_element_type=F32)
    for d in range(count):
        for f in range(fields):
            start = f * time + d * slots
            for p in range(pieces):
                out_ref[d, p, f * slots : (f + 1) * slots, :] = out[start : start + slots, p * LANES : (p + 1) * LANES]


def place_kernel(rows_ref, out_hbm, out_ref, sems):
    slots, fields, rows, cols = out_ref.shape
    pieces = cols // LANES
    copies = []
    for slot in range(slots):
        for f in range(fields):
            for p in range(pieces):
                line = (p * fields + f) * slots + slot
                out_ref[slot, f, :, p * LANES : (p + 1) * LANES] = rows_ref[
                    pl.ds(line, rows, stride=pieces * fields * slots), :
                ]
        copies.append(pltpu.make_async_copy(out_ref.at[slot], out_hbm.at[slot], sems.at[slot]))
        copies[-1].start()
    for copy in copies:
        copy.wait()


def params():
    return pltpu.CompilerParams(vmem_limit_bytes=24 * 1024 * 1024)


def body(increment, trajectory, input_weight, bias, output_weight, correlation):
    slots, fields, rows, cols = increment.shape
    channels = input_weight.shape[0]
    tm = lax.axis_size("tm")
    strips = lax.axis_size("space")
    time = correlation.shape[1]
    parts_across = tm // rows
    width = cols // parts_across

    hbm = pl.BlockSpec(memory_space=pltpu.HBM)
    whole = jax.ShapeDtypeStruct((2 * slots, cols // LANES, rows * fields, LANES), F32)
    half = jax.ShapeDtypeStruct((2 * slots, cols // LANES, rows // 2 * fields, LANES), F32)
    w1_taps = jnp.transpose(input_weight, (2, 3, 1, 0))
    w2_taps = jnp.transpose(output_weight, (2, 3, 0, 1))
    loaded = [
        jax.ShapeDtypeStruct(shape, F32) for shape in (w1_taps.shape, (1, channels), w2_taps.shape, correlation.shape)
    ]
    strip = pltpu.VMEM(increment.shape, F32)
    own, core, chip, w1_taps, bias_row, w2_taps, correlation = pl.pallas_call(
        pack_kernel,
        out_shape=(whole, half, half, *loaded),
        in_specs=[hbm] * 6,
        out_specs=(VMEM,) * 7,
        scratch_shapes=[strip, strip, pltpu.SemaphoreType.DMA((6,))],
        compiler_params=params(),
        name="pack",
    )(*[pltpu.with_memory_space_constraint(x, pltpu.HBM) for x in (trajectory, increment, w1_taps, bias[None], w2_taps, correlation)])

    def swapped(value, first):
        pairs = [(i, i + 1) for i in range(first, strips - 1, 2)]
        return lax.ppermute(value, "space", pairs + [(j, i) for i, j in pairs])

    chip_got = swapped(chip, 1)
    core_got = swapped(core, 0)

    packed = width // slots % LANES == 0
    block = (slots * fields, width + width // slots) if packed else ((slots + 2) * fields, width)
    w1, w2, w2_side, w2_half, w2_end, mix = pl.pallas_call(
        functools.partial(prepare_kernel, tm=tm, strips=strips, slots=slots),
        out_shape=(
            jax.ShapeDtypeStruct((WIN_OUT * channels, KEYS), BF16),
            jax.ShapeDtypeStruct((144, 2 * WIN_OUT * channels), BF16),
            jax.ShapeDtypeStruct((3, 96, 2 * WIN_OUT * channels), BF16),
            jax.ShapeDtypeStruct((96, WIN_OUT * channels), BF16),
            jax.ShapeDtypeStruct((48, WIN_OUT * channels), BF16),
            jax.ShapeDtypeStruct((fields * time, 3 * tm * (slots + 1) * fields), BF16),
        ),
        in_specs=[VMEM] * 4,
        out_specs=(VMEM,) * 6,
        compiler_params=params(),
        name="prepare",
    )(w1_taps, bias_row, w2_taps, correlation)

    kept = pl.pallas_call(
        functools.partial(inner_kernel, strips=strips, slots=slots),
        out_shape=jax.ShapeDtypeStruct((slots, 56, cols), F32),
        in_specs=[VMEM] * 7,
        out_specs=VMEM,
        compiler_params=params(),
        name="inner",
    )(own, core_got, w1, w2, w2_side, w2_half, w2_end)

    send = pl.pallas_call(
        functools.partial(outer_kernel, strips=strips, slots=slots, parts_across=parts_across),
        out_shape=jax.ShapeDtypeStruct((tm, *block), F32),
        in_specs=[VMEM] * 5,
        out_specs=VMEM,
        scratch_shapes=[pltpu.VMEM((slots, rows * fields, cols), F32)],
        compiler_params=params(),
        name="outer",
    )(own, chip_got, kept, w1, w2_side)

    blocks = lax.all_to_all(send, "tm", split_axis=0, concat_axis=0, tiled=True)
    mixed = pl.pallas_call(
        functools.partial(mix_kernel, slots=slots),
        out_shape=jax.ShapeDtypeStruct((tm, width // LANES, slots * fields, LANES), F32),
        in_specs=[VMEM] * 2,
        out_specs=VMEM,
        compiler_params=params(),
        name="mix",
    )(mix, blocks)
    back = lax.all_to_all(mixed, "tm", split_axis=0, concat_axis=0, tiled=True)
    return pl.pallas_call(
        place_kernel,
        out_shape=jax.ShapeDtypeStruct(increment.shape, F32),
        in_specs=[VMEM],
        out_specs=hbm,
        scratch_shapes=[strip, pltpu.SemaphoreType.DMA((slots,))],
        compiler_params=params(),
        name="place",
    )(back.reshape(-1, LANES))


def solution(mesh):
    placed = (P("tm", None, "space", None), P("tm", None, "space", None), P(), P(), P(), P())
    return jax.shard_map(
        body, mesh=mesh, in_specs=placed, out_specs=P("tm", None, "space", None), check_vma=False
    )
```

```python
import functools

import jax
import jax.numpy as jnp
from jax import lax
from jax.experimental import pallas as pl
from jax.experimental.pallas import tpu as pltpu
from jax.sharding import PartitionSpec as P

STEPS = 2
TENDENCY = 0.5
HALO = 2 * STEPS
F32 = jnp.float32
BF16 = jnp.bfloat16
EXACT = lax.Precision.HIGHEST
VMEM = pl.BlockSpec(memory_space=pltpu.VMEM)

WIN_OUT = 4
LANES = 128
KEYS = 256
HALF_KEYS = 160
COLUMN_BLOCKS = 2
CHUNK = 16


def iota(shape, dim):
    return lax.broadcasted_iota(jnp.int32, shape, dim)


def split(value):
    high = value.astype(BF16)
    return high, (value - high.astype(F32)).astype(BF16)


def pack_kernel(
    traj_hbm, incr_hbm, w1_hbm, bias_hbm, w2_hbm, corr_hbm,
    own_ref, core_ref, chip_ref, w1_ref, bias_ref, w2_ref, corr_ref,
    traj_ref, incr_ref, sems,
):
    pairs = (
        (traj_hbm, traj_ref), (incr_hbm, incr_ref), (w1_hbm, w1_ref), (bias_hbm, bias_ref), (w2_hbm, w2_ref), (corr_hbm, corr_ref)
    )
    copies = [pltpu.make_async_copy(src, dst, sems.at[n]) for n, (src, dst) in enumerate(pairs)]
    for copy in copies:
        copy.start()
    slots, fields, rows, _ = traj_ref.shape
    half = rows // 2 * fields
    odd = lax.axis_index("space") % 2
    core_half = pl.ds(pl.multiple_of((1 - odd) * half, half), half)
    chip_half = pl.ds(pl.multiple_of(odd * half, half), half)
    for kind, ref in enumerate((traj_ref, incr_ref)):
        copies[kind].wait()
        for slot in range(slots):
            index = kind * slots + slot
            for piece in range(own_ref.shape[1]):
                for f in range(fields):
                    own_ref[index, piece, pl.ds(f, rows, stride=fields), :] = ref[
                        slot, f, :, piece * LANES : (piece + 1) * LANES
                    ]
                core_ref[index, piece] = own_ref[index, piece, core_half, :]
                chip_ref[index, piece] = own_ref[index, piece, chip_half, :]
    for copy in copies[2:]:
        copy.wait()


def key_codes(shape, dim):
    key = iota(shape, dim)
    none = -1000
    q = key - 16
    front_high = (q // 32) * 24 + q % 16
    q = key - 112
    front_low = (q // 16) * 24 + q % 16
    q = key - 160
    back_high = (q // 16) * 24 + 16 + q % 8
    q = key - 208
    back_low = (q // 16) * 24 + 16 + q % 8
    high = jnp.where((key >= 16) & (key < 112), front_high, jnp.where((key >= 160) & (key < 208), back_high, none))
    low = jnp.where((key >= 112) & (key < 160), front_low, jnp.where(key >= 208, back_low, none))
    return high, low, key


def prepare_kernel(w1_ref, bias_ref, w2_ref, corr_ref, w1_out, w2_out, w2_side, w2_half, w2_end, mix_out, *, tm, strips, slots):
    fields = w1_ref.shape[2]
    channels = w1_ref.shape[3]
    time = corr_ref.shape[1]
    taps = [(a, b) for a in range(3) for b in range(3)]
    j = iota((40, KEYS), 0)
    t = j // 4
    a = (t >= 3).astype(jnp.int32) + (t >= 6).astype(jnp.int32)
    code = jnp.where(j < 36, (t - 3 * a) * 24 + a * 4 + j % 4, -5000)
    high_code, low_code, key = key_codes((40, KEYS), 1)
    table = jnp.concatenate(
        [w1_ref[a, b] for a, b in taps] + [bias_ref[...], jnp.zeros((3, channels), F32)], axis=0
    )
    bias_row = j == 36
    chosen = [
        jnp.concatenate([(code + 4 * out == codes) | (bias_row & (key == place)) for out in range(WIN_OUT)], axis=1)
        for codes, place in ((high_code, 0), (low_code, 1))
    ]
    chosen = jnp.concatenate([jnp.where(c, 1.0, 0.0) for c in chosen], axis=0).astype(BF16)
    parts = [p.astype(F32) for p in split(table)]
    blocks = lax.dot_general(
        jnp.concatenate(parts, axis=0).astype(BF16), chosen, (((0,), (0,)), ((), ())), preferred_element_type=F32
    )
    for out in range(WIN_OUT):
        w1_out[out * channels : (out + 1) * channels, :] = blocks[:, out * KEYS : (out + 1) * KEYS].astype(BF16)
    keys = WIN_OUT * channels
    spread = jnp.where(iota((channels, keys), 1) % channels == iota((channels, keys), 0), 1.0, 0.0).astype(BF16)
    halves = split(jnp.concatenate([w2_ref[a, b] for a, b in taps], axis=0) * TENDENCY)
    tables = jnp.concatenate([jnp.dot(h, spread, preferred_element_type=F32).astype(BF16) for h in halves], axis=1)
    mj = iota((72, 36), 0)
    mj_tap = jnp.where(mj >= 48, 2, jnp.where(mj >= 24, 1, 0))
    source = mj_tap * 4 + mj % 4
    repeat = jnp.concatenate(
        [jnp.where(iota((72, 36), 1) == tap_row * 12 + source, 1.0, 0.0) for tap_row in range(3)], axis=0
    ).astype(BF16)
    repeated = jnp.dot(repeat, tables, preferred_element_type=F32)
    m = iota((72, keys), 0)
    m_row = (m - jnp.where(m >= 48, 48, jnp.where(m >= 24, 24, 0))) // 4
    k_row = iota((72, keys), 1) // channels
    full = []
    for part in range(2):
        total = jnp.zeros((72, keys), F32)
        for tap_row in range(3):
            block = repeated[72 * tap_row : 72 * (tap_row + 1), keys * part : keys * (part + 1)]
            total = total + jnp.where(k_row == m_row - 2 + tap_row, block, 0.0)
        full.append(total)
    even, keep = chip_side(strips)

    def operand(tables):
        high, low = tables
        return jnp.concatenate(
            [jnp.concatenate([high, high], axis=1), jnp.concatenate([low, jnp.zeros(low.shape, F32)], axis=1)], axis=0
        ).astype(BF16)

    def groups_of(table, if_even, if_odd, count, width):
        rows = [
            jnp.where(even, table[24 * t + 8 * e : 24 * t + 8 * e + 8], table[24 * t + 8 * o : 24 * t + 8 * o + 8])
            for t in range(3)
            for e, o in list(zip(if_even, if_odd))[:count]
        ]
        return jnp.concatenate(rows, axis=0)[:, 0:width]

    first_out = (even & (k_row < 3)) | (~even & (k_row > 0))
    second_out = (even & (k_row < 1)) | (~even & (k_row > 2))
    w2_out[...] = operand(full)
    for form, (rows_out, if_even, if_odd) in enumerate(
        ((first_out, (1, 2), (1, 0)), (second_out, (1, 2), (1, 0)), (None, (1, 0), (1, 2)))
    ):
        kept = [t if rows_out is None else jnp.where(rows_out, t * keep, t) for t in full]
        w2_side[form] = operand([groups_of(t, if_even, if_odd, 2, keys) for t in kept])
    short = keys // 2
    w2_half[...] = operand([groups_of(t, (0, 1), (0, 1), 2, short) for t in full])
    w2_end[...] = operand([groups_of(t, (0,), (1,), 1, short) for t in full])
    main = tm * slots * fields
    key = iota((time, main + tm * fields), 1)
    slot = jnp.where(key < main, key // fields, (key - main) // fields * slots + slots)
    met = slot == iota(key.shape, 0)
    for f in range(fields):
        pick = jnp.where(met & (key % fields == f), 1.0, 0.0).astype(BF16)
        first = corr_ref[f].astype(BF16)
        rest = corr_ref[f] - first.astype(F32)
        second = rest.astype(BF16)
        rows = slice(f * time, (f + 1) * time)
        high = jnp.dot(first, pick, preferred_element_type=F32).astype(BF16)
        mix_out[rows, :] = jnp.concatenate([high, high, jnp.dot(second, pick, preferred_element_type=F32).astype(BF16)], axis=1)


def moved(value, shift):
    if shift == 0:
        return value
    cols = value.shape[1]
    column = iota(value.shape, 1)
    turned = pltpu.roll(value, shift % cols, 1)
    outside = column == (0 if shift > 0 else cols - 1)
    return jnp.where(outside, 0.0, turned)


def window_keys(groups, bias):
    cols = groups[0].shape[1]
    front_high, front_low, back_high, back_low = [], [], [], []
    high, low = split(jnp.concatenate(groups[:2], axis=0))
    if len(groups) == 3:
        rounded = groups[2].astype(BF16).astype(F32)
        both = jnp.concatenate([rounded, groups[2] - rounded], axis=0).astype(BF16)
    for tap in range(3):
        front_low.append(moved(high, 1 - tap))
        front_high += [front_low[-1], moved(low, 1 - tap)]
        if len(groups) == 3:
            back_high.append(moved(both, 1 - tap))
    back_low = back_high
    first = jnp.full((16, cols), 1.0 if bias else 0.0, BF16)
    return jnp.concatenate([first] + front_high + front_low + back_high + back_low, axis=0)


def hidden_pair(state_groups, tangent_groups, w1_ref):
    rows, keys = w1_ref.shape
    if len(state_groups) == 2:
        rows, keys = rows // 2, HALF_KEYS
    w1 = w1_ref[0:rows, 0:keys]
    state_keys = window_keys(state_groups, True)
    tangent_keys = window_keys(tangent_groups, False)
    cols = state_keys.shape[1]
    width = cols // COLUMN_BLOCKS
    result = ([], [])
    for start in range(0, cols, width):
        z = jnp.dot(w1, state_keys[:, start : start + width], preferred_element_type=F32)
        dz = jnp.dot(w1, tangent_keys[:, start : start + width], preferred_element_type=F32)
        parts = ([], [], [], [])
        for row in range(0, rows, CHUNK):
            h = jnp.tanh(z[row : row + CHUNK])
            g = (1.0 - h * h) * dz[row : row + CHUNK]
            for place, part in zip(parts, (*split(h), *split(g))):
                place.append(part)
        result[0].append(jnp.concatenate(parts[0] + parts[1], axis=0))
        result[1].append(jnp.concatenate(parts[2] + parts[3], axis=0))
    return result


def spread_hidden(hidden, weight):
    taps = []
    for block in hidden:
        product = jnp.dot(weight, block, preferred_element_type=F32)
        half = product.shape[0] // 2
        taps.append(product[:half] + product[half:])
    taps = jnp.concatenate(taps, axis=1)
    third = taps.shape[0] // 3
    total = moved(taps[0:third], 1) + taps[third : 2 * third] + moved(taps[2 * third :], -1)
    return [total[g : g + 8] for g in range(0, third, 8)]


def chip_side(strips):
    me = lax.axis_index("space")
    even = me % 2 == 0
    return even, jnp.where((me == 0) | (me == strips - 1), 0.0, 1.0)


def read_group(ref, index, g):
    pieces = ref.shape[1]
    return jnp.concatenate([ref[index, p, 8 * g : 8 * g + 8, :] for p in range(pieces)], axis=1)


def staggered(slots, one_slot, together, first=0):
    waiting = [one_slot(first + slot) for slot in range(slots)]
    running = []
    while waiting or running:
        starting = len(waiting) if together else 1
        running = waiting[:starting] + running
        waiting = waiting[starting:]
        running = [r for r in running if next(r, True) is None]


def inner_kernel(own_ref, core_got_ref, w1_ref, w2_ref, w2_side_ref, w2_half_ref, w2_end_ref, kept_ref, *, strips, slots):
    even, keep = chip_side(strips)

    def pick(if_even, if_odd):
        return jnp.where(even, if_even, if_odd)

    def in_order(values):
        return [pick(a, b) for a, b in zip(values, values[::-1])]

    def edge_slot(slot):
        outside = jnp.zeros((8, kept_ref.shape[2]), F32)
        lines = []
        for index in (slot, slots + slot):
            own = [read_group(own_ref, index, g) for g in range(4)]
            core = [read_group(core_got_ref, index, g) for g in range(2)]
            lines.append([outside] + in_order(own) + [pick(a, b) for a, b in zip(core, core[::-1])])
        pairs = []
        for start in (0, 2, 4):
            windows = [in_order(line[start : start + 3]) for line in lines]
            pairs.append(hidden_pair(windows[0], windows[1], w1_ref))
            yield
        moved_on = []
        for kind, line in enumerate(lines):
            a = spread_hidden(pairs[0][kind], w2_side_ref[1])
            b = in_order(spread_hidden(pairs[1][kind], w2_ref[...]))
            c = spread_hidden(pairs[2][kind], w2_side_ref[2])
            added = [a[0], a[1] + b[0], b[1], b[2] + c[1], c[0]]
            moved_on.append([outside] + [x + y for x, y in zip(line[1:6], added)])
        s, t = moved_on
        yield
        near = hidden_pair(in_order(s[0:3]), in_order(t[0:3]), w1_ref)
        middle = hidden_pair(in_order(s[2:5]), in_order(t[2:5]), w1_ref)
        far = hidden_pair(in_order(s[4:6]), in_order(t[4:6]), w1_ref)
        yield
        a = spread_hidden(near[1], w2_side_ref[1])
        b = in_order(spread_hidden(middle[1], w2_ref[...]))
        (c,) = spread_hidden(far[1], w2_end_ref[...])
        for g, value in enumerate([a[0], a[1] + b[0], b[1], b[2] + c]):
            kept_ref[slot, 8 * g : 8 * g + 8, :] = t[1 + g] + value

    def one_slot(slot):
        line, ends = [], []
        for index in (slot, slots + slot):
            own = [read_group(own_ref, index, g) for g in range(4)]
            core = [read_group(core_got_ref, index, g) for g in range(2)]
            line.append([pick(a, b) for a, b in zip(own + core[:1], core[1:] + own)])
            ends.append(core)
        first = hidden_pair(line[0][0:3], line[1][0:3], w1_ref)
        second = hidden_pair(line[0][2:5], line[1][2:5], w1_ref)
        last = hidden_pair(ends[0], ends[1], w1_ref)
        yield
        moved_on = []
        for kind in range(2):
            a = spread_hidden(first[kind], w2_ref[...])
            b = spread_hidden(second[kind], w2_ref[...])
            (c,) = spread_hidden(last[kind], w2_end_ref[...])
            added = [a[0] + pick(0.0, c), a[1], a[2] + b[0], b[1], b[2] + pick(c, 0.0)]
            moved_on.append([x + y for x, y in zip(line[kind], added)])
        s, t = moved_on
        yield
        outer = hidden_pair(
            [pick(a, b) for a, b in zip(s[2:5], s[0:3])], [pick(a, b) for a, b in zip(t[2:5], t[0:3])], w1_ref
        )
        middle = hidden_pair(
            [pick(a, b) for a, b in zip(s[1:3], s[2:4])], [pick(a, b) for a, b in zip(t[1:3], t[2:4])], w1_ref
        )
        yield
        u = spread_hidden(outer[1], w2_side_ref[2])
        v = spread_hidden(middle[1], w2_half_ref[...])
        kept = [
            pick(t[3], t[1]) + u[0],
            t[2] + u[1] + pick(v[1], v[0]),
            pick(t[1], t[3]) + pick(v[0], v[1]),
            pick(s[0], s[4]),
            pick(t[0], t[4]),
            pick(s[1], s[3]),
            pick(t[1], t[3]),
        ]
        for g, value in enumerate(kept):
            kept_ref[slot, 8 * g : 8 * g + 8, :] = value

    @pl.when(keep == 0.0)
    def _():
        staggered(slots, edge_slot, False)

    @pl.when(keep != 0.0)
    def _():
        staggered(slots, one_slot, False)


def outer_kernel(own_ref, chip_got_ref, kept_ref, w1_ref, w2_side_ref, send_ref, done_ref, *, strips, slots, parts_across):
    even, keep = chip_side(strips)
    cols = kept_ref.shape[2]
    width = cols // parts_across
    fields, rows = 4, 8
    packed = send_ref.shape[2] > width

    def pick(if_even, if_odd):
        return jnp.where(even, if_even, if_odd)

    def in_order(values):
        return [pick(a, b) for a, b in zip(values, values[::-1])]

    def send(value, slot):
        for y in range(rows):
            for block in range(parts_across):
                part = value[y * fields : (y + 1) * fields, block * width : (block + 1) * width]
                if slot < slots or not packed:
                    send_ref[y * parts_across + block, slot * fields : (slot + 1) * fields, 0:width] = part
                    continue
                for q in range(slots):
                    send_ref[y * parts_across + block, q * fields : (q + 1) * fields, width:] = part[
                        :, q * width // slots : (q + 1) * width // slots
                    ]

    def start(slot):
        return jnp.concatenate([read_group(own_ref, slots + slot, g) for g in range(4)], axis=0)

    def one_slot(slot):
        near = [kept_ref[slot, 8 * g : 8 * g + 8, :] for g in (3, 4)]
        frames = []
        for index in (slot, slots + slot):
            chip = [read_group(chip_got_ref, index, g) for g in range(2)]
            own = [read_group(own_ref, index, g) for g in (0, 3)]
            frames.append([pick(chip[0], own[1]), pick(chip[1], chip[0]), pick(own[0], chip[1])])
        pair = hidden_pair(frames[0], frames[1], w1_ref)
        yield
        moved_on = []
        for kind in range(2):
            w = spread_hidden(pair[kind], w2_side_ref[0])
            moved_on.append([frames[kind][1] + w[0], near[kind] + w[1]])
        state, tangent = moved_on
        yield
        f_outer, f_middle, f_inner, s_next, t_next = [kept_ref[slot, 8 * g : 8 * g + 8, :] for g in (0, 1, 2, 5, 6)]
        pair = hidden_pair(in_order(state + [s_next]), in_order(tangent + [t_next]), w1_ref)
        yield
        x = spread_hidden(pair[1], w2_side_ref[1])
        ends = [tangent[1] + x[0], f_inner + x[1], f_middle, f_outer]
        for g, value in enumerate(ends):
            done_ref[slot, 8 * g : 8 * g + 8, :] = value

    def residual(slot, ref):
        final = jnp.concatenate(in_order([ref[slot, 8 * g : 8 * g + 8, :] for g in range(4)]), axis=0)
        send(start(slot + 1) - final if slot < slots - 1 else -final, slot + 1)

    send(start(0), 0)

    @pl.when(keep == 0.0)
    def _():
        for slot in range(slots):
            residual(slot, kept_ref)

    @pl.when((keep != 0.0) & even)
    def _():
        staggered(slots, one_slot, True)

    @pl.when((keep != 0.0) & ~even)
    def _():
        def some_slots(turn, carry):
            staggered(2, one_slot, True, 2 * turn)
            return carry

        lax.fori_loop(0, slots // 2, some_slots, 0)

    @pl.when(keep != 0.0)
    def _():
        for slot in range(slots):
            residual(slot, done_ref)

    if not packed:
        send_ref[:, (slots + 1) * fields :, :] = jnp.zeros((rows * parts_across, fields, width), F32)


def mix_kernel(mix_ref, block_ref, out_ref, *, slots):
    count, pieces, rows, _ = out_ref.shape
    width = pieces * LANES
    fields = rows // slots
    time = count * slots
    main = block_ref[:, 0:rows, 0:width].reshape(count * rows, width)
    if block_ref.shape[2] > width:
        last = [
            jnp.concatenate([block_ref[d, q * fields : (q + 1) * fields, width:] for d in range(count)], axis=0)
            for q in range(slots)
        ]
        last = jnp.concatenate(last, axis=1)
    else:
        last = jnp.concatenate([block_ref[d, rows : rows + fields, :] for d in range(count)], axis=0)
    keys = jnp.concatenate([main, last], axis=0)
    high, low = split(keys)
    out = jnp.dot(mix_ref[...], jnp.concatenate([high, low, high], axis=0), preferred_element_type=F32)
    for d in range(count):
        for f in range(fields):
            start = f * time + d * slots
            for p in range(pieces):
                out_ref[d, p, f * slots : (f + 1) * slots, :] = out[start : start + slots, p * LANES : (p + 1) * LANES]


def place_kernel(rows_ref, out_hbm, out_ref, sems):
    slots, fields, rows, cols = out_ref.shape
    pieces = cols // LANES
    copies = []
    for slot in range(slots):
        for f in range(fields):
            for p in range(pieces):
                line = (p * fields + f) * slots + slot
                out_ref[slot, f, :, p * LANES : (p + 1) * LANES] = rows_ref[
                    pl.ds(line, rows, stride=pieces * fields * slots), :
                ]
        copies.append(pltpu.make_async_copy(out_ref.at[slot], out_hbm.at[slot], sems.at[slot]))
        copies[-1].start()
    for copy in copies:
        copy.wait()


def params():
    return pltpu.CompilerParams(vmem_limit_bytes=24 * 1024 * 1024)


def body(increment, trajectory, input_weight, bias, output_weight, correlation):
    slots, fields, rows, cols = increment.shape
    channels = input_weight.shape[0]
    tm = lax.axis_size("tm")
    strips = lax.axis_size("space")
    time = correlation.shape[1]
    parts_across = tm // rows
    width = cols // parts_across

    hbm = pl.BlockSpec(memory_space=pltpu.HBM)
    whole = jax.ShapeDtypeStruct((2 * slots, cols // LANES, rows * fields, LANES), F32)
    half = jax.ShapeDtypeStruct((2 * slots, cols // LANES, rows // 2 * fields, LANES), F32)
    w1_taps = jnp.transpose(input_weight, (2, 3, 1, 0))
    w2_taps = jnp.transpose(output_weight, (2, 3, 0, 1))
    loaded = [
        jax.ShapeDtypeStruct(shape, F32) for shape in (w1_taps.shape, (1, channels), w2_taps.shape, correlation.shape)
    ]
    strip = pltpu.VMEM(increment.shape, F32)
    own, core, chip, w1_taps, bias_row, w2_taps, correlation = pl.pallas_call(
        pack_kernel,
        out_shape=(whole, half, half, *loaded),
        in_specs=[hbm] * 6,
        out_specs=(VMEM,) * 7,
        scratch_shapes=[strip, strip, pltpu.SemaphoreType.DMA((6,))],
        compiler_params=params(),
        name="pack",
    )(*[pltpu.with_memory_space_constraint(x, pltpu.HBM) for x in (trajectory, increment, w1_taps, bias[None], w2_taps, correlation)])

    def swapped(value, first):
        pairs = [(i, i + 1) for i in range(first, strips - 1, 2)]
        return lax.ppermute(value, "space", pairs + [(j, i) for i, j in pairs])

    chip_got = swapped(chip, 1)
    core_got = swapped(core, 0)

    packed = width // slots % LANES == 0
    block = (slots * fields, width + width // slots) if packed else ((slots + 2) * fields, width)
    w1, w2, w2_side, w2_half, w2_end, mix = pl.pallas_call(
        functools.partial(prepare_kernel, tm=tm, strips=strips, slots=slots),
        out_shape=(
            jax.ShapeDtypeStruct((WIN_OUT * channels, KEYS), BF16),
            jax.ShapeDtypeStruct((144, 2 * WIN_OUT * channels), BF16),
            jax.ShapeDtypeStruct((3, 96, 2 * WIN_OUT * channels), BF16),
            jax.ShapeDtypeStruct((96, WIN_OUT * channels), BF16),
            jax.ShapeDtypeStruct((48, WIN_OUT * channels), BF16),
            jax.ShapeDtypeStruct((fields * time, 3 * tm * (slots + 1) * fields), BF16),
        ),
        in_specs=[VMEM] * 4,
        out_specs=(VMEM,) * 6,
        compiler_params=params(),
        name="prepare",
    )(w1_taps, bias_row, w2_taps, correlation)

    kept = pl.pallas_call(
        functools.partial(inner_kernel, strips=strips, slots=slots),
        out_shape=jax.ShapeDtypeStruct((slots, 56, cols), F32),
        in_specs=[VMEM] * 7,
        out_specs=VMEM,
        compiler_params=params(),
        name="inner",
    )(own, core_got, w1, w2, w2_side, w2_half, w2_end)

    send = pl.pallas_call(
        functools.partial(outer_kernel, strips=strips, slots=slots, parts_across=parts_across),
        out_shape=jax.ShapeDtypeStruct((tm, *block), F32),
        in_specs=[VMEM] * 5,
        out_specs=VMEM,
        scratch_shapes=[pltpu.VMEM((slots, rows * fields, cols), F32)],
        compiler_params=params(),
        name="outer",
    )(own, chip_got, kept, w1, w2_side)

    blocks = lax.all_to_all(send, "tm", split_axis=0, concat_axis=0, tiled=True)
    mixed = pl.pallas_call(
        functools.partial(mix_kernel, slots=slots),
        out_shape=jax.ShapeDtypeStruct((tm, width // LANES, slots * fields, LANES), F32),
        in_specs=[VMEM] * 2,
        out_specs=VMEM,
        compiler_params=params(),
        name="mix",
    )(mix, blocks)
    back = lax.all_to_all(mixed, "tm", split_axis=0, concat_axis=0, tiled=True)
    return pl.pallas_call(
        place_kernel,
        out_shape=jax.ShapeDtypeStruct(increment.shape, F32),
        in_specs=[VMEM],
        out_specs=hbm,
        scratch_shapes=[strip, pltpu.SemaphoreType.DMA((slots,))],
        compiler_params=params(),
        name="place",
    )(back.reshape(-1, LANES))


def solution(mesh):
    placed = (P("tm", None, "space", None), P("tm", None, "space", None), P(), P(), P(), P())
    return jax.shard_map(
        body, mesh=mesh, in_specs=placed, out_specs=P("tm", None, "space", None), check_vma=False
    )
```
